32 devices in a mesh: dp: 32 (over z, y, x, core).
Axes of the slice: x: 2, y: 2, z: 4, core: 2. Of those that a mesh axis runs over, the one named last changes fastest.
Arguments:
- images: bfloat16 [320, 16, 16, 3], P('dp'), may hold values from -6 to 6
- labels: int32 [320], P('dp'), may hold values from 0 to 9
- groups: int32 [320], P('dp'), may hold values from 0 to 1
- conv_w: float32 [4608, 256], P('dp'), may hold values from -0.125 to 0.125
- conv_m: float32 [4608, 256], P('dp'), may hold values from -0.00061035156 to 0.00061035156
- conv_v: float32 [4608, 256], P('dp'), may hold values from 1.2207031e-09 to 4.8828124e-09
- rot_bases: float32 [4, 256, 256], replicated, as said below
- stem_w: float32 [27, 256], replicated, may hold values from -1.25 to 1.25
- stem_m: float32 [27, 256], replicated, may hold values from -0.00061035156 to 0.00061035156
- stem_v: float32 [27, 256], replicated, may hold values from 1.2207031e-09 to 4.8828124e-09
- head_w: float32 [257, 10], replicated, may hold values from -4 to 4
- head_m: float32 [257, 10], replicated, may hold values from -0.0390625 to 0.0390625
- head_v: float32 [257, 10], replicated, may hold values from 5e-06 to 2e-05
- norm_p: float32 [6, 256], replicated
- norm_m: float32 [6, 256], replicated, may hold values from -0.0012207031 to 0.0012207031
- norm_v: float32 [6, 256], replicated, may hold values from 2.1875e-05 to 8.75e-05
Outputs:
- loss: float32 [2], replicated
- factors: float32 [1024, 256], P('dp')
- inverses: float32 [1024, 256], P('dp')
- conv_w_new: float32 [4608, 256], P('dp')
- conv_m_new: float32 [4608, 256], P('dp')
- conv_v_new: float32 [4608, 256], P('dp')
- rot_bases_new: float32 [4, 256, 256], replicated
- stem_w_new: float32 [27, 256], replicated
- stem_m_new: float32 [27, 256], replicated
- stem_v_new: float32 [27, 256], replicated
- head_w_new: float32 [257, 10], replicated
- head_m_new: float32 [257, 10], replicated
- head_v_new: float32 [257, 10], replicated
- norm_p_new: float32 [6, 256], replicated
- norm_m_new: float32 [6, 256], replicated
- norm_v_new: float32 [6, 256], replicated
- conv_bf16: bfloat16 [4608, 256], P('dp')
The draws below stay inside these ranges and needn't reach their ends.
Inputs may be any that keep to these rules, and one draw needn't show every extreme that they name: `rot_bases`: each of the four matrices is orthogonal.
All inputs are finite; a program needn't handle non-finite values.
Results may differ from the reference program's by a relative error of at most 0.012.
The reference program's roundings to bfloat16 on the way (of `hidden_one` and `hidden_two`) count: a program that leaves them out, or rounds other values in their place, can miss the bound.
Values may be sent and summed in bfloat16 or wider, within the bound.
No kernel may reach another device: no remote copies, remote signals or barrier semaphores. Data moves between devices by JAX's collectives and lax.ppermute only.
A program may use at most 192 MiB of HBM per device.

```python
import math
from functools import partial
import jax
import jax.numpy as jnp
from jax import lax

C = 256
CLASSES = 10
SIDE = 16
NS_ITERS = 6
STEP = 5
IMAGES = 320
PIXELS = 81920
BLOCK_IMG = 20


def draw_groups(key, part):
    key = jax.random.fold_in(key, 3)
    positions = jnp.arange(IMAGES, dtype=jnp.int32)
    threshold = 100 + 800 * positions // max(IMAGES - 1, 1)
    return (jax.random.randint(key, (IMAGES,), 0, 1000, dtype=jnp.int32) < threshold).astype(jnp.int32)


def draw_rot_bases(key, part):
    key = jax.random.fold_in(key, 11)
    vectors = jax.random.normal(key, (4, 48, C), jnp.float32)
    matrices = jnp.broadcast_to(jnp.eye(C, dtype=jnp.float32), (4, C, C))
    for reflect_id in range(48):
        unit_vec = vectors[:, reflect_id, :]
        unit_vec = unit_vec / jnp.sqrt(jnp.sum(unit_vec * unit_vec, axis=1, keepdims=True))
        projected = jnp.sum(matrices * unit_vec[:, None, :], axis=2)
        matrices = matrices - 2.0 * projected[:, :, None] * unit_vec[:, None, :]
    return matrices


def draw_norm_p(key, part):
    key = jax.random.fold_in(key, 5)
    gains = jax.random.uniform(jax.random.fold_in(key, 1), (3, C), jnp.float32, 0.6, 1.6)
    shifts = 0.3 * jax.random.normal(jax.random.fold_in(key, 2), (3, C), jnp.float32)
    return jnp.stack([gains, shifts], axis=1).reshape(6, C)


def place_ends(entries, rng, smallest, top_value):
    extent = entries.shape
    spot = [jax.random.randint(jax.random.fold_in(rng, axis), (), 0, extent[axis]) for axis in range(len(extent))]
    entries = entries.at[tuple(spot)].set(smallest)
    longest = extent.index(max(extent))
    spot[longest] = (spot[longest] + 1) % extent[longest]
    return entries.at[tuple(spot)].set(top_value)


def level_of(own_key, dims, cuts, low, top_value):
    gain = 1.0
    for position, parts in cuts:
        draws = jax.random.uniform(jax.random.fold_in(jax.random.fold_in(own_key, 6), position), (parts,), jnp.float32, low / len(cuts), top_value / len(cuts))
        gain = gain * jnp.repeat(jnp.exp(draws), dims[position] // parts).reshape((-1,) + (1,) * (len(dims) - 1 - position))
    return gain


def scatter_about(rng, extent, scale, limit, cuts=(), held_as=jnp.bfloat16):
    drawn = scale * jax.random.normal(rng, extent, jnp.float32)
    if cuts:
        drawn = drawn * level_of(rng, extent, cuts, -0.22, 0.18)
    return jnp.clip(drawn, -limit, limit).astype(held_as)


def setup_inputs(seed: int = 0) -> dict:
    streams_of = jax.random.split(jax.random.key(seed), 17)
    return {
        "images": scatter_about(streams_of[0], (IMAGES, SIDE, SIDE, 3), 1.0, 6.0, ((0, 32),)),
        "labels": place_ends(jax.random.randint(streams_of[1], (IMAGES,), 0, CLASSES), jax.random.fold_in(streams_of[1], 1), 0, CLASSES - 1).astype(jnp.int32),
        "groups": draw_groups(jax.random.fold_in(streams_of[16], 71), 0),
        "conv_w": scatter_about(streams_of[3], (18 * C, C), (9 * C) ** -0.5, 0.125, ((0, 32),), jnp.float32),
        "conv_m": scatter_about(streams_of[4], (18 * C, C), (0.011 / PIXELS ** 0.5), 0.00061035156, ((0, 32),), jnp.float32),
        "conv_v": jnp.clip(jnp.exp(math.log(4.882812376649781e-09) - 1.3862944 * jax.random.uniform(streams_of[5], (18 * C, C), jnp.float32) ** level_of(streams_of[5], (18 * C, C), ((0, 32),), -0.2, 0.2)), 1.2207030941624453e-09, 4.882812376649781e-09),
        "rot_bases": draw_rot_bases(jax.random.fold_in(streams_of[16], 71), 0),
        "stem_w": scatter_about(streams_of[7], (27, C), 27 ** -0.5, 1.25, (), jnp.float32),
        "stem_m": scatter_about(streams_of[8], (27, C), (0.011 / PIXELS ** 0.5), 0.00061035156, (), jnp.float32),
        "stem_v": jnp.clip(jnp.exp(jax.random.uniform(streams_of[9], (27, C), jnp.float32, math.log(1.2207030941624453e-09), math.log(4.882812376649781e-09))), 1.2207030941624453e-09, 4.882812376649781e-09),
        "head_w": scatter_about(streams_of[10], (C + 1, CLASSES), 0.25, 4.0, (), jnp.float32),
        "head_m": scatter_about(streams_of[11], (C + 1, CLASSES), (0.05 / IMAGES ** 0.5), 0.0390625, (), jnp.float32),
        "head_v": jnp.clip(jnp.exp(jax.random.uniform(streams_of[12], (C + 1, CLASSES), jnp.float32, math.log(4.999999873689376e-06), math.log(1.9999999494757503e-05))), 4.999999873689376e-06, 1.9999999494757503e-05),
        "norm_p": draw_norm_p(jax.random.fold_in(streams_of[16], 71), 0),
        "norm_m": scatter_about(streams_of[14], (6, C), (0.022 / PIXELS ** 0.5), 0.0012207031, (), jnp.float32),
        "norm_v": jnp.clip(jnp.exp(jax.random.uniform(streams_of[15], (6, C), jnp.float32, math.log(2.1874999220017344e-05), math.log(8.749999688006938e-05))), 2.1874999220017344e-05, 8.749999688006938e-05),
    }


EPS_NORM = 1e-05
BETA_ONE = 0.9
BETA_TWO = 0.99
ADAM_EPS = 1e-08
WEIGHT_DECAY = 0.01
DAMPING = 0.1
PROBIT_SCALE = math.pi / 8.0
RATE_CONV = 0.02
RATE_STEM = 0.1
RATE_HEAD = 0.1
RATE_NORM = 0.5
highest = lax.Precision.HIGHEST

@jax.custom_vjp
def low(v):
    return lax.optimization_barrier(v.astype(jnp.bfloat16)).astype(jnp.float32)

@jax.custom_vjp
def low_back(v):
    return v

def low_keep(v):
    return (low(v), None)

def low_pass(kept, grad):
    return (grad,)

def back_keep(v):
    return (v, None)

def back_low(kept, grad):
    return (low(grad),)
low.defvjp(low_keep, low_pass)
low_back.defvjp(back_keep, back_low)

def dot_high(left_in, right_in):
    return jnp.dot(left_in.astype(jnp.float32), right_in.astype(jnp.float32), precision=highest, preferred_element_type=jnp.float32)

def to_blocks(rows_in, count):
    width = rows_in.shape[1]
    return rows_in.reshape(width, count, width).transpose(1, 0, 2)

def from_blocks(stacked):
    return stacked.transpose(1, 0, 2).reshape(-1, stacked.shape[2])

def patches(images_in):
    side_len = images_in.shape[1]
    padded = jnp.pad(images_in, ((0, 0), (1, 1), (1, 1), (0, 0)))
    pieces = [padded[:, offset_a:offset_a + side_len, offset_b:offset_b + side_len, :] for offset_a in range(3) for offset_b in range(3)]
    return jnp.concatenate(pieces, axis=-1).reshape(-1, 9 * images_in.shape[-1])

def moments(values):
    return jnp.stack([lax.optimization_barrier(jnp.sum(values, axis=0)), lax.optimization_barrier(jnp.sum(values * values, axis=0))])

def normalize(values, stat_sums, gain_row, shift_row):
    mean_val = stat_sums[0] / PIXELS
    variance = stat_sums[1] / PIXELS - mean_val * mean_val
    return (values - mean_val) * lax.rsqrt(variance + EPS_NORM) * gain_row + shift_row

def forward_block(params, stat_sums, batch_in, probes, section_id):
    conv_w, stem_w, head_w, norm_p = params
    images_in, labels_in, weights_in = batch_in
    count_img, side_len = (images_in.shape[0], images_in.shape[1])
    channels = conv_w.shape[1]
    stem_out = low_back(dot_high(patches(images_in), low(stem_w)))
    if section_id == 0:
        return moments(stem_out)
    hidden_one = low(jax.nn.gelu(normalize(stem_out, stat_sums[0], norm_p[0], norm_p[1])))
    conv_one = low_back(dot_high(patches(hidden_one.reshape(count_img, side_len, side_len, channels)), low(conv_w[:9 * channels])) + probes[0])
    if section_id == 1:
        return moments(conv_one)
    hidden_two = low(jax.nn.gelu(normalize(conv_one, stat_sums[1], norm_p[2], norm_p[3])))
    conv_two = low_back(dot_high(patches(hidden_two.reshape(count_img, side_len, side_len, channels)), low(conv_w[9 * channels:])) + probes[1])
    residual = stem_out + conv_two
    if section_id == 2:
        return moments(residual)
    features = jax.nn.gelu(normalize(residual, stat_sums[2], norm_p[4], norm_p[5]))
    pooled = lax.optimization_barrier(jnp.mean(features.reshape(count_img, side_len * side_len, channels), axis=1))
    logits = low_back(dot_high(low(pooled), low(head_w[:channels])) + head_w[channels])
    spread = lax.optimization_barrier(jnp.mean(pooled * pooled, axis=1))
    scaled = logits * lax.rsqrt(1.0 + PROBIT_SCALE * spread)[:, None]
    targets = (labels_in[:, None] == jnp.arange(scaled.shape[1], dtype=jnp.int32)[None, :]).astype(jnp.float32)
    picked = lax.optimization_barrier(jnp.sum(scaled * targets, axis=1))
    loss_sum = jnp.sum(weights_in * (jax.nn.logsumexp(scaled, axis=1) - picked))
    if section_id == 3:
        return loss_sum
    return (moments(stem_out), moments(conv_one), moments(residual), loss_sum, hidden_one, hidden_two)

def block_sum(params, stat_sums, section_id, batches):
    local_fn = jax.checkpoint(partial(forward_block, probes=(0.0, 0.0), section_id=section_id))

    def add_block(running, batch_in):
        return (running + local_fn(params, stat_sums, batch_in), None)
    if section_id == 3:
        initial = jnp.zeros((), jnp.float32)
    else:
        initial = jnp.zeros((2, params[0].shape[1]), jnp.float32)
    return lax.scan(add_block, initial, batches)[0]

def adam_step(param_in, grad_in, first_in, second_in, rate_in, decay_in):
    first_new = BETA_ONE * first_in + (1.0 - BETA_ONE) * grad_in
    second_new = BETA_TWO * second_in + (1.0 - BETA_TWO) * grad_in * grad_in
    direction = first_new / (1.0 - BETA_ONE ** STEP) / (jnp.sqrt(second_new / (1.0 - BETA_TWO ** STEP)) + ADAM_EPS)
    return (param_in - rate_in * (direction + decay_in * param_in), first_new, second_new)

def reference(images, labels, groups, conv_w, conv_m, conv_v, rot_bases, stem_w, stem_m, stem_v, head_w, head_m, head_v, norm_p, norm_m, norm_v):
    channels = conv_w.shape[1]
    blocks = IMAGES // BLOCK_IMG
    conv_std = to_blocks(conv_w, 18).reshape(18 * channels, channels)
    conv_m_std = to_blocks(conv_m, 18).reshape(18 * channels, channels)
    conv_v_std = to_blocks(conv_v, 18).reshape(18 * channels, channels)
    weights_all = 1.0 + 3.0 * groups.astype(jnp.float32)
    weight_total = jnp.sum(weights_all)
    batches = (images.astype(jnp.float32).reshape(blocks, BLOCK_IMG, SIDE, SIDE, 3), labels.reshape(blocks, BLOCK_IMG), weights_all.reshape(blocks, BLOCK_IMG))
    params = (conv_std, stem_w, head_w, norm_p)

    def objective(params_in, shifts):
        stat_list = [jnp.zeros((2, channels), jnp.float32)] * 3
        for section_id in range(3):
            stat_list[section_id] = block_sum(params_in, tuple(stat_list), section_id, batches) + shifts[section_id]
        loss_sum = block_sum(params_in, tuple(stat_list), 3, batches)
        return (loss_sum / weight_total, (tuple(stat_list), loss_sum))
    shifts = jnp.zeros((3, 2, channels), jnp.float32)
    objective_val, pull_back, aux_vals = jax.vjp(objective, params, shifts, has_aux=True)
    stat_sums, loss_sum = aux_vals
    gradients, lambdas = pull_back(jnp.ones((), jnp.float32))

    def augmented(probes, batch_in):
        pieces = forward_block(params, stat_sums, batch_in, probes, 4)
        total_val = pieces[3] / weight_total
        for section_id in range(3):
            total_val = total_val + jnp.sum(lambdas[section_id] * pieces[section_id])
        return (total_val, (pieces[4], pieces[5]))
    pix_block = BLOCK_IMG * SIDE * SIDE

    def factor_block(totals, batch_in):
        zeros_pix = jnp.zeros((pix_block, channels), jnp.float32)
        out_val, pull_block, hidden = jax.vjp(lambda probe_in: augmented(probe_in, batch_in), (zeros_pix, zeros_pix), has_aux=True)
        back_one, back_two = pull_block(jnp.ones((), jnp.float32))[0]
        update = jnp.stack([dot_high(hidden[0].T, hidden[0]), dot_high(back_one.T, back_one), dot_high(hidden[1].T, hidden[1]), dot_high(back_two.T, back_two)])
        return (totals + update, None)
    factor_sums = lax.scan(factor_block, jnp.zeros((4, channels, channels), jnp.float32), batches)[0]
    scales = jnp.array([1.0 / PIXELS, PIXELS, 1.0 / PIXELS, PIXELS], jnp.float32)
    factors = factor_sums * scales[:, None, None]
    identity = jnp.eye(channels, dtype=jnp.float32)
    traces = jnp.trace(factors, axis1=1, axis2=2)
    damped = factors + (DAMPING * traces / channels)[:, None, None] * identity
    inverse = identity / jnp.sqrt(lax.optimization_barrier(jnp.sum(damped * damped, axis=(1, 2))))[:, None, None]
    for sweep_id in range(NS_ITERS):
        product = jnp.einsum('mab,mbc->mac', inverse, damped, precision=highest)
        inverse = 2.0 * inverse - jnp.einsum('mab,mbc->mac', product, inverse, precision=highest)
    turned = jnp.einsum('mab,mbc->mac', damped, rot_bases, precision=highest)
    gram_mat = jnp.einsum('mba,mbc->mac', turned, turned, precision=highest)
    lower_f = jnp.linalg.cholesky(gram_mat)
    bases_new = lax.linalg.triangular_solve(lower_f, turned, left_side=False, lower=True, transpose_a=True)
    conv_grad, stem_grad, head_grad, norm_grad = gradients
    left_q = rot_bases[0::2]
    right_q = rot_bases[1::2]
    grad_four = conv_grad.reshape(2, 9, channels, channels)
    half_turn = jnp.einsum('lki,ltkn->ltin', left_q, grad_four, precision=highest)
    rotated = jnp.einsum('ltin,lnd->ltid', half_turn, right_q, precision=highest).reshape(18 * channels, channels)
    first_conv = BETA_ONE * conv_m_std + (1.0 - BETA_ONE) * rotated
    second_conv = BETA_TWO * conv_v_std + (1.0 - BETA_TWO) * rotated * rotated
    direction = first_conv / (1.0 - BETA_ONE ** STEP) / (jnp.sqrt(second_conv / (1.0 - BETA_TWO ** STEP)) + ADAM_EPS)
    back_half = jnp.einsum('lik,ltkn->ltin', left_q, direction.reshape(2, 9, channels, channels), precision=highest)
    update = jnp.einsum('ltin,ldn->ltid', back_half, right_q, precision=highest).reshape(18 * channels, channels)
    conv_new_std = conv_std - RATE_CONV * (update + WEIGHT_DECAY * conv_std)

    def back_rows(std_rows):
        return from_blocks(std_rows.reshape(18, channels, channels))
    conv_new = back_rows(conv_new_std)
    stem_new, stem_first, stem_second = adam_step(stem_w, stem_grad, stem_m, stem_v, RATE_STEM, WEIGHT_DECAY)
    head_new, head_first, head_second = adam_step(head_w, head_grad, head_m, head_v, RATE_HEAD, WEIGHT_DECAY)
    norm_new, norm_first, norm_second = adam_step(norm_p, norm_grad, norm_m, norm_v, RATE_NORM, 0.0)
    loss = jnp.stack([loss_sum, weight_total])
    return (loss, from_blocks(factors), from_blocks(inverse), conv_new, back_rows(first_conv), back_rows(second_conv), bases_new, stem_new, stem_first, stem_second, head_new, head_first, head_second, norm_new, norm_first, norm_second, conv_new.astype(jnp.bfloat16))
```

```python
import math

import jax
import jax.numpy as jnp
from jax import lax
from jax.sharding import PartitionSpec as P

CLASSES = 10
NS_ITERS = 6
STEP = 5


EPS_NORM = 1e-05
BETA_ONE = 0.9
BETA_TWO = 0.99
ADAM_EPS = 1e-08
WEIGHT_DECAY = 0.01
DAMPING = 0.1
PROBIT_SCALE = math.pi / 8.0
RATE_CONV = 0.02
RATE_STEM = 0.1
RATE_HEAD = 0.1
RATE_NORM = 0.5
highest = lax.Precision.HIGHEST


def to_blocks(rows_in, count):
    width = rows_in.shape[1]
    return rows_in.reshape(width, count, width).transpose(1, 0, 2)


def from_blocks(stacked):
    return stacked.transpose(1, 0, 2).reshape(-1, stacked.shape[2])


def patches(images_in):
    side_len = images_in.shape[1]
    padded = jnp.pad(images_in, ((0, 0), (1, 1), (1, 1), (0, 0)))
    pieces = [
        padded[:, offset_a : offset_a + side_len, offset_b : offset_b + side_len, :]
        for offset_a in range(3)
        for offset_b in range(3)
    ]
    return jnp.concatenate(pieces, axis=-1).reshape(-1, 9 * images_in.shape[-1])


def inner_rows(left_in, right_in):
    return lax.dot_general(
        left_in, right_in, (((0,), (0,)), ((), ())), preferred_element_type=jnp.float32
    )


def bit_groups(devices):
    total_bits = devices.bit_length() - 1
    groups = [(0, 1)]
    while groups[-1][0] + groups[-1][1] < total_bits:
        first = groups[-1][0] + groups[-1][1]
        groups.append((first, min(2, total_bits - first)))
    return groups


def swap(values, mask, devices):
    return lax.ppermute(values, "dp", [(i, i ^ mask) for i in range(devices)])


def sum_small(values):
    devices = lax.axis_size("dp")
    copies = jnp.broadcast_to(values[None], (devices,) + values.shape)
    return jnp.sum(lax.all_to_all(copies, "dp", 0, 0, tiled=True), axis=0)


def gather_all(piece):
    devices = lax.axis_size("dp")
    me = lax.axis_index("dp")
    groups = bit_groups(devices)[::-1]
    held = piece[(None,) * len(groups)]
    for axis, (first, width) in enumerate(groups):
        radix = 1 << width
        mine = (me >> first) & (radix - 1)
        got = [held] + [swap(held, k << first, devices) for k in range(1, radix)]
        ordered = []
        for j in range(radix):
            value = got[j]
            for m in range(1, radix):
                value = jnp.where(mine == m, got[j ^ m], value)
            ordered.append(value)
        held = jnp.concatenate(ordered, axis=axis)
    return held.reshape((devices,) + piece.shape)


def scatter_sum(pieces, sent_as):
    devices = lax.axis_size("dp")
    me = lax.axis_index("dp")
    groups = bit_groups(devices)
    held = pieces.reshape(tuple(1 << width for _, width in groups[::-1]) + pieces.shape[1:])
    for order, (first, width) in enumerate(groups):
        axis = len(groups) - 1 - order
        radix = 1 << width
        mine = (me >> first) & (radix - 1)
        parts = [lax.dynamic_slice_in_dim(held, mine ^ k, 1, axis=axis) for k in range(radix)]
        total = parts[0].astype(jnp.float32)
        for k in range(1, radix):
            total = total + swap(parts[k].astype(sent_as), k << first, devices).astype(jnp.float32)
        held = total
    return held.reshape(pieces.shape[1:])


def moments(values):
    return jnp.stack([jnp.sum(values, axis=0), jnp.sum(values * values, axis=0)])


def pool_stats(values, extra):
    extra_row = jnp.full((1, values.shape[1]), extra, jnp.float32)
    total = sum_small(jnp.concatenate([moments(values), extra_row], axis=0))
    return total[:2], total[2, 0]


def normalize(values, stat_sums, gain_row, shift_row, pixels):
    mean_val = stat_sums[0] / pixels
    variance = stat_sums[1] / pixels - mean_val * mean_val
    inv_std = lax.rsqrt(variance + EPS_NORM)
    centered = (values - mean_val) * inv_std
    return (centered * gain_row + shift_row, centered, inv_std)


def norm_back(grad_out, centered, inv_std, gain_row, pixels):
    local_sums = jnp.stack([jnp.sum(grad_out, axis=0), jnp.sum(grad_out * centered, axis=0)])
    total_sums = sum_small(local_sums)
    grad_in = (
        inv_std
        * gain_row
        * (grad_out - total_sums[0] / pixels - centered * (total_sums[1] / pixels))
    )
    return (grad_in, total_sums)


def gelu_back(pre_act, grad_out):
    return jax.vjp(jax.nn.gelu, pre_act)[1](grad_out)[0]


def layer_forward(inputs, stat_sums, gain_row, shift_row, weight, pixels, count_img, side_len):
    pre_act, centered, inv_std = normalize(inputs, stat_sums, gain_row, shift_row, pixels)
    hidden = jax.nn.gelu(pre_act).astype(jnp.bfloat16)
    columns = patches(hidden.reshape(count_img, side_len, side_len, -1))
    output = jnp.dot(columns, weight, preferred_element_type=jnp.float32)
    return (output, (pre_act, centered, inv_std, hidden, columns))


def layer_backward(grad_out, kept_vals, gain_row, weight, pixels, count_img, side_len):
    pre_act, centered, inv_std, hidden, columns = kept_vals
    channels = weight.shape[1]
    grad_low = grad_out.astype(jnp.bfloat16)
    weight_grad = inner_rows(columns, grad_low)
    flipped = (
        weight.reshape(9, channels, channels)[::-1]
        .transpose(0, 2, 1)
        .reshape(9 * channels, channels)
    )
    grad_hidden = jnp.dot(
        patches(grad_low.reshape(count_img, side_len, side_len, channels)),
        flipped,
        preferred_element_type=jnp.float32,
    )
    grad_pre = gelu_back(pre_act, grad_hidden)
    grad_in, total_sums = norm_back(grad_pre, centered, inv_std, gain_row, pixels)
    factor_a = inner_rows(hidden, hidden) / pixels
    factor_g = inner_rows(grad_low, grad_low) * pixels
    return (grad_in, weight_grad, total_sums, factor_a, factor_g)


def adam_step(param_in, grad_in, first_in, second_in, rate_in, decay_in):
    first_new = BETA_ONE * first_in + (1.0 - BETA_ONE) * grad_in
    second_new = BETA_TWO * second_in + (1.0 - BETA_TWO) * grad_in * grad_in
    direction = (
        first_new
        / (1.0 - BETA_ONE**STEP)
        / (jnp.sqrt(second_new / (1.0 - BETA_TWO**STEP)) + ADAM_EPS)
    )
    return (param_in - rate_in * (direction + decay_in * param_in), first_new, second_new)


def damp_all(factor_full, channels):
    identity = jnp.eye(channels, dtype=jnp.float32)
    traces = jnp.trace(factor_full, axis1=1, axis2=2)
    return factor_full + (DAMPING * traces / channels)[:, None, None] * identity


def local(
    images,
    labels,
    groups,
    conv_w,
    conv_m,
    conv_v,
    rot_bases,
    stem_w,
    stem_m,
    stem_v,
    head_w,
    head_m,
    head_v,
    norm_p,
    norm_m,
    norm_v,
):
    devices = lax.axis_size("dp")
    my_index = lax.axis_index("dp")
    count_img, side_len = (images.shape[0], images.shape[1])
    channels = conv_w.shape[1]
    pixels = count_img * side_len * side_len * devices
    conv_gathered = gather_all(conv_w.astype(jnp.bfloat16)).reshape(18 * channels, channels)
    conv_full = to_blocks(conv_gathered, 18).reshape(18 * channels, channels)
    weights_img = 1.0 + 3.0 * groups.astype(jnp.float32)
    stem_cols = patches(images)
    stem_out = jnp.dot(stem_cols, stem_w.astype(jnp.bfloat16), preferred_element_type=jnp.float32)
    stat_sums, weight_total = pool_stats(stem_out, jnp.sum(weights_img))
    current = stem_out
    kept_all = []
    for layer_id in range(2):
        if layer_id > 0:
            stat_sums = pool_stats(current, jnp.zeros((), jnp.float32))[0]
        weight = conv_full[layer_id * 9 * channels : (layer_id + 1) * 9 * channels]
        current, kept_vals = layer_forward(
            current,
            stat_sums,
            norm_p[2 * layer_id],
            norm_p[2 * layer_id + 1],
            weight,
            pixels,
            count_img,
            side_len,
        )
        kept_all.append(kept_vals)
    residual = stem_out + current
    stat_sums = pool_stats(residual, jnp.zeros((), jnp.float32))[0]
    pre_last, centered_last, inv_last = normalize(residual, stat_sums, norm_p[4], norm_p[5], pixels)
    features = jax.nn.gelu(pre_last)
    pooled = jnp.mean(features.reshape(count_img, side_len * side_len, channels), axis=1)
    pooled_low = pooled.astype(jnp.bfloat16)
    head_low = head_w[:channels].astype(jnp.bfloat16)
    logits = jnp.dot(pooled_low, head_low, preferred_element_type=jnp.float32) + head_w[channels]
    spread = jnp.mean(pooled * pooled, axis=1)
    shrink = lax.rsqrt(1.0 + PROBIT_SCALE * spread)
    scaled = logits * shrink[:, None]
    targets = (labels[:, None] == jnp.arange(CLASSES, dtype=jnp.int32)[None, :]).astype(jnp.float32)
    log_total = jax.nn.logsumexp(scaled, axis=1)
    loss_local = jnp.sum(weights_img * (log_total - jnp.sum(scaled * targets, axis=1)))
    grad_scaled = (jnp.exp(scaled - log_total[:, None]) - targets) * (weights_img / weight_total)[
        :, None
    ]
    grad_logits = (grad_scaled * shrink[:, None]).astype(jnp.bfloat16)
    grad_shrink = jnp.sum(grad_scaled * logits, axis=1)
    grad_spread = grad_shrink * (-0.5 * PROBIT_SCALE) * shrink * shrink * shrink
    grad_pooled = lax.dot_general(
        grad_logits, head_low, (((1,), (1,)), ((), ())), preferred_element_type=jnp.float32
    )
    grad_pooled = grad_pooled + grad_spread[:, None] * 2.0 * pooled / channels
    head_grad = jnp.concatenate(
        [
            inner_rows(pooled_low, grad_logits),
            jnp.sum(grad_logits.astype(jnp.float32), axis=0)[None, :],
        ],
        axis=0,
    )
    grad_feat = jnp.broadcast_to(
        grad_pooled[:, None, :] / (side_len * side_len), (count_img, side_len * side_len, channels)
    ).reshape(-1, channels)
    grad_res, sums_last = norm_back(
        gelu_back(pre_last, grad_feat), centered_last, inv_last, norm_p[4], pixels
    )
    current = grad_res
    conv_grads = [None, None]
    norm_sums = [None, None, sums_last]
    factor_list = [None, None, None, None]
    for layer_id in (1, 0):
        weight = conv_full[layer_id * 9 * channels : (layer_id + 1) * 9 * channels]
        current, weight_grad, total_sums, factor_a, factor_g = layer_backward(
            current, kept_all[layer_id], norm_p[2 * layer_id], weight, pixels, count_img, side_len
        )
        conv_grads[layer_id] = weight_grad
        norm_sums[layer_id] = total_sums
        factor_list[2 * layer_id] = factor_a
        factor_list[2 * layer_id + 1] = factor_g
    grad_stem_out = (current + grad_res).astype(jnp.bfloat16)
    stem_grad = inner_rows(stem_cols, grad_stem_out)
    norm_grad = jnp.stack(
        [
            norm_sums[0][1],
            norm_sums[0][0],
            norm_sums[1][1],
            norm_sums[1][0],
            norm_sums[2][1],
            norm_sums[2][0],
        ]
    )
    factor_stack = from_blocks(jnp.stack(factor_list))
    factor_count = factor_stack.shape[0] // devices
    identity = jnp.eye(channels, dtype=jnp.float32)
    row_factor = scatter_sum(
        factor_stack.reshape(devices, factor_count, channels), jnp.float32
    )
    factor_all = gather_all(row_factor).reshape(4 * channels, channels)
    factor_full = to_blocks(factor_all, 4)
    damped = damp_all(factor_full, channels)
    inverse = identity / jnp.sqrt(jnp.sum(damped * damped, axis=(1, 2)))[:, None, None]
    for sweep_id in range(NS_ITERS):
        product = jnp.einsum("mab,mbc->mac", inverse, damped, precision=highest)
        inverse = 2.0 * inverse - jnp.einsum("mab,mbc->mac", product, inverse, precision=highest)
    inverse_rows = lax.dynamic_slice_in_dim(
        from_blocks(inverse), my_index * factor_count, factor_count, 0
    )
    turned = jnp.einsum("mab,mbc->mac", damped, rot_bases, precision=highest)
    gram_mat = jnp.einsum("mba,mbc->mac", turned, turned, precision=highest)
    lower_f = jnp.linalg.cholesky(gram_mat)
    bases_new = lax.linalg.triangular_solve(
        lower_f, turned, left_side=False, lower=True, transpose_a=True
    )
    left_q = rot_bases[0::2]
    right_q = rot_bases[1::2]
    row_channels = channels // devices
    tail_sums = jnp.concatenate(
        [
            stem_grad,
            jnp.pad(head_grad.T, ((0, 0), (0, 2 * channels - head_grad.shape[0]))).reshape(-1, channels),
            jnp.full((1, channels), loss_local, jnp.float32),
        ],
        axis=0,
    )
    tail_total = sum_small(tail_sums)
    stem_rows = stem_w.shape[0]
    stem_total = tail_total[:stem_rows]
    head_total = tail_total[stem_rows : stem_rows + 2 * CLASSES].reshape(CLASSES, 2 * channels).T[: channels + 1]
    loss_total = tail_total[-1, 0]
    right_rot = []
    for layer_id in range(2):
        left_turned = jnp.einsum(
            "ki,tkn->itn",
            left_q[layer_id],
            conv_grads[layer_id].reshape(9, channels, channels),
            precision=lax.Precision.HIGH,
        )
        own_rows = scatter_sum(
            left_turned.astype(jnp.bfloat16).reshape(devices, row_channels, 9, channels), jnp.bfloat16
        )
        right_rot.append(jnp.einsum("rtn,nd->rtd", own_rows, right_q[layer_id], precision=highest))
    rotated = jnp.stack(right_rot, axis=1).reshape(-1, channels)
    first_conv = BETA_ONE * conv_m + (1.0 - BETA_ONE) * rotated
    second_conv = BETA_TWO * conv_v + (1.0 - BETA_TWO) * rotated * rotated
    direction = (
        first_conv
        / (1.0 - BETA_ONE**STEP)
        / (jnp.sqrt(second_conv / (1.0 - BETA_TWO**STEP)) + ADAM_EPS)
    )
    direction_own = direction.reshape(row_channels, 2, 9, channels)
    updates = []
    for layer_id in range(2):
        half = jnp.einsum(
            "rtn,dn->rtd", direction_own[:, layer_id], right_q[layer_id], precision=highest
        )
        full = gather_all(half.astype(jnp.bfloat16)).reshape(channels, 9 * channels)
        own_left = lax.dynamic_slice_in_dim(left_q[layer_id], my_index * row_channels, row_channels, 0)
        updates.append(
            jnp.dot(own_left.astype(jnp.bfloat16), full, preferred_element_type=jnp.float32).reshape(
                row_channels, 9, channels
            )
        )
    update = jnp.stack(updates, axis=1).reshape(-1, channels)
    conv_new = conv_w - RATE_CONV * (update + WEIGHT_DECAY * conv_w)
    stem_new, stem_first, stem_second = adam_step(
        stem_w, stem_total, stem_m, stem_v, RATE_STEM, WEIGHT_DECAY
    )
    head_new, head_first, head_second = adam_step(
        head_w, head_total, head_m, head_v, RATE_HEAD, WEIGHT_DECAY
    )
    norm_new, norm_first, norm_second = adam_step(norm_p, norm_grad, norm_m, norm_v, RATE_NORM, 0.0)
    loss = jnp.stack([loss_total, weight_total])
    return (
        loss,
        row_factor,
        inverse_rows,
        conv_new,
        first_conv,
        second_conv,
        bases_new,
        stem_new,
        stem_first,
        stem_second,
        head_new,
        head_first,
        head_second,
        norm_new,
        norm_first,
        norm_second,
        conv_new.astype(jnp.bfloat16),
    )


def solution(mesh):
    return jax.shard_map(
        local,
        mesh=mesh,
        in_specs=(
            P("dp", None, None, None),
            P("dp"),
            P("dp"),
            P("dp", None),
            P("dp", None),
            P("dp", None),
            P(),
            P(),
            P(),
            P(),
            P(),
            P(),
            P(),
            P(),
            P(),
            P(),
        ),
        out_specs=(
            P(),
            P("dp", None),
            P("dp", None),
            P("dp", None),
            P("dp", None),
            P("dp", None),
            P(),
            P(),
            P(),
            P(),
            P(),
            P(),
            P(),
            P(),
            P(),
            P(),
            P("dp", None),
        ),
        check_vma=False,
    )
```

```python
import functools
import math

import jax
import jax.numpy as jnp
from jax import lax
from jax.experimental import pallas as pl
from jax.experimental.pallas import tpu as pltpu
from jax.sharding import PartitionSpec as P

CLASSES = 10
NS_ITERS = 6
STEP = 5


EPS_NORM = 1e-05
BETA_ONE = 0.9
BETA_TWO = 0.99
ADAM_EPS = 1e-08
WEIGHT_DECAY = 0.01
DAMPING = 0.1
PROBIT_SCALE = math.pi / 8.0
RATE_CONV = 0.02
RATE_STEM = 0.1
RATE_HEAD = 0.1
RATE_NORM = 0.5
highest = lax.Precision.HIGHEST


def to_blocks(rows_in, count):
    width = rows_in.shape[1]
    return rows_in.reshape(width, count, width).transpose(1, 0, 2)


def from_blocks(stacked):
    return stacked.transpose(1, 0, 2).reshape(-1, stacked.shape[2])


def patches(images_in):
    side_len = images_in.shape[1]
    padded = jnp.pad(images_in, ((0, 0), (1, 1), (1, 1), (0, 0)))
    pieces = [
        padded[:, offset_a : offset_a + side_len, offset_b : offset_b + side_len, :]
        for offset_a in range(3)
        for offset_b in range(3)
    ]
    return jnp.concatenate(pieces, axis=-1).reshape(-1, 9 * images_in.shape[-1])


def inner_rows(left_in, right_in):
    return lax.dot_general(
        left_in, right_in, (((0,), (0,)), ((), ())), preferred_element_type=jnp.float32
    )


def bit_groups(devices):
    total_bits = devices.bit_length() - 1
    groups = [(0, 1)]
    while groups[-1][0] + groups[-1][1] < total_bits:
        first = groups[-1][0] + groups[-1][1]
        groups.append((first, min(2, total_bits - first)))
    return groups


def swap(values, mask, devices):
    return lax.ppermute(values, "dp", [(i, i ^ mask) for i in range(devices)])


def sum_small(values):
    devices = lax.axis_size("dp")
    copies = jnp.broadcast_to(values[None], (devices,) + values.shape)
    return jnp.sum(lax.all_to_all(copies, "dp", 0, 0, tiled=True), axis=0)


def gather_all(piece):
    devices = lax.axis_size("dp")
    me = lax.axis_index("dp")
    groups = bit_groups(devices)[::-1]
    held = piece[(None,) * len(groups)]
    for axis, (first, width) in enumerate(groups):
        radix = 1 << width
        mine = (me >> first) & (radix - 1)
        got = [held] + [swap(held, k << first, devices) for k in range(1, radix)]
        ordered = []
        for j in range(radix):
            value = got[j]
            for m in range(1, radix):
                value = jnp.where(mine == m, got[j ^ m], value)
            ordered.append(value)
        held = jnp.concatenate(ordered, axis=axis)
    return held.reshape((devices,) + piece.shape)


def scatter_sum(pieces, sent_as):
    devices = lax.axis_size("dp")
    me = lax.axis_index("dp")
    groups = bit_groups(devices)
    held = pieces.reshape(tuple(1 << width for _, width in groups[::-1]) + pieces.shape[1:])
    for order, (first, width) in enumerate(groups):
        axis = len(groups) - 1 - order
        radix = 1 << width
        mine = (me >> first) & (radix - 1)
        parts = [lax.dynamic_slice_in_dim(held, mine ^ k, 1, axis=axis) for k in range(radix)]
        total = parts[0].astype(jnp.float32)
        for k in range(1, radix):
            total = total + swap(parts[k].astype(sent_as), k << first, devices).astype(jnp.float32)
        held = total
    return held.reshape(pieces.shape[1:])


def moments(values):
    return jnp.stack([jnp.sum(values, axis=0), jnp.sum(values * values, axis=0)])


def pool_stats(values, extra):
    extra_row = jnp.full((1, values.shape[1]), extra, jnp.float32)
    total = sum_small(jnp.concatenate([moments(values), extra_row], axis=0))
    return total[:2], total[2, 0]


def normalize(values, stat_sums, gain_row, shift_row, pixels):
    mean_val = stat_sums[0] / pixels
    variance = stat_sums[1] / pixels - mean_val * mean_val
    inv_std = lax.rsqrt(variance + EPS_NORM)
    centered = (values - mean_val) * inv_std
    return (centered * gain_row + shift_row, centered, inv_std)


def norm_back(grad_out, centered, inv_std, gain_row, pixels):
    local_sums = jnp.stack([jnp.sum(grad_out, axis=0), jnp.sum(grad_out * centered, axis=0)])
    total_sums = sum_small(local_sums)
    grad_in = (
        inv_std
        * gain_row
        * (grad_out - total_sums[0] / pixels - centered * (total_sums[1] / pixels))
    )
    return (grad_in, total_sums)


def gelu_back(pre_act, grad_out):
    return jax.vjp(jax.nn.gelu, pre_act)[1](grad_out)[0]


def layer_forward(inputs, stat_sums, gain_row, shift_row, weight, pixels, count_img, side_len):
    pre_act, centered, inv_std = normalize(inputs, stat_sums, gain_row, shift_row, pixels)
    hidden = jax.nn.gelu(pre_act).astype(jnp.bfloat16)
    columns = patches(hidden.reshape(count_img, side_len, side_len, -1))
    output = jnp.dot(columns, weight, preferred_element_type=jnp.float32)
    return (output, (pre_act, centered, inv_std, hidden, columns))


def layer_backward(grad_out, kept_vals, gain_row, weight, pixels, count_img, side_len):
    pre_act, centered, inv_std, hidden, columns = kept_vals
    channels = weight.shape[1]
    grad_low = grad_out.astype(jnp.bfloat16)
    weight_grad = inner_rows(columns, grad_low)
    flipped = (
        weight.reshape(9, channels, channels)[::-1]
        .transpose(0, 2, 1)
        .reshape(9 * channels, channels)
    )
    grad_hidden = jnp.dot(
        patches(grad_low.reshape(count_img, side_len, side_len, channels)),
        flipped,
        preferred_element_type=jnp.float32,
    )
    grad_pre = gelu_back(pre_act, grad_hidden)
    grad_in, total_sums = norm_back(grad_pre, centered, inv_std, gain_row, pixels)
    factor_a = inner_rows(hidden, hidden) / pixels
    factor_g = inner_rows(grad_low, grad_low) * pixels
    return (grad_in, weight_grad, total_sums, factor_a, factor_g)


def adam_step(param_in, grad_in, first_in, second_in, rate_in, decay_in):
    first_new = BETA_ONE * first_in + (1.0 - BETA_ONE) * grad_in
    second_new = BETA_TWO * second_in + (1.0 - BETA_TWO) * grad_in * grad_in
    direction = (
        first_new
        / (1.0 - BETA_ONE**STEP)
        / (jnp.sqrt(second_new / (1.0 - BETA_TWO**STEP)) + ADAM_EPS)
    )
    return (param_in - rate_in * (direction + decay_in * param_in), first_new, second_new)


def dotp(a,b,dims=((1,),(0,)),prec=highest):
    return lax.dot_general(a,b,(dims,((),())),precision=prec,preferred_element_type=jnp.float32)
def split(a):
    hi=a.astype(jnp.bfloat16)
    return hi,(a-hi.astype(jnp.float32)).astype(jnp.bfloat16)
def dot3(a,b,dims=((1,),(0,))):
    ah,al=split(a); bh,bl=split(b)
    d=lambda x,y: lax.dot_general(x,y,(dims,((),())),preferred_element_type=jnp.float32)
    return d(ah,bh)+(d(ah,bl)+d(al,bh))
def fac_kernel(f_ref,q_ref,inv_ref,qn_ref,b_ref,*,nb):
    n=f_ref.shape[1]; M4=f_ref.shape[0]
    r=lax.broadcasted_iota(jnp.int32,(n,n),0); c=lax.broadcasted_iota(jnp.int32,(n,n),1)
    eye=(r==c).astype(jnp.float32)
    Ms=[]
    for m in range(M4):
        F=f_ref[m]
        tr=jnp.sum(F*eye)
        M=F+(DAMPING*tr/n)*eye
        Ms.append(M)
    if True:
        for m in range(M4):
            Yt=dotp(q_ref[m],Ms[m],((0,),(0,)))
            b_ref[m,:,n:]=Yt
            b_ref[m,:,:n]=dotp(Yt,Yt,((1,),(1,)))
        ri=lax.broadcasted_iota(jnp.int32,(M4,nb,128),1); li=lax.broadcasted_iota(jnp.int32,(M4,nb,128),2)
        for k in range(n//nb):
            lo=k*nb; t0=(lo//128)*128; off=lo-t0
            D=b_ref[:,lo:lo+nb,t0:t0+128]
            if off: D=pltpu.roll(D,128-off,2)
            V=jnp.where(li<nb,D,jnp.where(li-nb==ri,1.0,0.0)) if nb<128 else D
            for j in range(nb):
                s=8*(j//8)
                row=V[:,j:j+1,:]
                act=V[:,s:,:]
                col=act[:,:,j:j+1]
                d=row[:,:,j:j+1]
                fac=jnp.where(ri[:,s:,:1]>j,col,0.0)
                upd=act-fac*(row*(1.0/d))
                V=jnp.concatenate([V[:,:s,:],upd],axis=1) if s else upd
            dv=jnp.sum(jnp.where(ri==li,V,0.0),axis=2,keepdims=True)
            E=V[:,:,nb:]*lax.rsqrt(dv)
            for m in range(M4):
                Li=E[m]
                U=dotp(Li,b_ref[m,lo:lo+nb,:])
                b_ref[m,lo:lo+nb,:]=U
                if lo+nb<n:
                    b_ref[m,lo+nb:,:]=b_ref[m,lo+nb:,:]-dotp(U[:,lo+nb:n],U,((0,),(0,)))
        for m in range(M4):
            qn_ref[m]=b_ref[m,:,n:].T
    if True:
        for m in range(M4):
            M=Ms[m]
            X=eye*lax.rsqrt(jnp.sum(M*M))
            for _ in range(NS_ITERS):
                X=2.0*X-dot3(dot3(X,M),X)
            inv_ref[m]=X
def fac(F,Q,nb=64):
    m,n,_=F.shape
    return pl.pallas_call(functools.partial(fac_kernel,nb=nb),
        out_shape=(jax.ShapeDtypeStruct((m,n,n),jnp.float32),)*2,
        scratch_shapes=[pltpu.VMEM((m,n,2*n),jnp.float32)],
        compiler_params=pltpu.CompilerParams(vmem_limit_bytes=48*2**20),
        name="factor_chain")(F,Q)


def local(
    images,
    labels,
    groups,
    conv_w,
    conv_m,
    conv_v,
    rot_bases,
    stem_w,
    stem_m,
    stem_v,
    head_w,
    head_m,
    head_v,
    norm_p,
    norm_m,
    norm_v,
):
    devices = lax.axis_size("dp")
    my_index = lax.axis_index("dp")
    count_img, side_len = (images.shape[0], images.shape[1])
    channels = conv_w.shape[1]
    pixels = count_img * side_len * side_len * devices
    conv_gathered = gather_all(conv_w.astype(jnp.bfloat16)).reshape(18 * channels, channels)
    conv_full = to_blocks(conv_gathered, 18).reshape(18 * channels, channels)
    weights_img = 1.0 + 3.0 * groups.astype(jnp.float32)
    stem_cols = patches(images)
    stem_out = jnp.dot(stem_cols, stem_w.astype(jnp.bfloat16), preferred_element_type=jnp.float32)
    stat_sums, weight_total = pool_stats(stem_out, jnp.sum(weights_img))
    current = stem_out
    kept_all = []
    for layer_id in range(2):
        if layer_id > 0:
            stat_sums = pool_stats(current, jnp.zeros((), jnp.float32))[0]
        weight = conv_full[layer_id * 9 * channels : (layer_id + 1) * 9 * channels]
        current, kept_vals = layer_forward(
            current,
            stat_sums,
            norm_p[2 * layer_id],
            norm_p[2 * layer_id + 1],
            weight,
            pixels,
            count_img,
            side_len,
        )
        kept_all.append(kept_vals)
    residual = stem_out + current
    stat_sums = pool_stats(residual, jnp.zeros((), jnp.float32))[0]
    pre_last, centered_last, inv_last = normalize(residual, stat_sums, norm_p[4], norm_p[5], pixels)
    features = jax.nn.gelu(pre_last)
    pooled = jnp.mean(features.reshape(count_img, side_len * side_len, channels), axis=1)
    pooled_low = pooled.astype(jnp.bfloat16)
    head_low = head_w[:channels].astype(jnp.bfloat16)
    logits = jnp.dot(pooled_low, head_low, preferred_element_type=jnp.float32) + head_w[channels]
    spread = jnp.mean(pooled * pooled, axis=1)
    shrink = lax.rsqrt(1.0 + PROBIT_SCALE * spread)
    scaled = logits * shrink[:, None]
    targets = (labels[:, None] == jnp.arange(CLASSES, dtype=jnp.int32)[None, :]).astype(jnp.float32)
    log_total = jax.nn.logsumexp(scaled, axis=1)
    loss_local = jnp.sum(weights_img * (log_total - jnp.sum(scaled * targets, axis=1)))
    grad_scaled = (jnp.exp(scaled - log_total[:, None]) - targets) * (weights_img / weight_total)[
        :, None
    ]
    grad_logits = (grad_scaled * shrink[:, None]).astype(jnp.bfloat16)
    grad_shrink = jnp.sum(grad_scaled * logits, axis=1)
    grad_spread = grad_shrink * (-0.5 * PROBIT_SCALE) * shrink * shrink * shrink
    grad_pooled = lax.dot_general(
        grad_logits, head_low, (((1,), (1,)), ((), ())), preferred_element_type=jnp.float32
    )
    grad_pooled = grad_pooled + grad_spread[:, None] * 2.0 * pooled / channels
    head_grad = jnp.concatenate(
        [
            inner_rows(pooled_low, grad_logits),
            jnp.sum(grad_logits.astype(jnp.float32), axis=0)[None, :],
        ],
        axis=0,
    )
    grad_feat = jnp.broadcast_to(
        grad_pooled[:, None, :] / (side_len * side_len), (count_img, side_len * side_len, channels)
    ).reshape(-1, channels)
    grad_res, sums_last = norm_back(
        gelu_back(pre_last, grad_feat), centered_last, inv_last, norm_p[4], pixels
    )
    current = grad_res
    conv_grads = [None, None]
    norm_sums = [None, None, sums_last]
    factor_list = [None, None, None, None]
    for layer_id in (1, 0):
        weight = conv_full[layer_id * 9 * channels : (layer_id + 1) * 9 * channels]
        current, weight_grad, total_sums, factor_a, factor_g = layer_backward(
            current, kept_all[layer_id], norm_p[2 * layer_id], weight, pixels, count_img, side_len
        )
        conv_grads[layer_id] = weight_grad
        norm_sums[layer_id] = total_sums
        factor_list[2 * layer_id] = factor_a
        factor_list[2 * layer_id + 1] = factor_g
    grad_stem_out = (current + grad_res).astype(jnp.bfloat16)
    stem_grad = inner_rows(stem_cols, grad_stem_out)
    norm_grad = jnp.stack(
        [
            norm_sums[0][1],
            norm_sums[0][0],
            norm_sums[1][1],
            norm_sums[1][0],
            norm_sums[2][1],
            norm_sums[2][0],
        ]
    )
    factor_stack = from_blocks(jnp.stack(factor_list))
    factor_count = factor_stack.shape[0] // devices
    row_factor = scatter_sum(
        factor_stack.reshape(devices, factor_count, channels), jnp.float32
    )
    factor_all = gather_all(row_factor).reshape(4 * channels, channels)
    factor_full = to_blocks(factor_all, 4)
    inverse, bases_new = fac(factor_full, rot_bases)
    inverse_rows = lax.dynamic_slice_in_dim(
        from_blocks(inverse), my_index * factor_count, factor_count, 0
    )
    left_q = rot_bases[0::2]
    right_q = rot_bases[1::2]
    row_channels = channels // devices
    tail_sums = jnp.concatenate(
        [
            stem_grad,
            jnp.pad(head_grad.T, ((0, 0), (0, 2 * channels - head_grad.shape[0]))).reshape(-1, channels),
            jnp.full((1, channels), loss_local, jnp.float32),
        ],
        axis=0,
    )
    tail_total = sum_small(tail_sums)
    stem_rows = stem_w.shape[0]
    stem_total = tail_total[:stem_rows]
    head_total = tail_total[stem_rows : stem_rows + 2 * CLASSES].reshape(CLASSES, 2 * channels).T[: channels + 1]
    loss_total = tail_total[-1, 0]
    right_rot = []
    for layer_id in range(2):
        left_turned = jnp.einsum(
            "ki,tkn->itn",
            left_q[layer_id],
            conv_grads[layer_id].reshape(9, channels, channels),
            precision=lax.Precision.HIGH,
        )
        own_rows = scatter_sum(
            left_turned.reshape(devices, row_channels, 9, channels), jnp.float32
        )
        right_rot.append(jnp.einsum("rtn,nd->rtd", own_rows, right_q[layer_id], precision=highest))
    rotated = jnp.stack(right_rot, axis=1).reshape(-1, channels)
    first_conv = BETA_ONE * conv_m + (1.0 - BETA_ONE) * rotated
    second_conv = BETA_TWO * conv_v + (1.0 - BETA_TWO) * rotated * rotated
    direction = (
        first_conv
        / (1.0 - BETA_ONE**STEP)
        / (jnp.sqrt(second_conv / (1.0 - BETA_TWO**STEP)) + ADAM_EPS)
    )
    direction_own = direction.reshape(row_channels, 2, 9, channels)
    updates = []
    for layer_id in range(2):
        half = jnp.einsum(
            "rtn,dn->rtd", direction_own[:, layer_id], right_q[layer_id], precision=highest
        )
        full = gather_all(half.astype(jnp.bfloat16)).reshape(channels, 9 * channels)
        own_left = lax.dynamic_slice_in_dim(left_q[layer_id], my_index * row_channels, row_channels, 0)
        updates.append(
            jnp.dot(own_left.astype(jnp.bfloat16), full, preferred_element_type=jnp.float32).reshape(
                row_channels, 9, channels
            )
        )
    update = jnp.stack(updates, axis=1).reshape(-1, channels)
    conv_new = conv_w - RATE_CONV * (update + WEIGHT_DECAY * conv_w)
    stem_new, stem_first, stem_second = adam_step(
        stem_w, stem_total, stem_m, stem_v, RATE_STEM, WEIGHT_DECAY
    )
    head_new, head_first, head_second = adam_step(
        head_w, head_total, head_m, head_v, RATE_HEAD, WEIGHT_DECAY
    )
    norm_new, norm_first, norm_second = adam_step(norm_p, norm_grad, norm_m, norm_v, RATE_NORM, 0.0)
    loss = jnp.stack([loss_total, weight_total])
    return (
        loss,
        row_factor,
        inverse_rows,
        conv_new,
        first_conv,
        second_conv,
        bases_new,
        stem_new,
        stem_first,
        stem_second,
        head_new,
        head_first,
        head_second,
        norm_new,
        norm_first,
        norm_second,
        conv_new.astype(jnp.bfloat16),
    )


def solution(mesh):
    return jax.shard_map(
        local,
        mesh=mesh,
        in_specs=(
            P("dp", None, None, None),
            P("dp"),
            P("dp"),
            P("dp", None),
            P("dp", None),
            P("dp", None),
            P(),
            P(),
            P(),
            P(),
            P(),
            P(),
            P(),
            P(),
            P(),
            P(),
        ),
        out_specs=(
            P(),
            P("dp", None),
            P("dp", None),
            P("dp", None),
            P("dp", None),
            P("dp", None),
            P(),
            P(),
            P(),
            P(),
            P(),
            P(),
            P(),
            P(),
            P(),
            P(),
            P("dp", None),
        ),
        check_vma=False,
    )
```

```python
import functools
import math

import jax
import jax.numpy as jnp
from jax import lax
from jax.experimental import pallas as pl
from jax.experimental.pallas import tpu as pltpu
from jax.sharding import PartitionSpec as P

NS_ITERS=6; DAMPING=0.1
highest=HI=lax.Precision.HIGHEST
def dotp(a,b,dims=((1,),(0,)),prec=HI):
    return lax.dot_general(a,b,(dims,((),())),precision=prec,preferred_element_type=jnp.float32)
def split(a):
    hi=a.astype(jnp.bfloat16)
    return hi,(a-hi.astype(jnp.float32)).astype(jnp.bfloat16)
def dot3(a,b,dims=((1,),(0,))):
    ah,al=split(a); bh,bl=split(b)
    d=lambda x,y: lax.dot_general(x,y,(dims,((),())),preferred_element_type=jnp.float32)
    return d(ah,bh)+(d(ah,bl)+d(al,bh))
def inverse_kernel(me_ref,all_ref,inv_ref,fac_ref,m_ref,p_ref,x_ref):
    devices,_,n=all_ref.shape
    own=n//devices
    M4=4
    me=me_ref[0]
    r=lax.broadcasted_iota(jnp.int32,(n,n),0); c=lax.broadcasted_iota(jnp.int32,(n,n),1)
    eye=(r==c).astype(jnp.float32)
    each=all_ref.shape[1]-2*own
    Fs=[]
    for k in range(2):
        for j in range(devices): p_ref[j*own:(j+1)*own,:]=all_ref[j,k*own:(k+1)*own,:]
        P=p_ref[...]
        Pt=P.T
        diag=all_ref[(DIAG+k)//each,2*own+(DIAG+k)%each:2*own+(DIAG+k)%each+1,:]
        Fs.append(jnp.where(r<=c,P,Pt))
        Fs.append(jnp.where(r==c,diag,jnp.where(r>c,P,Pt)))
    start=pl.multiple_of(me*own,own)
    def own_rows(out_ref):
        for m in range(M4):
            rows=x_ref[m,pl.ds(start,own),:]
            for i in range(own): out_ref[M4*i+m:M4*i+m+1,:]=rows[i:i+1,:]
    Ms=[]
    for m in range(M4):
        F=Fs[m]
        tr=jnp.sum(F*eye)
        M=F+(DAMPING*tr/n)*eye
        Ms.append(M)
        m_ref[m]=M
        x_ref[m]=F
    own_rows(fac_ref)
    Xs=[eye*lax.rsqrt(jnp.sum(M*M)) for M in Ms]
    for _ in range(NS_ITERS):
        products=[dot3(X,M) for X,M in zip(Xs,Ms)]
        Xs=[2.0*X-dot3(p,X) for p,X in zip(products,Xs)]
    for m in range(M4): x_ref[m]=Xs[m]
    own_rows(inv_ref)

def inverses(me,everything,m4):
    devices,_,n=everything.shape
    own=n//devices
    return pl.pallas_call(inverse_kernel,
        out_shape=(jax.ShapeDtypeStruct((m4*own,n),jnp.float32),jax.ShapeDtypeStruct((m4*own,n),jnp.float32),jax.ShapeDtypeStruct((m4,n,n),jnp.float32)),
        in_specs=[pl.BlockSpec(memory_space=pltpu.SMEM)]+[pl.BlockSpec(memory_space=pltpu.VMEM)],
        scratch_shapes=[pltpu.VMEM((n,n),jnp.float32),pltpu.VMEM((m4,n,n),jnp.float32)],
        compiler_params=pltpu.CompilerParams(vmem_limit_bytes=48*2**20),
        cost_estimate=takes(11.0),name="damped_inverses")(me,everything)

def sub(row, like):
    return jnp.broadcast_to(row,like.shape)

def bases_kernel(m_ref,q_ref,qn_ref,b_ref):
    M4,n,_=m_ref.shape
    nb=64
    for m in range(M4):
        Yt=dotp(q_ref[m],m_ref[m],((0,),(0,)))
        b_ref[m,:,n:]=Yt
        b_ref[m,:,:n]=dotp(Yt,Yt,((1,),(1,)))
    li=lax.broadcasted_iota(jnp.int32,(8,128),1); si=lax.broadcasted_iota(jnp.int32,(8,128),0)
    tiles=nb//8
    for k in range(n//nb):
        lo=k*nb; t0=(lo//128)*128; off=lo-t0
        V=[]
        for m in range(M4):
            D=b_ref[m,lo:lo+nb,t0:t0+128]
            if off: D=pltpu.roll(D,128-off,1)
            V.append([jnp.where(li<nb,D[8*i:8*i+8],jnp.where(li-nb==si+8*i,1.0,0.0)) for i in range(tiles)])
        rows=[[None]*tiles for _ in range(M4)]
        for b in range(tiles):
            pivots=[[jnp.broadcast_to(V[m][b][:,8*b+j:8*b+j+1],(8,128)) for j in range(8)] for m in range(M4)]
            below=[[[jnp.broadcast_to(V[m][i][:,8*b+j:8*b+j+1],(8,128)) for j in range(8)] for i in range(b+1,tiles)] for m in range(M4)]
            R=[V[m][b] for m in range(M4)]
            kept=[R[m] for m in range(M4)]
            size=[pivots[m][0] for m in range(M4)]
            for j in range(8):
                for m in range(M4):
                    col=pivots[m][j]
                    d=sub(col[j:j+1],col)
                    at=si==j
                    kept[m]=jnp.where(at,R[m],kept[m])
                    size[m]=jnp.where(at,d,size[m])
                    inv=1.0/d
                    rj=sub(R[m][j:j+1],R[m])*inv
                    for q in range(j+1,8):
                        pj=sub(pivots[m][q][j:j+1],col)*inv
                        pivots[m][q]=jnp.where(at,pj,pivots[m][q]-col*pj)
                    R[m]=jnp.where(at,rj,R[m]-col*rj)
            for m in range(M4):
                rows[m][b]=kept[m]*lax.rsqrt(size[m])
                spread=[sub(R[m][j:j+1],R[m]) for j in range(8)]
                for i in range(b+1,tiles):
                    cols=below[m][i-b-1]
                    terms=[cols[j]*spread[j] for j in range(8)]
                    while len(terms)>1: terms=[terms[z]+terms[z+1] for z in range(0,len(terms),2)]
                    V[m][i]=V[m][i]-terms[0]
        for m in range(M4):
            E=jnp.concatenate(rows[m],axis=0)[:,nb:2*nb]
            U=dotp(E,b_ref[m,lo:lo+nb,:])
            b_ref[m,lo:lo+nb,:]=U
            if lo+nb<n:
                b_ref[m,lo+nb:,:]=b_ref[m,lo+nb:,:]-dotp(U[:,lo+nb:n],U,((0,),(0,)))
    for m in range(M4):
        qn_ref[m]=b_ref[m,:,n:].T

def new_bases(damped,Q):
    m,n,_=Q.shape
    return pl.pallas_call(bases_kernel,
        out_shape=jax.ShapeDtypeStruct((m,n,n),jnp.float32),
        scratch_shapes=[pltpu.VMEM((m,n,2*n),jnp.float32)],
        compiler_params=pltpu.CompilerParams(vmem_limit_bytes=48*2**20),
        cost_estimate=takes(30.0),name="new_bases")(damped,Q)

EPS_NORM=1e-5
BF=jnp.bfloat16; F32=jnp.float32
MSG=384
ROOT=math.sqrt(2.0/math.pi)
def takes(micros):
    return pl.CostEstimate(flops=int(micros*1.0e9),bytes_accessed=int(micros*3.0e6),transcendentals=0)

PARAMS=pltpu.CompilerParams(vmem_limit_bytes=48*2**20)

def mm(a,b,dims=((1,),(0,))):
    return lax.dot_general(a,b,(dims,((),())),preferred_element_type=F32)

def gelu_parts(x, need_value=True, need_slope=False):
    sq=x*x
    t=jnp.tanh(x*(ROOT+(ROOT*0.044715)*sq))
    half=0.5+0.5*t
    value=x*half if need_value else None
    slope=None
    if need_slope:
        slope=half+(0.5*x)*(1.0-t*t)*(ROOT+(3.0*ROOT*0.044715)*sq)
    return value,slope

def fold_norm(sums, gain, shift, pixels):
    mean=sums[0:1]/pixels
    var=sums[1:2]/pixels-mean*mean
    inv=lax.rsqrt(var+EPS_NORM)
    return mean,inv,gain*inv,shift-mean*(gain*inv)

def shift_taps(v, side):
    col=lax.broadcasted_iota(jnp.int32,v.shape,0)%side
    n=v.shape[0]
    left=jnp.where(col==0,0.0,pltpu.roll(v,1,0))
    right=jnp.where(col==side-1,0.0,pltpu.roll(v,n-1,0))
    return left,right

def clear_borders(p3, side):
    b,rows,w=p3.shape
    for i in range(b):
        p3[i,0:side,:]=jnp.zeros((side,w),BF)
        p3[i,rows-side:rows,:]=jnp.zeros((side,w),BF)

def put_taps(p3, i, v, side):
    n,c=v.shape
    left,right=shift_taps(v,side)
    p3[i,side:side+n,0:c]=left.astype(BF)
    p3[i,side:side+n,c:2*c]=v.astype(BF)
    p3[i,side:side+n,2*c:3*c]=right.astype(BF)

def tap_dots(p3, w_ref, i, n, side, c, back):
    acc=None
    for a in range(3):
        for b in range(3):
            t=3*a+b
            lhs=p3[i,side*a:side*a+n,b*c:(b+1)*c]
            tt=8-t if back else t
            w=w_ref[:,tt*c:(tt+1)*c]
            d=mm(lhs,w,((1,),(1,)) if back else ((1,),(0,)))
            acc=d if acc is None else acc+d
    return acc

def fold8(v):
    n,c=v.shape
    return jnp.sum(v.reshape(n//8,8,c),axis=0)

def send_sums(out_ref, s0, s1, extra=None):
    n=out_ref.shape[0]
    rows=jnp.concatenate([jnp.sum(s0,axis=0,keepdims=True),jnp.sum(s1,axis=0,keepdims=True)],axis=0)
    tail=jnp.zeros((2,MSG-rows.shape[1]),F32) if extra is None else extra
    msg=jnp.concatenate([rows,tail],axis=1)
    out_ref[...]=jnp.broadcast_to(msg[None],out_ref.shape)

def fwd_kernel(x_ref,parts_ref,norm_ref,w_ref,*rest,pixels,side,residual):
    if residual: stem_ref,y_ref,msg_ref,h_ref,p3=rest
    else: y_ref,msg_ref,h_ref,p3=rest
    images,n,_=p3.shape
    n-=2*side
    c=x_ref.shape[1]
    sums=jnp.sum(parts_ref[...],axis=0)[:,:c]
    _,_,scale,offset=fold_norm(sums,norm_ref[0:1],norm_ref[1:2],pixels)
    clear_borders(p3,side)
    def prep(i):
        v=x_ref[i*n:(i+1)*n,:]*scale+offset
        h,_=gelu_parts(v)
        put_taps(p3,i,h,side)
        h_ref[i*n:(i+1)*n,:]=h.astype(BF)
    s0=jnp.zeros((8,c),F32); s1=jnp.zeros((8,c),F32)
    prep(0)
    for i in range(images):
        if i+1<images: prep(i+1)
        y=tap_dots(p3,w_ref,i,n,side,c,False)
        if residual: y=y+stem_ref[i*n:(i+1)*n,:]
        y_ref[i*n:(i+1)*n,:]=y
        s0=s0+fold8(y); s1=s1+fold8(y*y)
    send_sums(msg_ref,s0,s1)

def layer_spec(w,layer):
    c=w.shape[0]
    return pl.BlockSpec((c,9*c),lambda i: (0,layer))

VMEM_SPEC=pl.BlockSpec(memory_space=pltpu.VMEM)

def forward(x,parts,norm,w,layer,stem,pixels,side):
    rows,c=x.shape
    n=side*side
    images=rows//n
    dev=parts.shape[0]
    args=(x,parts,norm,w)+((stem,) if stem is not None else ())
    return pl.pallas_call(functools.partial(fwd_kernel,pixels=pixels,side=side,residual=stem is not None),
        out_shape=(jax.ShapeDtypeStruct((rows,c),F32),jax.ShapeDtypeStruct((dev,2,MSG),F32),jax.ShapeDtypeStruct((rows,c),BF)),
        grid=(1,),in_specs=[VMEM_SPEC]*3+[layer_spec(w,layer)]+[VMEM_SPEC]*(len(args)-4),
        scratch_shapes=[pltpu.VMEM((images,n+2*side,3*c),BF)],
        compiler_params=PARAMS,cost_estimate=takes(7.5),name="conv_forward")(*args)

def stem_kernel(x_ref,w_ref,wt_ref,y_ref,msg_ref,pt_ref,gram_ref,pt,*,side,images):
    n=side*side
    c=w_ref.shape[1]
    x=x_ref[...]
    lane=lax.broadcasted_iota(jnp.int32,x.shape,1)
    row,col=lane//side,lane%side
    pt[...]=jnp.zeros(pt.shape,F32)
    for a in range(3):
        for b in range(3):
            off=(a-1)*side+(b-1)
            v=pltpu.roll(x,(-off)%n,1) if off else x
            ok=None
            if a==0: ok=row>0
            if a==2: ok=row<side-1
            if b==0: ok=(col>0) if ok is None else ok&(col>0)
            if b==2: ok=(col<side-1) if ok is None else ok&(col<side-1)
            if ok is not None: v=jnp.where(ok,v,0.0)
            t=3*a+b
            for i in range(images):
                pt[i,3*t:3*t+3,:]=v[3*i:3*i+3,:]
    w=jnp.concatenate([w_ref[...],jnp.zeros((pt.shape[1]-w_ref.shape[0],c),F32)],axis=0).astype(BF)
    s0=jnp.zeros((8,c),F32); s1=jnp.zeros((8,c),F32)
    sub=lax.broadcasted_iota(jnp.int32,(pt.shape[1],n),0)
    for i in range(images):
        p=pt[i]
        y=mm(p.astype(BF),w,((0,),(0,)))
        y_ref[i*n:(i+1)*n,:]=y
        pt_ref[:,i*n:(i+1)*n]=jnp.where(sub==w_ref.shape[0],1.0,p).astype(BF)
        s0=s0+fold8(y); s1=s1+fold8(y*y)
    send_sums(msg_ref,s0,s1,jnp.broadcast_to(jnp.sum(wt_ref[...]),(2,MSG-c)))
    taps=pt_ref[...]
    gram_ref[...]=mm(taps,taps,((1,),(1,)))

def stem(x,w,weights,devices,side):
    images=x.shape[0]//3
    n=side*side
    rows,c=images*n,w.shape[1]
    taps=(w.shape[0]+1+15)//16*16
    return pl.pallas_call(functools.partial(stem_kernel,side=side,images=images),
        out_shape=(jax.ShapeDtypeStruct((rows,c),F32),jax.ShapeDtypeStruct((devices,2,MSG),F32),jax.ShapeDtypeStruct((taps,rows),BF),jax.ShapeDtypeStruct((taps,taps),F32)),
        scratch_shapes=[pltpu.VMEM((images,taps,n),F32)],
        compiler_params=PARAMS,cost_estimate=takes(1.5),name="stem_forward")(x,w,weights)

def head_kernel(x_ref,parts_ref,norm_ref,ht_ref,bias_ref,tg_ref,wt_ref,wsum_ref,slope_ref,g_ref,msg_ref,hg_ref,loss_ref,pool,sl0,sl1,*,pixels,side):
    n=side*side
    rows,c=x_ref.shape
    images=rows//n
    sums=jnp.sum(parts_ref[...],axis=0)[:,:c]
    mean,inv,scale,offset=fold_norm(sums,norm_ref[0:1],norm_ref[1:2],pixels)
    for i in range(images):
        v=x_ref[i*n:(i+1)*n,:]
        f,gp=gelu_parts(v*scale+offset,True,True)
        slope_ref[i*n:(i+1)*n,:]=gp
        pool[i:i+1,:]=jnp.sum(fold8(f),axis=0,keepdims=True)*(1.0/n)
        sl0[i:i+1,:]=jnp.sum(fold8(gp),axis=0,keepdims=True)
        sl1[i:i+1,:]=jnp.sum(fold8(gp*((v-mean)*inv)),axis=0,keepdims=True)
    pooled=pool[0:images,:]
    low=pooled.astype(BF)
    head=ht_ref[:,0:c].astype(BF)
    logits=mm(low,head,((1,),(1,)))+bias_ref[...]
    spread=jnp.sum(pooled*pooled,axis=1,keepdims=True)/c
    k=math.pi/8.0
    shrink=lax.rsqrt(1.0+k*spread)
    scaled=logits*shrink
    top=jnp.max(scaled,axis=1,keepdims=True)
    ex=jnp.exp(scaled-top)
    tot=jnp.sum(ex,axis=1,keepdims=True)
    logtot=top+jnp.log(tot)
    wt=wt_ref[...]
    tg=tg_ref[...]
    loss_ref[...]=jnp.broadcast_to(jnp.sum(wt*(logtot-jnp.sum(scaled*tg,axis=1,keepdims=True))),loss_ref.shape)
    gs=(jnp.exp(scaled-logtot)-tg)*(wt/wsum_ref[0:1,0:1])
    gl=(gs*shrink).astype(BF)
    gsh=jnp.sum(gs*logits,axis=1,keepdims=True)
    gspread=gsh*(-0.5*k)*shrink*shrink*shrink
    gp=mm(gl,head)+gspread*(2.0/c)*pooled
    g=gp*(1.0/n)
    g_ref[0:images,:]=g
    s0=g*sl0[0:images,:]; s1=g*sl1[0:images,:]
    send_sums(msg_ref,s0,s1)
    hg_ref[:,0:c]=mm(gl,low,((0,),(0,)))
    ones=jnp.ones((images,128),BF)
    hg_ref[:,c:]=mm(gl,ones,((0,),(0,)))

def head(x,parts,norm,head_t,bias,targets,weights,wsum,pixels,side):
    rows,c=x.shape
    images=rows//(side*side)
    dev=parts.shape[0]
    cls=bias.shape[1]
    pad=(images+7)//8*8
    return pl.pallas_call(functools.partial(head_kernel,pixels=pixels,side=side),
        out_shape=(jax.ShapeDtypeStruct((rows,c),F32),jax.ShapeDtypeStruct((pad,c),F32),jax.ShapeDtypeStruct((dev,2,MSG),F32),jax.ShapeDtypeStruct((cls,c+128),F32),jax.ShapeDtypeStruct((1,128),F32)),
        scratch_shapes=[pltpu.VMEM((pad,c),F32)]*3,
        compiler_params=PARAMS,cost_estimate=takes(5.1),name="head_loss")(x,parts,norm,head_t,bias,targets,weights,wsum)

def read_sums(ref,c):
    return jnp.sum(ref[...],axis=0)[:,:c]

def back_two_kernel(res_ref,slope_ref,g_ref,ps_ref,pg_ref,na_ref,one_ref,p1_ref,nb_ref,w_ref,dres_ref,du_ref,msg_ref,p3,*,pixels,side):
    n=side*side
    rows,c=res_ref.shape
    images=rows//n
    mean2,inv2,scale2,_=fold_norm(read_sums(ps_ref,c),na_ref[0:1],na_ref[1:2],pixels)
    gs=read_sums(pg_ref,c)
    k0=scale2*gs[0:1]*(1.0/pixels); k1=scale2*inv2*gs[1:2]*(1.0/pixels)
    base=k1*mean2-k0
    mean1,inv1,scale1,offset1=fold_norm(read_sums(p1_ref,c),nb_ref[0:1],nb_ref[1:2],pixels)
    clear_borders(p3,side)
    def prep(i):
        sl=slice(i*n,(i+1)*n)
        d=slope_ref[sl,:]*(scale2*g_ref[i:i+1,:])-res_ref[sl,:]*k1+base
        dres_ref[sl,:]=d
        put_taps(p3,i,d,side)
    s0=jnp.zeros((8,c),F32); s1=jnp.zeros((8,c),F32)
    prep(0)
    for i in range(images):
        if i+1<images: prep(i+1)
        sl=slice(i*n,(i+1)*n)
        gh=tap_dots(p3,w_ref,i,n,side,c,True)
        v=one_ref[sl,:]
        _,gp=gelu_parts(v*scale1+offset1,False,True)
        du=gp*gh
        du_ref[sl,:]=du
        s0=s0+fold8(du); s1=s1+fold8(du*((v-mean1)*inv1))
    send_sums(msg_ref,s0,s1)

def back_two(res,slope,g,parts_stat,parts_grad,norm_a,conv_one,parts_one,norm_b,w,pixels,side):
    rows,c=res.shape
    n=side*side
    images=rows//n
    dev=parts_stat.shape[0]
    return pl.pallas_call(functools.partial(back_two_kernel,pixels=pixels,side=side),
        out_shape=(jax.ShapeDtypeStruct((rows,c),F32),jax.ShapeDtypeStruct((rows,c),F32),jax.ShapeDtypeStruct((dev,2,MSG),F32),jax.ShapeDtypeStruct((images,n+2*side,3*c),BF)),
        grid=(1,),in_specs=[VMEM_SPEC]*9+[layer_spec(w,1)],
        compiler_params=PARAMS,cost_estimate=takes(10.6),name="back_two")(res,slope,g,parts_stat,parts_grad,norm_a,conv_one,parts_one,norm_b,w)

def turn_kernel(h_ref,qt_ref,qm_ref,hq_ref,a_ref,*,scale):
    c=h_ref.shape[1]
    h=h_ref[...]
    q=qt_ref[...]
    qh=q.astype(BF); ql=(q-qh.astype(F32)).astype(BF)
    hq_ref[0:c,:]=(mm(qh,h,((1,),(1,)))+mm(ql,h,((1,),(1,)))-qm_ref[:,0:1]).astype(BF)
    extra=hq_ref.shape[0]-c
    sub=lax.broadcasted_iota(jnp.int32,(extra,h.shape[0]),0)
    hq_ref[c:,:]=jnp.where(sub==0,1.0,0.0).astype(BF)
    a_ref[...]=mm(h,h,((0,),(0,)))*scale

def turn(h,qt,qmu,scale):
    rows,c=h.shape
    return pl.pallas_call(functools.partial(turn_kernel,scale=scale),
        out_shape=(jax.ShapeDtypeStruct((c+16,rows),BF),jax.ShapeDtypeStruct((c,c),F32)),
        compiler_params=PARAMS,cost_estimate=takes(1.3),name="turn_hidden")(h,qt,qmu)

def weight_dots(p3,hq_ref,gw_ref,ones_ref,gf_ref,side,scale):
    images,rows,w=p3.shape
    n=rows-2*side
    c=w//3
    hq=hq_ref[...]
    for a in range(3):
        for b in range(3):
            t=8-(3*a+b)
            rhs=p3[:,side*a:side*a+n,b*c:(b+1)*c].reshape(images*n,c)
            d=mm(hq,rhs)
            gw_ref[:,t*c:(t+1)*c]=d[0:c].astype(gw_ref.dtype)
            ones_ref[:,t*c:(t+1)*c]=d[c:c+8]
    mid=p3[:,side:side+n,c:2*c].reshape(images*n,c)
    gf_ref[...]=mm(mid,mid,((0,),(0,)))*scale

def weight_two_kernel(p3,hq_ref,gw_ref,ones_ref,gf_ref,*,side,scale):
    weight_dots(p3,hq_ref,gw_ref,ones_ref,gf_ref,side,scale)

def weight_shapes(c,dt):
    return (jax.ShapeDtypeStruct((c,9*c),dt),jax.ShapeDtypeStruct((8,9*c),F32),jax.ShapeDtypeStruct((c,c),F32))

def weight_two(p3,hq,side,scale,dt=BF):
    c=p3.shape[2]//3
    return pl.pallas_call(functools.partial(weight_two_kernel,side=side,scale=scale),
        out_shape=weight_shapes(c,dt),compiler_params=PARAMS,cost_estimate=takes(6.0),name="weight_two")(p3,hq)

def weight_one_kernel(one_ref,du_ref,p1_ref,pg_ref,nb_ref,hq_ref,p3,gw_ref,ones_ref,gf_ref,*,pixels,side,scale):
    n=side*side
    rows,c=one_ref.shape
    images=rows//n
    mean1,inv1,scale1,_=fold_norm(read_sums(p1_ref,c),nb_ref[0:1],nb_ref[1:2],pixels)
    gs=read_sums(pg_ref,c)
    k0=scale1*gs[0:1]*(1.0/pixels); k1=scale1*inv1*gs[1:2]*(1.0/pixels)
    base=k1*mean1-k0
    clear_borders(p3,side)
    for i in range(images):
        sl=slice(i*n,(i+1)*n)
        put_taps(p3,i,du_ref[sl,:]*scale1-one_ref[sl,:]*k1+base,side)
    weight_dots(p3,hq_ref,gw_ref,ones_ref,gf_ref,side,scale)

def weight_one(conv_one,du,parts_one,parts_grad,norm_b,hq,pixels,side,scale,dt=BF):
    rows,c=conv_one.shape
    n=side*side
    images=rows//n
    return pl.pallas_call(functools.partial(weight_one_kernel,pixels=pixels,side=side,scale=scale),
        out_shape=(jax.ShapeDtypeStruct((images,n+2*side,3*c),BF),)+weight_shapes(c,dt),
        compiler_params=PARAMS,cost_estimate=takes(6.4),name="weight_one")(conv_one,du,parts_one,parts_grad,norm_b,hq)

def back_one_kernel(p3,w_ref,stem_ref,p0_ref,n0_ref,dres_ref,pt_ref,ps_ref,*,pixels,side):
    images,rows,w3=p3.shape
    n=rows-2*side
    c=w3//3
    mean0,inv0,scale0,offset0=fold_norm(read_sums(p0_ref,c),n0_ref[0:1],n0_ref[1:2],pixels)
    taps=pt_ref.shape[0]
    s0=jnp.zeros((8,c),F32); s1=jnp.zeros((8,c),F32)
    acc=jnp.zeros((taps,c),F32)
    for i in range(images):
        sl=slice(i*n,(i+1)*n)
        gh=tap_dots(p3,w_ref,i,n,side,c,True)
        v=stem_ref[sl,:]
        _,gp=gelu_parts(v*scale0+offset0,False,True)
        du=gp*gh
        s0=s0+fold8(du); s1=s1+fold8(du*((v-mean0)*inv0))
        z=du*scale0+dres_ref[sl,:]
        zh=z.astype(BF); zl=(z-zh.astype(F32)).astype(BF)
        p=pt_ref[:,sl]
        acc=acc+mm(p,zh)+mm(p,zl)
    ps_ref[0:taps,:]=acc
    ps_ref[taps:taps+1,:]=jnp.sum(s0,axis=0,keepdims=True)
    ps_ref[taps+1:taps+2,:]=jnp.sum(s1,axis=0,keepdims=True)
    ps_ref[taps+2:,:]=jnp.zeros((ps_ref.shape[0]-taps-2,c),F32)

def back_one(p3,w,stem_out,parts0,norm0,dres,pt,pixels,side):
    c=p3.shape[2]//3
    taps=pt.shape[0]
    return pl.pallas_call(functools.partial(back_one_kernel,pixels=pixels,side=side),
        out_shape=jax.ShapeDtypeStruct((taps+8,c),F32),
        grid=(1,),in_specs=[VMEM_SPEC]+[layer_spec(w,0)]+[VMEM_SPEC]*5,
        compiler_params=PARAMS,cost_estimate=takes(8.8),name="back_one")(p3,w,stem_out,parts0,norm0,dres,pt)


DIAG,HEAD,SIDE,BORDER,SMALL=0,8,32,64,96

def pack_kernel(a1_ref,g1_ref,a2_ref,g2_ref,hg_ref,loss_ref,gram_ref,b1_ref,b2_ref,out_ref,small):
    devices,rows,c=out_ref.shape
    own=c//devices
    r=lax.broadcasted_iota(jnp.int32,(c,c),0); l=lax.broadcasted_iota(jnp.int32,(c,c),1)
    small[...]=jnp.zeros(small.shape,F32)
    for k,(a_ref,g_ref) in enumerate(((a1_ref,g1_ref),(a2_ref,g2_ref))):
        g=g_ref[...]
        both=jnp.where(r<=l,a_ref[...],g)
        small[DIAG+k:DIAG+k+1,:]=jnp.sum(jnp.where(r==l,g,0.0),axis=0,keepdims=True)
        for j in range(devices): out_ref[j,k*own:(k+1)*own,:]=both[j*own:(j+1)*own]
    cls=hg_ref.shape[0]
    small[HEAD:HEAD+cls,:]=hg_ref[:,0:c]
    small[SIDE:SIDE+gram_ref.shape[0],0:gram_ref.shape[1]]=gram_ref[...]
    small[SIDE:SIDE+cls,128:256]=hg_ref[:,c:c+128]
    small[SIDE+16:SIDE+17,128:256]=loss_ref[...]
    for k,b_ref in enumerate((b1_ref,b2_ref)):
        for t in range(9): small[BORDER+9*k+t:BORDER+9*k+t+1,:]=b_ref[0:1,t*c:(t+1)*c]
    each=rows-2*own
    for j in range(devices):
        if (j+1)*each<=small.shape[0]: out_ref[j,2*own:,:]=small[j*each:(j+1)*each,:]
        else: out_ref[j,2*own:,:]=jnp.zeros((each,c),F32)

def pack(a1,g1,a2,g2,hg,loss,gram,b1,b2,devices):
    c=a1.shape[0]
    rows=2*(c//devices)+-(-SMALL//devices)
    return pl.pallas_call(pack_kernel,out_shape=jax.ShapeDtypeStruct((devices,rows,c),F32),
        scratch_shapes=[pltpu.VMEM((SMALL,c),F32)],
        compiler_params=PARAMS,cost_estimate=takes(1.5),name="pack_sums")(a1,g1,a2,g2,hg,loss,gram,b1,b2)

def add_kernel(got_ref,out_ref):
    t=got_ref[0]
    for j in range(1,got_ref.shape[0]): t=t+got_ref[j]
    for j in range(got_ref.shape[0]): out_ref[j]=t

def add_pieces(got):
    return pl.pallas_call(add_kernel,out_shape=jax.ShapeDtypeStruct(got.shape,F32),compiler_params=PARAMS,cost_estimate=takes(1.0),name="add_pieces")(got)

def unpack_small(all_ref,small,own):
    devices,rows,c=all_ref.shape
    each=rows-2*own
    for j in range(min(devices,SMALL//each)): small[j*each:(j+1)*each,:]=all_ref[j,2*own:,:]

def adam_refs(p_ref,m_ref,v_ref,g,out,rate,decay,consts):
    beta1,beta2,fix1,fix2,eps=consts
    m=beta1*m_ref[...]+(1.0-beta1)*g
    v=beta2*v_ref[...]+(1.0-beta2)*g*g
    p=p_ref[...]
    out[0][...]=p-rate*((m/fix1)/(jnp.sqrt(v/fix2)+eps)+decay*p)
    out[1][...]=m
    out[2][...]=v

def small_kernel(all_ref,st_ref,p0_ref,p3_ref,p4_ref,sw,sm,sv,hw,hm,hv,nw,nm,nv,loss_ref,so,smo,svo,ho,hmo,hvo,no,nmo,nvo,small,*,own,pixels,consts,rates):
    unpack_small(all_ref,small,own)
    c=sw.shape[1]
    rows=sw.shape[0]
    taps=(rows+1+15)//16*16
    st=st_ref[...]
    s00=st[taps:taps+1]; s01=st[taps+1:taps+2]
    mean0,inv0,scale0,_=fold_norm(read_sums(p0_ref,c),nw[0:1],nw[1:2],pixels)
    gram=small[SIDE:SIDE+taps,0:128]
    ones0=gram[0:rows,rows:rows+1]
    w=sw[...].astype(BF).astype(F32)
    w=jnp.concatenate([w,jnp.zeros((128-rows,c),F32)],axis=0)
    cross=lax.dot_general(gram[0:rows],w,(((1,),(0,)),((),())),precision=highest,preferred_element_type=F32)
    xs=inv0*(cross-ones0*mean0)
    grad=st[0:rows]-ones0*(scale0*s00/pixels)-xs*(scale0*s01/pixels)
    adam_refs(sw,sm,sv,grad,(so,smo,svo),rates[0],rates[1],consts)
    cls=hw.shape[0]
    hg=jnp.concatenate([small[HEAD:HEAD+cls,:],small[SIDE:SIDE+cls,128:129]],axis=1)
    adam_refs(hw,hm,hv,hg,(ho,hmo,hvo),rates[2],rates[3],consts)
    s3=read_sums(p3_ref,c); s4=read_sums(p4_ref,c)
    ng=jnp.concatenate([s01,s00,s4[1:2],s4[0:1],s3[1:2],s3[0:1]],axis=0)
    adam_refs(nw,nm,nv,ng,(no,nmo,nvo),rates[4],0.0,consts)
    wsum=jnp.sum(p0_ref[...],axis=0)[0:1,c:c+128]
    lane=lax.broadcasted_iota(jnp.int32,(1,128),1)
    loss_ref[...]=jnp.where(lane==0,small[SIDE+16:SIDE+17,128:256],wsum)

def small_updates(everything,stem_total,parts0,parts3,parts4,stem3,head3,norm3,pixels,consts,rates):
    c=stem3[0].shape[1]
    own=c//everything.shape[0]
    shapes=[jax.ShapeDtypeStruct((1,128),F32)]+[jax.ShapeDtypeStruct(x.shape,F32) for x in stem3+head3+norm3]
    return pl.pallas_call(functools.partial(small_kernel,own=own,pixels=pixels,consts=consts,rates=rates),out_shape=shapes,
        scratch_shapes=[pltpu.VMEM((SMALL,c),F32)],
        compiler_params=PARAMS,cost_estimate=takes(1.5),name="small_updates")(everything,stem_total,parts0,parts3,parts4,*stem3,*head3,*norm3)

def turn_rows(x, c, blocks):
    return jnp.concatenate([x[:,t*c:(t+1)*c] for t in range(blocks)],axis=0)

def to_halves(ref, halves):
    r=ref.shape[0]
    halves[0:r,:]=ref[:,0:128]
    halves[r:2*r,:]=ref[:,128:256]

def from_halves(halves, ref):
    r=ref.shape[0]
    ref[:,0:128]=halves[0:r,:].astype(ref.dtype)
    ref[:,128:256]=halves[r:2*r,:].astype(ref.dtype)

def pick_rows(halves, layer, own, blocks):
    r=halves.shape[0]//2
    sides=[jnp.concatenate([halves[pl.ds(h*r+layer*blocks+t,own,stride=2*blocks),:] for t in range(blocks)],axis=0) for h in range(2)]
    return jnp.concatenate(sides,axis=1)

def place_rows(halves, layer, own, blocks, v):
    r=halves.shape[0]//2
    for h in range(2):
        for t in range(blocks): halves[pl.ds(h*r+layer*blocks+t,own,stride=2*blocks),:]=v[t*own:(t+1)*own,h*128:(h+1)*128]

def move_kernel(g_ref,all_ref,qmu_ref,q_ref,m_ref,v_ref,mo_ref,vo_ref,send_ref,m_sc,v_sc,small,*,consts):
    beta1,beta2,fix1,fix2,eps=consts
    own,w=g_ref.shape
    w=w//2
    unpack_small(all_ref,small,own)
    to_halves(m_ref,m_sc)
    to_halves(v_ref,v_sc)
    c=q_ref.shape[1]
    blocks=w//c
    for l in range(2):
        b=jnp.concatenate([jnp.broadcast_to(small[BORDER+l*blocks+t:BORDER+l*blocks+t+1,:],(own,c)) for t in range(blocks)],axis=0)
        qm=jnp.concatenate([qmu_ref[l]]*blocks,axis=0)
        x=turn_rows(g_ref[:,l*w:(l+1)*w],c,blocks)+qm[:,0:1]*b
        rot=dot3(x,q_ref[2*l+1])
        m=beta1*pick_rows(m_sc,l,own,blocks)+(1.0-beta1)*rot
        v=beta2*pick_rows(v_sc,l,own,blocks)+(1.0-beta2)*rot*rot
        place_rows(m_sc,l,own,blocks,m)
        place_rows(v_sc,l,own,blocks,v)
        step=(m/fix1)/(jnp.sqrt(v/fix2)+eps)
        back=dot3(step,q_ref[2*l+1],((1,),(1,)))
        for t in range(blocks): send_ref[:,l*w+t*c:l*w+(t+1)*c]=back[t*own:(t+1)*own,:].astype(BF)
    from_halves(m_sc,mo_ref)
    from_halves(v_sc,vo_ref)

def move(g,everything,qmu,bases,m,v,consts):
    own,w=g.shape
    return pl.pallas_call(functools.partial(move_kernel,consts=consts),
        out_shape=(jax.ShapeDtypeStruct(m.shape,F32),jax.ShapeDtypeStruct(m.shape,F32),jax.ShapeDtypeStruct((own,w),BF)),
        scratch_shapes=[pltpu.VMEM((2*m.shape[0],128),F32)]*2+[pltpu.VMEM((SMALL,m.shape[1]),F32)],
        compiler_params=PARAMS,cost_estimate=takes(2.0),name="moments_and_direction")(g,everything,qmu,bases,m,v)

def finish_kernel(full_ref,rows_ref,w_ref,out_ref,low_ref,w_sc,*,rate,decay):
    to_halves(w_ref,w_sc)
    c=full_ref.shape[0]
    half=full_ref.shape[1]//2
    own=w_ref.shape[0]*c//half//2
    blocks=half//c
    for l in range(2):
        q=rows_ref[l]
        qh=q.astype(BF); ql=(q-qh.astype(F32)).astype(BF)
        both=jnp.concatenate([qh,ql],axis=0)
        d=mm(both,full_ref[:,l*half:(l+1)*half])
        d=d[0:own]+d[own:2*own]
        w=pick_rows(w_sc,l,own,blocks)
        place_rows(w_sc,l,own,blocks,w-rate*(turn_rows(d,c,blocks)+decay*w))
    from_halves(w_sc,out_ref)
    from_halves(w_sc,low_ref)

def finish(full,rows,w,rate,decay):
    return pl.pallas_call(functools.partial(finish_kernel,rate=rate,decay=decay),
        out_shape=(jax.ShapeDtypeStruct(w.shape,F32),jax.ShapeDtypeStruct(w.shape,BF)),
        scratch_shapes=[pltpu.VMEM((2*w.shape[0],128),F32)],
        compiler_params=PARAMS,cost_estimate=takes(2.5),name="new_weights")(full,rows,w)

CLASSES=10
STEP=5
BETA_ONE=0.9
BETA_TWO=0.99
ADAM_EPS=1e-08
WEIGHT_DECAY=0.01
RATE_CONV=0.02
RATE_STEM=0.1
RATE_HEAD=0.1
RATE_NORM=0.5


def bit_groups(devices):
    total_bits=devices.bit_length()-1
    groups=[(0,1)]
    while groups[-1][0]+groups[-1][1]<total_bits:
        first=groups[-1][0]+groups[-1][1]
        groups.append((first,min(2,total_bits-first)))
    return groups

def swap(values, mask, devices):
    return lax.ppermute(values,"dp",[(i,i^mask) for i in range(devices)])

def exchange(pieces):
    return lax.all_to_all(pieces,"dp",0,0,tiled=True)

def gather_all(piece, first_wait=(), last_wait=(), between=None):
    devices=lax.axis_size("dp")
    me=lax.axis_index("dp")
    groups=bit_groups(devices)[::-1]
    held=piece[(None,)*len(groups)]
    for axis,(first,width) in enumerate(groups):
        radix=1<<width
        mine=(me>>first)&(radix-1)
        got=[held]+[swap(held,k<<first,devices) for k in range(1,radix)]
        ordered=[]
        for j in range(radix):
            value=got[j]
            for m in range(1,radix): value=jnp.where(mine==m,got[j^m],value)
            ordered.append(value)
        held=jnp.concatenate(ordered,axis=axis)
        if axis==0:
            held=after(held,*first_wait)
            early=held
            if between is not None: last_wait=(between(held),)
        if axis==len(groups)-2 and last_wait: held=after(held,*last_wait)
    return held.reshape((devices,)+piece.shape),last_wait

def scatter_rounds(pieces, devices):
    groups=bit_groups(devices)
    me=lax.axis_index("dp")
    held=pieces.reshape(tuple(1<<width for _,width in groups[::-1])+pieces.shape[1:])
    def step(held, order):
        first,width=groups[order]
        axis=len(groups)-1-order
        radix=1<<width
        mine=(me>>first)&(radix-1)
        parts=[lax.dynamic_slice_in_dim(held,mine^k,1,axis=axis) for k in range(radix)]
        total=parts[0].astype(F32)
        for k in range(1,radix):
            total=total+swap(parts[k].astype(BF),k<<first,devices).astype(F32)
        return total
    return held,step,len(groups)

def rows_to_sum(rows):
    devices=lax.axis_size("dp")
    count,c=rows.shape
    each=-(-count//devices)
    return jnp.pad(rows,((0,each*devices-count),(0,0))).reshape(devices,each,c)

def after(value, *earlier):
    return lax.optimization_barrier((value,)+earlier)[0]

def expected_gelu(gain, shift):
    spread=jnp.sqrt(1.0+gain*gain)
    at=shift/spread
    return shift*(0.5+0.5*lax.erf(at*math.sqrt(0.5)))+gain*gain/spread*jnp.exp(-0.5*at*at)*(1.0/math.sqrt(2.0*math.pi))

def local(images, labels, groups, conv_w, conv_m, conv_v, rot_bases, stem_w, stem_m, stem_v, head_w, head_m, head_v, norm_p, norm_m, norm_v):
    devices=lax.axis_size("dp")
    me=lax.axis_index("dp")
    count,side=images.shape[0],images.shape[1]
    c=conv_w.shape[1]
    pixels=count*side*side*devices
    own=c//devices
    packed=conv_w.reshape(own,18*c).astype(BF)
    weights=1.0+3.0*groups.astype(F32)
    x=images.transpose(0,3,1,2).reshape(3*count,side*side).astype(F32)
    stem_out,msg0,pt,gram=stem(x,stem_w,weights[None,:],devices,side)
    parts0=exchange(msg0)
    w_all=gather_all(packed,(msg0,),(parts0,))[0].reshape(c,18*c)
    left_t=rot_bases[0::2].transpose(0,2,1)
    mu=[expected_gelu(norm_p[2*l],norm_p[2*l+1]) for l in range(2)]
    qmu=[jnp.dot(left_t[l],mu[l][:,None],precision=highest) for l in range(2)]
    targets=(labels[:,None]==jnp.arange(CLASSES,dtype=jnp.int32)[None,:]).astype(F32)
    conv_one,msg1,hid1=forward(stem_out,parts0,norm_p[0:2],w_all,0,None,pixels,side)
    parts1=exchange(msg1)
    hq1,a_one=turn(hid1,left_t[0],qmu[0],1.0/pixels)
    residual,msg2,hid2=forward(conv_one,after(parts1,a_one),norm_p[2:4],w_all,1,stem_out,pixels,side)
    parts2=exchange(msg2)
    hq2,a_two=turn(hid2,left_t[1],qmu[1],1.0/pixels)
    wsum=jnp.sum(parts0[:,0:1,c:c+1],axis=0)
    slope,g,msg3,head_g,loss=head(residual,after(parts2,a_two),norm_p[4:6],head_w.T,head_w[c:c+1],targets,weights[:,None],wsum,pixels,side)
    parts3=exchange(msg3)
    dres,du1,msg4,p3two=back_two(residual,slope,g,parts2,parts3,norm_p[4:6],conv_one,parts1,norm_p[2:4],w_all,pixels,side)
    parts4=exchange(msg4)
    gw_two,ones_two,g_two=weight_two(p3two,hq2,side,float(pixels))
    two,step,rounds=scatter_rounds(gw_two.reshape(devices,own,9*c),devices)
    two=step(two,0)
    p3one,gw_one,ones_one,g_one=weight_one(conv_one,du1,parts1,after(parts4,ones_two),norm_p[2:4],hq1,pixels,side,float(pixels))
    packed_sums=pack(a_one,g_one,a_two,g_two,head_g,loss,gram,ones_one,ones_two,devices)
    got_sums=exchange(packed_sums)
    one,step,_=scatter_rounds(gw_one.reshape(devices,own,9*c),devices)
    both=step(jnp.concatenate([step(after(one,packed_sums),0),two],axis=-1),1)
    stem_sums=back_one(after(p3one,packed_sums),w_all,stem_out,parts0,norm_p[0:2],dres,pt,pixels,side)
    added=add_pieces(after(got_sums,stem_sums))
    everything=exchange(added)
    both=after(both,added)
    for order in range(2,rounds): both=step(both,order)
    both=both.reshape(own,18*c)
    inverse,factors,damped=inverses(jnp.reshape(me,(1,)).astype(jnp.int32),everything,4)
    stem_parts=exchange(rows_to_sum(after(stem_sums,everything)))
    stem_own=jnp.sum(stem_parts,axis=0)
    stem_all=exchange(jnp.broadcast_to(stem_own[None],stem_parts.shape))
    stem_total=stem_all.reshape(-1,c)
    consts=(BETA_ONE,BETA_TWO,1.0-BETA_ONE**STEP,1.0-BETA_TWO**STEP,ADAM_EPS)
    q_own=jnp.stack([lax.dynamic_slice_in_dim(qmu[l],me*own,own,0) for l in range(2)])
    m_new,v_new,half=move(after(both,inverse,stem_own),everything,q_own,rot_bases,conv_m,conv_v,consts)
    full,waited=gather_all(half,(stem_all,),(),lambda held: new_bases(after(damped,held),rot_bases))
    bases_new=waited[0]
    full=full.reshape(c,18*c)
    rows=lax.dynamic_slice_in_dim(rot_bases,me*own,own,1)[0::2]
    conv_new,conv_low=finish(full,rows,conv_w,RATE_CONV,WEIGHT_DECAY)
    small=small_updates(everything,stem_total,parts0,parts3,parts4,(stem_w,stem_m,stem_v),(head_w.T,head_m.T,head_v.T),(norm_p,norm_m,norm_v),pixels,consts,(RATE_STEM,WEIGHT_DECAY,RATE_HEAD,WEIGHT_DECAY,RATE_NORM))
    return (small[0][0,0:2],factors,inverse,conv_new,m_new,v_new,bases_new,small[1],small[2],small[3],small[4].T,small[5].T,small[6].T,small[7],small[8],small[9],conv_low)

def solution(mesh):
    one=P("dp",None)
    return jax.shard_map(local,mesh=mesh,in_specs=(P("dp",None,None,None),P("dp"),P("dp"),one,one,one)+(P(),)*10,out_specs=(P(),one,one,one,one,one)+(P(),)*10+(one,),check_vma=False)
```

```python
import functools
import math

import jax
import jax.numpy as jnp
from jax import lax
from jax.experimental import pallas as pl
from jax.experimental.pallas import tpu as pltpu
from jax.sharding import PartitionSpec as P

NS_ITERS=6; DAMPING=0.1
highest=HI=lax.Precision.HIGHEST
def dotp(a,b,dims=((1,),(0,)),prec=HI):
    return lax.dot_general(a,b,(dims,((),())),precision=prec,preferred_element_type=jnp.float32)
def split(a):
    hi=a.astype(jnp.bfloat16)
    return hi,(a-hi.astype(jnp.float32)).astype(jnp.bfloat16)
def dot3(a,b,dims=((1,),(0,))):
    ah,al=split(a); bh,bl=split(b)
    d=lambda x,y: lax.dot_general(x,y,(dims,((),())),preferred_element_type=jnp.float32)
    return d(ah,bh)+(d(ah,bl)+d(al,bh))
def inverse_kernel(me_ref,all_ref,inv_ref,fac_ref,m_ref,p_ref,x_ref):
    devices,_,n=all_ref.shape
    own=n//devices
    M4=4
    me=me_ref[0]
    r=lax.broadcasted_iota(jnp.int32,(n,n),0); c=lax.broadcasted_iota(jnp.int32,(n,n),1)
    eye=(r==c).astype(jnp.float32)
    each=all_ref.shape[1]-2*own
    Fs=[]
    for k in range(2):
        for j in range(devices): p_ref[j*own:(j+1)*own,:]=all_ref[j,k*own:(k+1)*own,:]
        P=p_ref[...]
        Pt=P.T
        diag=all_ref[(DIAG+k)//each,2*own+(DIAG+k)%each:2*own+(DIAG+k)%each+1,:]
        Fs.append(jnp.where(r<=c,P,Pt))
        Fs.append(jnp.where(r==c,diag,jnp.where(r>c,P,Pt)))
    start=pl.multiple_of(me*own,own)
    def own_rows(out_ref):
        for m in range(M4):
            rows=x_ref[m,pl.ds(start,own),:]
            for i in range(own): out_ref[M4*i+m:M4*i+m+1,:]=rows[i:i+1,:]
    Ms=[]
    for m in range(M4):
        F=Fs[m]
        tr=jnp.sum(F*eye)
        M=F+(DAMPING*tr/n)*eye
        Ms.append(M)
        m_ref[m]=M
        x_ref[m]=F
    own_rows(fac_ref)
    Xs=[eye*lax.rsqrt(jnp.sum(M*M)) for M in Ms]
    for _ in range(NS_ITERS):
        products=[dot3(X,M) for X,M in zip(Xs,Ms)]
        Xs=[2.0*X-dot3(p,X) for p,X in zip(products,Xs)]
    for m in range(M4): x_ref[m]=Xs[m]
    own_rows(inv_ref)

def inverses(me,everything,m4):
    devices,_,n=everything.shape
    own=n//devices
    return pl.pallas_call(inverse_kernel,
        out_shape=(jax.ShapeDtypeStruct((m4*own,n),jnp.float32),jax.ShapeDtypeStruct((m4*own,n),jnp.float32),jax.ShapeDtypeStruct((m4,n,n),jnp.float32)),
        in_specs=[pl.BlockSpec(memory_space=pltpu.SMEM)]+[pl.BlockSpec(memory_space=pltpu.VMEM)],
        scratch_shapes=[pltpu.VMEM((n,n),jnp.float32),pltpu.VMEM((m4,n,n),jnp.float32)],
        compiler_params=pltpu.CompilerParams(vmem_limit_bytes=48*2**20),
        cost_estimate=takes(11.0),name="damped_inverses")(me,everything)

def sub(row, like):
    return jnp.broadcast_to(row,like.shape)

def bases_kernel(m_ref,q_ref,qn_ref,b_ref):
    M4,n,_=m_ref.shape
    nb=64
    for m in range(M4):
        Yt=dotp(q_ref[m],m_ref[m],((0,),(0,)))
        b_ref[m,:,n:]=Yt
        b_ref[m,:,:n]=dotp(Yt,Yt,((1,),(1,)))
    li=lax.broadcasted_iota(jnp.int32,(8,128),1); si=lax.broadcasted_iota(jnp.int32,(8,128),0)
    tiles=nb//8
    for k in range(n//nb):
        lo=k*nb; t0=(lo//128)*128; off=lo-t0
        V=[]
        for m in range(M4):
            D=b_ref[m,lo:lo+nb,t0:t0+128]
            if off: D=pltpu.roll(D,128-off,1)
            V.append([jnp.where(li<nb,D[8*i:8*i+8],jnp.where(li-nb==si+8*i,1.0,0.0)) for i in range(tiles)])
        rows=[[None]*tiles for _ in range(M4)]
        for b in range(tiles):
            pivots=[[jnp.broadcast_to(V[m][b][:,8*b+j:8*b+j+1],(8,128)) for j in range(8)] for m in range(M4)]
            below=[[[jnp.broadcast_to(V[m][i][:,8*b+j:8*b+j+1],(8,128)) for j in range(8)] for i in range(b+1,tiles)] for m in range(M4)]
            R=[V[m][b] for m in range(M4)]
            kept=[R[m] for m in range(M4)]
            size=[pivots[m][0] for m in range(M4)]
            for j in range(8):
                for m in range(M4):
                    col=pivots[m][j]
                    d=sub(col[j:j+1],col)
                    at=si==j
                    kept[m]=jnp.where(at,R[m],kept[m])
                    size[m]=jnp.where(at,d,size[m])
                    inv=1.0/d
                    rj=sub(R[m][j:j+1],R[m])*inv
                    for q in range(j+1,8):
                        pj=sub(pivots[m][q][j:j+1],col)*inv
                        pivots[m][q]=jnp.where(at,pj,pivots[m][q]-col*pj)
                    R[m]=jnp.where(at,rj,R[m]-col*rj)
            for m in range(M4):
                rows[m][b]=kept[m]*lax.rsqrt(size[m])
                spread=[sub(R[m][j:j+1],R[m]) for j in range(8)]
                for i in range(b+1,tiles):
                    cols=below[m][i-b-1]
                    terms=[cols[j]*spread[j] for j in range(8)]
                    while len(terms)>1: terms=[terms[z]+terms[z+1] for z in range(0,len(terms),2)]
                    V[m][i]=V[m][i]-terms[0]
        for m in range(M4):
            E=jnp.concatenate(rows[m],axis=0)[:,nb:2*nb]
            U=dotp(E,b_ref[m,lo:lo+nb,:])
            b_ref[m,lo:lo+nb,:]=U
            if lo+nb<n:
                b_ref[m,lo+nb:,:]=b_ref[m,lo+nb:,:]-dotp(U[:,lo+nb:n],U,((0,),(0,)))
    for m in range(M4):
        qn_ref[m]=b_ref[m,:,n:].T

def new_bases(damped,Q):
    m,n,_=Q.shape
    return pl.pallas_call(bases_kernel,
        out_shape=jax.ShapeDtypeStruct((m,n,n),jnp.float32),
        scratch_shapes=[pltpu.VMEM((m,n,2*n),jnp.float32)],
        compiler_params=pltpu.CompilerParams(vmem_limit_bytes=48*2**20),
        cost_estimate=takes(30.0),name="new_bases")(damped,Q)

EPS_NORM=1e-5
BF=jnp.bfloat16; F32=jnp.float32
MSG=384
ROOT=math.sqrt(2.0/math.pi)
def takes(micros):
    return pl.CostEstimate(flops=int(micros*1.0e9),bytes_accessed=int(micros*3.0e6),transcendentals=0)

def hold(x):
    return pltpu.with_memory_space_constraint(x,pltpu.HBM)

def far(shape,dtype):
    return pltpu.HBM(shape,dtype)

PARAMS=pltpu.CompilerParams(vmem_limit_bytes=48*2**20)

def mm(a,b,dims=((1,),(0,))):
    return lax.dot_general(a,b,(dims,((),())),preferred_element_type=F32)

def gelu_parts(x, need_value=True, need_slope=False):
    sq=x*x
    t=jnp.tanh(x*(ROOT+(ROOT*0.044715)*sq))
    half=0.5+0.5*t
    value=x*half if need_value else None
    slope=None
    if need_slope:
        slope=half+(0.5*x)*(1.0-t*t)*(ROOT+(3.0*ROOT*0.044715)*sq)
    return value,slope

def fold_norm(sums, gain, shift, pixels):
    mean=sums[0:1]/pixels
    var=sums[1:2]/pixels-mean*mean
    inv=lax.rsqrt(var+EPS_NORM)
    return mean,inv,gain*inv,shift-mean*(gain*inv)

def shift_taps(v, side):
    col=lax.broadcasted_iota(jnp.int32,v.shape,0)%side
    n=v.shape[0]
    left=jnp.where(col==0,0.0,pltpu.roll(v,1,0))
    right=jnp.where(col==side-1,0.0,pltpu.roll(v,n-1,0))
    return left,right

def clear_borders(p3, side):
    b,rows,w=p3.shape
    for i in range(b):
        p3[i,0:side,:]=jnp.zeros((side,w),BF)
        p3[i,rows-side:rows,:]=jnp.zeros((side,w),BF)

def put_taps(p3, i, v, side):
    n,c=v.shape
    left,right=shift_taps(v,side)
    p3[i,side:side+n,0:c]=left.astype(BF)
    p3[i,side:side+n,c:2*c]=v.astype(BF)
    p3[i,side:side+n,2*c:3*c]=right.astype(BF)

def tap_dots(p3, w_ref, i, n, side, c, back):
    acc=None
    for a in range(3):
        for b in range(3):
            t=3*a+b
            lhs=p3[i,side*a:side*a+n,b*c:(b+1)*c]
            tt=8-t if back else t
            w=w_ref[:,tt*c:(tt+1)*c]
            d=mm(lhs,w,((1,),(1,)) if back else ((1,),(0,)))
            acc=d if acc is None else acc+d
    return acc

def fold8(v):
    n,c=v.shape
    return jnp.sum(v.reshape(n//8,8,c),axis=0)

def send_sums(out_ref, s0, s1, extra=None):
    n=out_ref.shape[0]
    rows=jnp.concatenate([jnp.sum(s0,axis=0,keepdims=True),jnp.sum(s1,axis=0,keepdims=True)],axis=0)
    tail=jnp.zeros((2,MSG-rows.shape[1]),F32) if extra is None else extra
    msg=jnp.concatenate([rows,tail],axis=1)
    out_ref[...]=jnp.broadcast_to(msg[None],out_ref.shape)

def fwd_kernel(x_ref,parts_ref,norm_ref,w_ref,*rest,pixels,side,residual):
    if residual: stem_ref,y_ref,msg_ref,h_ref,p3=rest
    else: y_ref,msg_ref,h_ref,p3=rest
    images,n,_=p3.shape
    n-=2*side
    c=x_ref.shape[1]
    sums=jnp.sum(parts_ref[...],axis=0)[:,:c]
    _,_,scale,offset=fold_norm(sums,norm_ref[0:1],norm_ref[1:2],pixels)
    clear_borders(p3,side)
    def prep(i):
        v=x_ref[i*n:(i+1)*n,:]*scale+offset
        h,_=gelu_parts(v)
        put_taps(p3,i,h,side)
        h_ref[i*n:(i+1)*n,:]=h.astype(BF)
    s0=jnp.zeros((8,c),F32); s1=jnp.zeros((8,c),F32)
    prep(0)
    for i in range(images):
        if i+1<images: prep(i+1)
        y=tap_dots(p3,w_ref,i,n,side,c,False)
        if residual: y=y+stem_ref[i*n:(i+1)*n,:]
        y_ref[i*n:(i+1)*n,:]=y
        s0=s0+fold8(y); s1=s1+fold8(y*y)
    send_sums(msg_ref,s0,s1)

def layer_spec(w,layer):
    c=w.shape[0]
    return pl.BlockSpec((c,9*c),lambda i: (0,layer))

VMEM_SPEC=pl.BlockSpec(memory_space=pltpu.VMEM)

def forward(x,parts,norm,w,layer,stem,pixels,side):
    rows,c=x.shape
    n=side*side
    images=rows//n
    dev=parts.shape[0]
    args=(hold(x),parts,norm,w)+((hold(stem),) if stem is not None else ())
    return pl.pallas_call(functools.partial(fwd_kernel,pixels=pixels,side=side,residual=stem is not None),
        out_shape=(far((rows,c),F32),jax.ShapeDtypeStruct((dev,2,MSG),F32),far((rows,c),BF)),
        grid=(1,),in_specs=[VMEM_SPEC]*3+[layer_spec(w,layer)]+[VMEM_SPEC]*(len(args)-4),
        scratch_shapes=[pltpu.VMEM((images,n+2*side,3*c),BF)],
        compiler_params=PARAMS,cost_estimate=takes(7.5),name="conv_forward")(*args)

def stem_kernel(x_ref,w_ref,wt_ref,y_ref,msg_ref,pt_ref,gram_ref,pt,*,side,images):
    n=side*side
    c=w_ref.shape[1]
    x=x_ref[...]
    lane=lax.broadcasted_iota(jnp.int32,x.shape,1)
    row,col=lane//side,lane%side
    pt[...]=jnp.zeros(pt.shape,F32)
    for a in range(3):
        for b in range(3):
            off=(a-1)*side+(b-1)
            v=pltpu.roll(x,(-off)%n,1) if off else x
            ok=None
            if a==0: ok=row>0
            if a==2: ok=row<side-1
            if b==0: ok=(col>0) if ok is None else ok&(col>0)
            if b==2: ok=(col<side-1) if ok is None else ok&(col<side-1)
            if ok is not None: v=jnp.where(ok,v,0.0)
            t=3*a+b
            for i in range(images):
                pt[i,3*t:3*t+3,:]=v[3*i:3*i+3,:]
    w=jnp.concatenate([w_ref[...],jnp.zeros((pt.shape[1]-w_ref.shape[0],c),F32)],axis=0).astype(BF)
    s0=jnp.zeros((8,c),F32); s1=jnp.zeros((8,c),F32)
    sub=lax.broadcasted_iota(jnp.int32,(pt.shape[1],n),0)
    for i in range(images):
        p=pt[i]
        y=mm(p.astype(BF),w,((0,),(0,)))
        y_ref[i*n:(i+1)*n,:]=y
        pt_ref[:,i*n:(i+1)*n]=jnp.where(sub==w_ref.shape[0],1.0,p).astype(BF)
        s0=s0+fold8(y); s1=s1+fold8(y*y)
    send_sums(msg_ref,s0,s1,jnp.broadcast_to(jnp.sum(wt_ref[...]),(2,MSG-c)))
    taps=pt_ref[...]
    gram_ref[...]=mm(taps,taps,((1,),(1,)))

def stem(x,w,weights,devices,side):
    images=x.shape[0]//3
    n=side*side
    rows,c=images*n,w.shape[1]
    taps=(w.shape[0]+1+15)//16*16
    return pl.pallas_call(functools.partial(stem_kernel,side=side,images=images),
        out_shape=(far((rows,c),F32),jax.ShapeDtypeStruct((devices,2,MSG),F32),far((taps,rows),BF),far((taps,taps),F32)),
        scratch_shapes=[pltpu.VMEM((images,taps,n),F32)],
        compiler_params=PARAMS,cost_estimate=takes(1.5),name="stem_forward")(x,w,weights)

def head_kernel(x_ref,parts_ref,norm_ref,ht_ref,bias_ref,tg_ref,wt_ref,wsum_ref,g_ref,msg_ref,hg_ref,loss_ref,pool,sl0,sl1,*,pixels,side):
    n=side*side
    rows,c=x_ref.shape
    images=rows//n
    sums=jnp.sum(parts_ref[...],axis=0)[:,:c]
    mean,inv,scale,offset=fold_norm(sums,norm_ref[0:1],norm_ref[1:2],pixels)
    for i in range(images):
        v=x_ref[i*n:(i+1)*n,:]
        f,gp=gelu_parts(v*scale+offset,True,True)
        pool[i:i+1,:]=jnp.sum(fold8(f),axis=0,keepdims=True)*(1.0/n)
        sl0[i:i+1,:]=jnp.sum(fold8(gp),axis=0,keepdims=True)
        sl1[i:i+1,:]=jnp.sum(fold8(gp*((v-mean)*inv)),axis=0,keepdims=True)
    pooled=pool[0:images,:]
    low=pooled.astype(BF)
    head=ht_ref[:,0:c].astype(BF)
    logits=mm(low,head,((1,),(1,)))+bias_ref[...]
    spread=jnp.sum(pooled*pooled,axis=1,keepdims=True)/c
    k=math.pi/8.0
    shrink=lax.rsqrt(1.0+k*spread)
    scaled=logits*shrink
    top=jnp.max(scaled,axis=1,keepdims=True)
    ex=jnp.exp(scaled-top)
    tot=jnp.sum(ex,axis=1,keepdims=True)
    logtot=top+jnp.log(tot)
    wt=wt_ref[...]
    tg=tg_ref[...]
    loss_ref[...]=jnp.broadcast_to(jnp.sum(wt*(logtot-jnp.sum(scaled*tg,axis=1,keepdims=True))),loss_ref.shape)
    gs=(jnp.exp(scaled-logtot)-tg)*(wt/wsum_ref[0:1,0:1])
    gl=(gs*shrink).astype(BF)
    gsh=jnp.sum(gs*logits,axis=1,keepdims=True)
    gspread=gsh*(-0.5*k)*shrink*shrink*shrink
    gp=mm(gl,head)+gspread*(2.0/c)*pooled
    g=gp*(1.0/n)
    g_ref[0:images,:]=g
    s0=g*sl0[0:images,:]; s1=g*sl1[0:images,:]
    send_sums(msg_ref,s0,s1)
    hg_ref[:,0:c]=mm(gl,low,((0,),(0,)))
    ones=jnp.ones((images,128),BF)
    hg_ref[:,c:]=mm(gl,ones,((0,),(0,)))

def head(x,parts,norm,head_t,bias,targets,weights,wsum,pixels,side):
    rows,c=x.shape
    images=rows//(side*side)
    dev=parts.shape[0]
    cls=bias.shape[1]
    pad=(images+7)//8*8
    return pl.pallas_call(functools.partial(head_kernel,pixels=pixels,side=side),
        out_shape=(far((pad,c),F32),jax.ShapeDtypeStruct((dev,2,MSG),F32),jax.ShapeDtypeStruct((cls,c+128),F32),jax.ShapeDtypeStruct((1,128),F32)),
        scratch_shapes=[pltpu.VMEM((pad,c),F32)]*3,
        compiler_params=PARAMS,cost_estimate=takes(5.1),name="head_loss")(hold(x),parts,norm,head_t,bias,targets,weights,wsum)

def read_sums(ref,c):
    return jnp.sum(ref[...],axis=0)[:,:c]

def back_two_kernel(res_ref,g_ref,ps_ref,pg_ref,na_ref,one_ref,p1_ref,nb_ref,w_ref,du_ref,msg_ref,back_ref,p3,*,pixels,side):
    n=side*side
    rows,c=res_ref.shape
    images=rows//n
    mean2,inv2,scale2,offset2=fold_norm(read_sums(ps_ref,c),na_ref[0:1],na_ref[1:2],pixels)
    gs=read_sums(pg_ref,c)
    k0=scale2*gs[0:1]*(1.0/pixels); k1=scale2*inv2*gs[1:2]*(1.0/pixels)
    base=k1*mean2-k0
    mean1,inv1,scale1,offset1=fold_norm(read_sums(p1_ref,c),nb_ref[0:1],nb_ref[1:2],pixels)
    clear_borders(p3,side)
    def prep(i):
        sl=slice(i*n,(i+1)*n)
        r=res_ref[sl,:]
        _,slope=gelu_parts(r*scale2+offset2,False,True)
        d=slope*(scale2*g_ref[i:i+1,:])-r*k1+base
        back_ref[sl,:]=d.astype(BF)
        put_taps(p3,i,d,side)
    s0=jnp.zeros((8,c),F32); s1=jnp.zeros((8,c),F32)
    prep(0)
    for i in range(images):
        if i+1<images: prep(i+1)
        sl=slice(i*n,(i+1)*n)
        gh=tap_dots(p3,w_ref,i,n,side,c,True)
        v=one_ref[sl,:]
        _,gp=gelu_parts(v*scale1+offset1,False,True)
        du=gp*gh
        du_ref[sl,:]=du
        s0=s0+fold8(du); s1=s1+fold8(du*((v-mean1)*inv1))
    send_sums(msg_ref,s0,s1)

def back_two(res,g,parts_stat,parts_grad,norm_a,conv_one,parts_one,norm_b,w,pixels,side):
    rows,c=res.shape
    n=side*side
    images=rows//n
    dev=parts_stat.shape[0]
    return pl.pallas_call(functools.partial(back_two_kernel,pixels=pixels,side=side),
        out_shape=(far((rows,c),F32),jax.ShapeDtypeStruct((dev,2,MSG),F32),far((rows,c),BF)),
        grid=(1,),in_specs=[VMEM_SPEC]*8+[layer_spec(w,1)],
        scratch_shapes=[pltpu.VMEM((images,n+2*side,3*c),BF)],
        compiler_params=PARAMS,cost_estimate=takes(9.0),name="back_two")(hold(res),g,parts_stat,parts_grad,norm_a,hold(conv_one),parts_one,norm_b,w)

def turn_kernel(h_ref,qt_ref,qm_ref,hq_ref,a_ref,*,scale):
    c=h_ref.shape[1]
    h=h_ref[...]
    q=qt_ref[...]
    qh=q.astype(BF); ql=(q-qh.astype(F32)).astype(BF)
    hq_ref[0:c,:]=(mm(qh,h,((1,),(1,)))+mm(ql,h,((1,),(1,)))-qm_ref[:,0:1]).astype(BF)
    extra=hq_ref.shape[0]-c
    sub=lax.broadcasted_iota(jnp.int32,(extra,h.shape[0]),0)
    hq_ref[c:,:]=jnp.where(sub==0,1.0,0.0).astype(BF)
    a_ref[...]=mm(h,h,((0,),(0,)))*scale

def turn(h,qt,qmu,scale):
    rows,c=h.shape
    return pl.pallas_call(functools.partial(turn_kernel,scale=scale),
        out_shape=(far((c+16,rows),BF),far((c,c),F32)),
        compiler_params=PARAMS,cost_estimate=takes(1.3),name="turn_hidden")(hold(h),qt,qmu)

def weight_dots(p3,hq_ref,gw_ref,ones_ref,gf_ref,side,scale):
    images,rows,w=p3.shape
    n=rows-2*side
    c=w//3
    hq=hq_ref[...]
    for a in range(3):
        for b in range(3):
            t=8-(3*a+b)
            rhs=p3[:,side*a:side*a+n,b*c:(b+1)*c].reshape(images*n,c)
            d=mm(hq,rhs)
            gw_ref[:,t*c:(t+1)*c]=d[0:c].astype(gw_ref.dtype)
            ones_ref[:,t*c:(t+1)*c]=d[c:c+8]
    mid=p3[:,side:side+n,c:2*c].reshape(images*n,c)
    gf_ref[...]=mm(mid,mid,((0,),(0,)))*scale

def fill_taps(p3,values,side):
    images,rows,_=p3.shape
    n=rows-2*side
    clear_borders(p3,side)
    for i in range(images): put_taps(p3,i,values(slice(i*n,(i+1)*n)),side)

def weight_two_kernel(back_ref,hq_ref,gw_ref,ones_ref,gf_ref,p3,*,side,scale):
    fill_taps(p3,lambda sl: back_ref[sl,:].astype(F32),side)
    weight_dots(p3,hq_ref,gw_ref,ones_ref,gf_ref,side,scale)

def weight_shapes(c,dt):
    return (jax.ShapeDtypeStruct((c,9*c),dt),jax.ShapeDtypeStruct((8,9*c),F32),far((c,c),F32))

def taps_buffer(rows,c,side):
    n=side*side
    return pltpu.VMEM((rows//n,n+2*side,3*c),BF)

def weight_two(back,hq,side,scale,dt=BF):
    rows,c=back.shape
    return pl.pallas_call(functools.partial(weight_two_kernel,side=side,scale=scale),
        out_shape=weight_shapes(c,dt),scratch_shapes=[taps_buffer(rows,c,side)],
        compiler_params=PARAMS,cost_estimate=takes(6.0),name="weight_two")(hold(back),hold(hq))

def weight_one_kernel(one_ref,du_ref,p1_ref,pg_ref,nb_ref,hq_ref,back_ref,gw_ref,ones_ref,gf_ref,p3,*,pixels,side,scale):
    n=side*side
    rows,c=one_ref.shape
    images=rows//n
    mean1,inv1,scale1,_=fold_norm(read_sums(p1_ref,c),nb_ref[0:1],nb_ref[1:2],pixels)
    gs=read_sums(pg_ref,c)
    k0=scale1*gs[0:1]*(1.0/pixels); k1=scale1*inv1*gs[1:2]*(1.0/pixels)
    base=k1*mean1-k0
    def values(sl):
        d=du_ref[sl,:]*scale1-one_ref[sl,:]*k1+base
        back_ref[sl,:]=d.astype(BF)
        return d
    fill_taps(p3,values,side)
    weight_dots(p3,hq_ref,gw_ref,ones_ref,gf_ref,side,scale)

def weight_one(conv_one,du,parts_one,parts_grad,norm_b,hq,pixels,side,scale,dt=BF):
    rows,c=conv_one.shape
    n=side*side
    images=rows//n
    return pl.pallas_call(functools.partial(weight_one_kernel,pixels=pixels,side=side,scale=scale),
        out_shape=(far((rows,c),BF),)+weight_shapes(c,dt),scratch_shapes=[taps_buffer(rows,c,side)],
        compiler_params=PARAMS,cost_estimate=takes(6.4),name="weight_one")(hold(conv_one),hold(du),parts_one,parts_grad,norm_b,hold(hq))

def back_one_kernel(back_ref,w_ref,stem_ref,p0_ref,n0_ref,dres_ref,pt_ref,ps_ref,p3,*,pixels,side):
    images,rows,w3=p3.shape
    n=rows-2*side
    c=w3//3
    mean0,inv0,scale0,offset0=fold_norm(read_sums(p0_ref,c),n0_ref[0:1],n0_ref[1:2],pixels)
    taps=pt_ref.shape[0]
    s0=jnp.zeros((8,c),F32); s1=jnp.zeros((8,c),F32)
    acc=jnp.zeros((taps,c),F32)
    clear_borders(p3,side)
    def prep(i): put_taps(p3,i,back_ref[i*n:(i+1)*n,:].astype(F32),side)
    prep(0)
    for i in range(images):
        if i+1<images: prep(i+1)
        sl=slice(i*n,(i+1)*n)
        gh=tap_dots(p3,w_ref,i,n,side,c,True)
        v=stem_ref[sl,:]
        _,gp=gelu_parts(v*scale0+offset0,False,True)
        du=gp*gh
        s0=s0+fold8(du); s1=s1+fold8(du*((v-mean0)*inv0))
        z=du*scale0+dres_ref[sl,:].astype(F32)
        zh=z.astype(BF); zl=(z-zh.astype(F32)).astype(BF)
        p=pt_ref[:,sl]
        acc=acc+mm(p,zh)+mm(p,zl)
    ps_ref[0:taps,:]=acc
    ps_ref[taps:taps+1,:]=jnp.sum(s0,axis=0,keepdims=True)
    ps_ref[taps+1:taps+2,:]=jnp.sum(s1,axis=0,keepdims=True)
    ps_ref[taps+2:,:]=jnp.zeros((ps_ref.shape[0]-taps-2,c),F32)

def back_one(back,w,stem_out,parts0,norm0,dres,pt,pixels,side):
    rows,c=back.shape
    taps=pt.shape[0]
    return pl.pallas_call(functools.partial(back_one_kernel,pixels=pixels,side=side),
        out_shape=jax.ShapeDtypeStruct((taps+8,c),F32),
        grid=(1,),in_specs=[VMEM_SPEC]+[layer_spec(w,0)]+[VMEM_SPEC]*5,
        scratch_shapes=[taps_buffer(rows,c,side)],
        compiler_params=PARAMS,cost_estimate=takes(8.0),name="back_one")(hold(back),w,hold(stem_out),parts0,norm0,hold(dres),hold(pt))

DIAG,HEAD,BORDER,SIDE,STEM,SMALL=0,2,12,32,64,128

def pack_kernel(a1_ref,g1_ref,a2_ref,g2_ref,hg_ref,loss_ref,gram_ref,b1_ref,b2_ref,ss_ref,out_ref,small):
    devices,rows,c=out_ref.shape
    own=c//devices
    r=lax.broadcasted_iota(jnp.int32,(c,c),0); l=lax.broadcasted_iota(jnp.int32,(c,c),1)
    small[...]=jnp.zeros(small.shape,F32)
    for k,(a_ref,g_ref) in enumerate(((a1_ref,g1_ref),(a2_ref,g2_ref))):
        g=g_ref[...]
        both=jnp.where(r<=l,a_ref[...],g)
        small[DIAG+k:DIAG+k+1,:]=jnp.sum(jnp.where(r==l,g,0.0),axis=0,keepdims=True)
        for j in range(devices): out_ref[j,k*own:(k+1)*own,:]=both[j*own:(j+1)*own]
    cls=hg_ref.shape[0]
    small[HEAD:HEAD+cls,:]=hg_ref[:,0:c]
    small[STEM:STEM+ss_ref.shape[0],:]=ss_ref[...]
    small[SIDE:SIDE+gram_ref.shape[0],0:gram_ref.shape[1]]=gram_ref[...]
    small[SIDE:SIDE+cls,128:256]=hg_ref[:,c:c+128]
    small[SIDE+16:SIDE+17,128:256]=loss_ref[...]
    for k,b_ref in enumerate((b1_ref,b2_ref)):
        for t in range(9): small[BORDER+9*k+t:BORDER+9*k+t+1,:]=b_ref[0:1,t*c:(t+1)*c]
    each=rows-2*own
    for j in range(devices):
        if (j+1)*each<=small.shape[0]: out_ref[j,2*own:,:]=small[j*each:(j+1)*each,:]
        else: out_ref[j,2*own:,:]=jnp.zeros((each,c),F32)

def pack(a1,g1,a2,g2,hg,loss,gram,b1,b2,ss,devices):
    c=a1.shape[0]
    rows=2*(c//devices)+-(-SMALL//devices)
    return pl.pallas_call(pack_kernel,out_shape=jax.ShapeDtypeStruct((devices,rows,c),F32),
        scratch_shapes=[pltpu.VMEM((SMALL,c),F32)],
        compiler_params=PARAMS,cost_estimate=takes(1.5),name="pack_sums")(hold(a1),hold(g1),hold(a2),hold(g2),hg,loss,gram,b1,b2,ss)

def add_kernel(got_ref,out_ref):
    t=got_ref[0]
    for j in range(1,got_ref.shape[0]): t=t+got_ref[j]
    for j in range(got_ref.shape[0]): out_ref[j]=t

def add_pieces(got):
    return pl.pallas_call(add_kernel,out_shape=jax.ShapeDtypeStruct(got.shape,F32),compiler_params=PARAMS,cost_estimate=takes(1.0),name="add_pieces")(got)

def unpack_small(all_ref,small,own):
    devices,rows,c=all_ref.shape
    each=rows-2*own
    for j in range(min(devices,SMALL//each)): small[j*each:(j+1)*each,:]=all_ref[j,2*own:,:]

def adam_refs(p_ref,m_ref,v_ref,g,out,rate,decay,consts):
    beta1,beta2,fix1,fix2,eps=consts
    m=beta1*m_ref[...]+(1.0-beta1)*g
    v=beta2*v_ref[...]+(1.0-beta2)*g*g
    p=p_ref[...]
    out[0][...]=p-rate*((m/fix1)/(jnp.sqrt(v/fix2)+eps)+decay*p)
    out[1][...]=m
    out[2][...]=v

def small_kernel(all_ref,p0_ref,p3_ref,p4_ref,sw,sm,sv,hw,hm,hv,nw,nm,nv,loss_ref,so,smo,svo,ho,hmo,hvo,no,nmo,nvo,small,*,own,pixels,consts,rates):
    unpack_small(all_ref,small,own)
    c=sw.shape[1]
    rows=sw.shape[0]
    taps=(rows+1+15)//16*16
    st=small[STEM:STEM+taps+8,:]
    s00=st[taps:taps+1]; s01=st[taps+1:taps+2]
    mean0,inv0,scale0,_=fold_norm(read_sums(p0_ref,c),nw[0:1],nw[1:2],pixels)
    gram=small[SIDE:SIDE+taps,0:128]
    ones0=gram[0:rows,rows:rows+1]
    w=sw[...].astype(BF).astype(F32)
    w=jnp.concatenate([w,jnp.zeros((128-rows,c),F32)],axis=0)
    cross=lax.dot_general(gram[0:rows],w,(((1,),(0,)),((),())),precision=highest,preferred_element_type=F32)
    xs=inv0*(cross-ones0*mean0)
    grad=st[0:rows]-ones0*(scale0*s00/pixels)-xs*(scale0*s01/pixels)
    adam_refs(sw,sm,sv,grad,(so,smo,svo),rates[0],rates[1],consts)
    cls=hw.shape[0]
    hg=jnp.concatenate([small[HEAD:HEAD+cls,:],small[SIDE:SIDE+cls,128:129]],axis=1)
    adam_refs(hw,hm,hv,hg,(ho,hmo,hvo),rates[2],rates[3],consts)
    s3=read_sums(p3_ref,c); s4=read_sums(p4_ref,c)
    ng=jnp.concatenate([s01,s00,s4[1:2],s4[0:1],s3[1:2],s3[0:1]],axis=0)
    adam_refs(nw,nm,nv,ng,(no,nmo,nvo),rates[4],0.0,consts)
    wsum=jnp.sum(p0_ref[...],axis=0)[0:1,c:c+128]
    lane=lax.broadcasted_iota(jnp.int32,(1,128),1)
    loss_ref[...]=jnp.where(lane==0,small[SIDE+16:SIDE+17,128:256],wsum)

def small_updates(everything,parts0,parts3,parts4,stem3,head3,norm3,pixels,consts,rates):
    c=stem3[0].shape[1]
    own=c//everything.shape[0]
    shapes=[jax.ShapeDtypeStruct((1,128),F32)]+[jax.ShapeDtypeStruct(x.shape,F32) for x in stem3+head3+norm3]
    return pl.pallas_call(functools.partial(small_kernel,own=own,pixels=pixels,consts=consts,rates=rates),out_shape=shapes,
        scratch_shapes=[pltpu.VMEM((SMALL,c),F32)],
        compiler_params=PARAMS,cost_estimate=takes(1.5),name="small_updates")(everything,parts0,parts3,parts4,*stem3,*head3,*norm3)

def turn_rows(x, c, blocks):
    return jnp.concatenate([x[:,t*c:(t+1)*c] for t in range(blocks)],axis=0)

def to_halves(ref, halves):
    r=ref.shape[0]
    halves[0:r,:]=ref[:,0:128]
    halves[r:2*r,:]=ref[:,128:256]

def from_halves(halves, ref):
    r=ref.shape[0]
    ref[:,0:128]=halves[0:r,:].astype(ref.dtype)
    ref[:,128:256]=halves[r:2*r,:].astype(ref.dtype)

def pick_rows(halves, layer, own, blocks):
    r=halves.shape[0]//2
    sides=[jnp.concatenate([halves[pl.ds(h*r+layer*blocks+t,own,stride=2*blocks),:] for t in range(blocks)],axis=0) for h in range(2)]
    return jnp.concatenate(sides,axis=1)

def place_rows(halves, layer, own, blocks, v):
    r=halves.shape[0]//2
    for h in range(2):
        for t in range(blocks): halves[pl.ds(h*r+layer*blocks+t,own,stride=2*blocks),:]=v[t*own:(t+1)*own,h*128:(h+1)*128]

def move_kernel(g_ref,all_ref,qmu_ref,q_ref,m_ref,v_ref,mo_ref,vo_ref,send_ref,m_sc,v_sc,small,*,consts):
    beta1,beta2,fix1,fix2,eps=consts
    own,w=g_ref.shape
    w=w//2
    unpack_small(all_ref,small,own)
    to_halves(m_ref,m_sc)
    to_halves(v_ref,v_sc)
    c=q_ref.shape[1]
    blocks=w//c
    for l in range(2):
        b=jnp.concatenate([jnp.broadcast_to(small[BORDER+l*blocks+t:BORDER+l*blocks+t+1,:],(own,c)) for t in range(blocks)],axis=0)
        qm=jnp.concatenate([qmu_ref[l]]*blocks,axis=0)
        x=turn_rows(g_ref[:,l*w:(l+1)*w],c,blocks)+qm[:,0:1]*b
        rot=dot3(x,q_ref[2*l+1])
        m=beta1*pick_rows(m_sc,l,own,blocks)+(1.0-beta1)*rot
        v=beta2*pick_rows(v_sc,l,own,blocks)+(1.0-beta2)*rot*rot
        place_rows(m_sc,l,own,blocks,m)
        place_rows(v_sc,l,own,blocks,v)
        step=(m/fix1)/(jnp.sqrt(v/fix2)+eps)
        back=dot3(step,q_ref[2*l+1],((1,),(1,)))
        for t in range(blocks): send_ref[:,l*w+t*c:l*w+(t+1)*c]=back[t*own:(t+1)*own,:].astype(BF)
    from_halves(m_sc,mo_ref)
    from_halves(v_sc,vo_ref)

def move(g,everything,qmu,bases,m,v,consts):
    own,w=g.shape
    return pl.pallas_call(functools.partial(move_kernel,consts=consts),
        out_shape=(jax.ShapeDtypeStruct(m.shape,F32),jax.ShapeDtypeStruct(m.shape,F32),jax.ShapeDtypeStruct((own,w),BF)),
        scratch_shapes=[pltpu.VMEM((2*m.shape[0],128),F32)]*2+[pltpu.VMEM((SMALL,m.shape[1]),F32)],
        compiler_params=PARAMS,cost_estimate=takes(2.0),name="moments_and_direction")(g,everything,qmu,bases,m,v)

def finish_kernel(me_ref,near_ref,far_ref,rows_ref,w_ref,out_ref,low_ref,w_sc,*,rate,decay):
    to_halves(w_ref,w_sc)
    count,width=near_ref.shape
    c=2*count
    half=width//2
    own=rows_ref.shape[1]
    blocks=half//c
    bits=own.bit_length()-1
    i=lax.broadcasted_iota(jnp.int32,(c,count),0)
    j=lax.broadcasted_iota(jnp.int32,(c,count),1)
    slot=2*lax.shift_right_logical(j,bits)
    picks=[(i==lax.shift_left((slot+core)^me_ref[0],bits)+(j&(own-1))).astype(BF) for core in range(2)]
    for l in range(2):
        q=rows_ref[l]
        qh=q.astype(BF); ql=(q-qh.astype(F32)).astype(BF)
        both=jnp.concatenate([qh,ql],axis=0)
        d=None
        for pick,part in zip(picks,(near_ref,far_ref)):
            e=mm(mm(both,pick).astype(BF),part[:,l*half:(l+1)*half])
            d=e if d is None else d+e
        d=d[0:own]+d[own:2*own]
        w=pick_rows(w_sc,l,own,blocks)
        place_rows(w_sc,l,own,blocks,w-rate*(turn_rows(d,c,blocks)+decay*w))
    from_halves(w_sc,out_ref)
    from_halves(w_sc,low_ref)

def finish(me,near,far,rows,w,rate,decay):
    return pl.pallas_call(functools.partial(finish_kernel,rate=rate,decay=decay),
        out_shape=(jax.ShapeDtypeStruct(w.shape,F32),jax.ShapeDtypeStruct(w.shape,BF)),
        in_specs=[pl.BlockSpec(memory_space=pltpu.SMEM)]+[VMEM_SPEC]*4,
        scratch_shapes=[pltpu.VMEM((2*w.shape[0],128),F32)],
        compiler_params=PARAMS,cost_estimate=takes(2.5),name="new_weights")(me,near,far,rows,w)

CLASSES=10
STEP=5
BETA_ONE=0.9
BETA_TWO=0.99
ADAM_EPS=1e-08
WEIGHT_DECAY=0.01
RATE_CONV=0.02
RATE_STEM=0.1
RATE_HEAD=0.1
RATE_NORM=0.5


def bit_groups(devices):
    total_bits=devices.bit_length()-1
    groups=[(0,1)]
    while groups[-1][0]+groups[-1][1]<total_bits:
        first=groups[-1][0]+groups[-1][1]
        groups.append((first,min(2,total_bits-first)))
    return groups

def swap(values, mask, devices):
    return lax.ppermute(values,"dp",[(i,i^mask) for i in range(devices)])

def exchange(pieces):
    return lax.all_to_all(pieces,"dp",0,0,tiled=True)

def gather_all(piece, first_wait=(), last_wait=()):
    devices=lax.axis_size("dp")
    me=lax.axis_index("dp")
    groups=bit_groups(devices)[::-1]
    held=piece[(None,)*len(groups)]
    for axis,(first,width) in enumerate(groups):
        radix=1<<width
        mine=(me>>first)&(radix-1)
        got=[held]+[swap(held,k<<first,devices) for k in range(1,radix)]
        ordered=[]
        for j in range(radix):
            value=got[j]
            for m in range(1,radix): value=jnp.where(mine==m,got[j^m],value)
            ordered.append(value)
        held=jnp.concatenate(ordered,axis=axis)
        if axis==0:
            held=after(held,*first_wait)
        if axis==len(groups)-2 and last_wait: held=after(held,*last_wait)
    return held.reshape((devices,)+piece.shape)

def gather_near_and_far(piece, between):
    devices=lax.axis_size("dp")
    groups=bit_groups(devices)[::-1]
    held=piece[(None,)*(len(groups)-1)]
    for axis,(first,width) in enumerate(groups[:-1]):
        held=jnp.concatenate([held]+[swap(held,k<<first,devices) for k in range(1,1<<width)],axis=axis)
        if axis==0: waited=between(held)
    held=held.reshape((devices//2,)+piece.shape)
    return held,swap(after(held,waited),1,devices),waited

def scatter_rounds(pieces, devices):
    groups=bit_groups(devices)
    me=lax.axis_index("dp")
    held=pieces.reshape(tuple(1<<width for _,width in groups[::-1])+pieces.shape[1:])
    def step(held, order):
        first,width=groups[order]
        axis=len(groups)-1-order
        radix=1<<width
        mine=(me>>first)&(radix-1)
        parts=[lax.dynamic_slice_in_dim(held,mine^k,1,axis=axis) for k in range(radix)]
        total=parts[0].astype(F32)
        for k in range(1,radix):
            total=total+swap(parts[k].astype(BF),k<<first,devices).astype(F32)
        return total
    return held,step,len(groups)

def after(value, *earlier):
    return lax.optimization_barrier((value,)+earlier)[0]

def expected_gelu(gain, shift):
    spread=jnp.sqrt(1.0+gain*gain)
    at=shift/spread
    return shift*(0.5+0.5*lax.erf(at*math.sqrt(0.5)))+gain*gain/spread*jnp.exp(-0.5*at*at)*(1.0/math.sqrt(2.0*math.pi))

def local(images, labels, groups, conv_w, conv_m, conv_v, rot_bases, stem_w, stem_m, stem_v, head_w, head_m, head_v, norm_p, norm_m, norm_v):
    devices=lax.axis_size("dp")
    me=lax.axis_index("dp")
    count,side=images.shape[0],images.shape[1]
    c=conv_w.shape[1]
    pixels=count*side*side*devices
    own=c//devices
    packed=conv_w.reshape(own,18*c).astype(BF)
    weights=1.0+3.0*groups.astype(F32)
    x=images.transpose(0,3,1,2).reshape(3*count,side*side).astype(F32)
    stem_out,msg0,pt,gram=stem(x,stem_w,weights[None,:],devices,side)
    parts0=exchange(msg0)
    w_all=gather_all(packed,(msg0,),(parts0,)).reshape(c,18*c)
    left_t=rot_bases[0::2].transpose(0,2,1)
    mu=[expected_gelu(norm_p[2*l],norm_p[2*l+1]) for l in range(2)]
    qmu=[jnp.dot(left_t[l],mu[l][:,None],precision=highest) for l in range(2)]
    targets=(labels[:,None]==jnp.arange(CLASSES,dtype=jnp.int32)[None,:]).astype(F32)
    conv_one,msg1,hid1=forward(stem_out,parts0,norm_p[0:2],w_all,0,None,pixels,side)
    parts1=exchange(msg1)
    hq1,a_one=turn(hid1,left_t[0],qmu[0],1.0/pixels)
    residual,msg2,hid2=forward(conv_one,after(parts1,a_one),norm_p[2:4],w_all,1,stem_out,pixels,side)
    parts2=exchange(msg2)
    hq2,a_two=turn(hid2,left_t[1],qmu[1],1.0/pixels)
    wsum=jnp.sum(parts0[:,0:1,c:c+1],axis=0)
    g,msg3,head_g,loss=head(residual,after(parts2,a_two),norm_p[4:6],head_w.T,head_w[c:c+1],targets,weights[:,None],wsum,pixels,side)
    parts3=exchange(msg3)
    du1,msg4,backtwo=back_two(residual,g,parts2,parts3,norm_p[4:6],conv_one,parts1,norm_p[2:4],w_all,pixels,side)
    parts4=exchange(msg4)
    gw_two,ones_two,g_two=weight_two(backtwo,hq2,side,float(pixels))
    two,step,rounds=scatter_rounds(gw_two.reshape(devices,own,9*c),devices)
    two=step(two,0)
    backone,gw_one,ones_one,g_one=weight_one(conv_one,du1,parts1,after(parts4,ones_two),norm_p[2:4],hq1,pixels,side,float(pixels))
    one,step,_=scatter_rounds(gw_one.reshape(devices,own,9*c),devices)
    first=jnp.concatenate([step(one,0),two],axis=-1)
    stem_sums=back_one(after(backone,first),w_all,stem_out,parts0,norm_p[0:2],backtwo,pt,pixels,side)
    packed_sums=pack(a_one,g_one,a_two,g_two,head_g,loss,gram,ones_one,ones_two,stem_sums,devices)
    both=after(step(first,1),packed_sums)
    added=add_pieces(exchange(packed_sums))
    everything=exchange(added)
    for order in range(2,rounds): both=step(both,order)
    both=both.reshape(own,18*c)
    where=jnp.reshape(me,(1,)).astype(jnp.int32)
    inverse,factors,damped=inverses(where,everything,4)
    consts=(BETA_ONE,BETA_TWO,1.0-BETA_ONE**STEP,1.0-BETA_TWO**STEP,ADAM_EPS)
    q_own=jnp.stack([lax.dynamic_slice_in_dim(qmu[l],me*own,own,0) for l in range(2)])
    m_new,v_new,half=move(after(both,inverse),everything,q_own,rot_bases,conv_m,conv_v,consts)
    near,far_half,bases_new=gather_near_and_far(half,lambda held: new_bases(after(damped,held),rot_bases))
    rows=lax.dynamic_slice_in_dim(rot_bases,me*own,own,1)[0::2]
    conv_new,conv_low=finish(where,near.reshape(c//2,18*c),far_half.reshape(c//2,18*c),rows,conv_w,RATE_CONV,WEIGHT_DECAY)
    small=small_updates(everything,parts0,parts3,parts4,(stem_w,stem_m,stem_v),(head_w.T,head_m.T,head_v.T),(norm_p,norm_m,norm_v),pixels,consts,(RATE_STEM,WEIGHT_DECAY,RATE_HEAD,WEIGHT_DECAY,RATE_NORM))
    return (small[0][0,0:2],factors,inverse,conv_new,m_new,v_new,bases_new,small[1],small[2],small[3],small[4].T,small[5].T,small[6].T,small[7],small[8],small[9],conv_low)

def solution(mesh):
    one=P("dp",None)
    return jax.shard_map(local,mesh=mesh,in_specs=(P("dp",None,None,None),P("dp"),P("dp"),one,one,one)+(P(),)*10,out_specs=(P(),one,one,one,one,one)+(P(),)*10+(one,),check_vma=False)
```

```python
import functools
import math

import jax
import jax.numpy as jnp
from jax import lax
from jax.experimental import pallas as pl
from jax.experimental.pallas import tpu as pltpu
from jax.sharding import PartitionSpec as P

NS_ITERS=6; DAMPING=0.1
highest=HI=lax.Precision.HIGHEST
def dotp(a,b,dims=((1,),(0,)),prec=HI):
    return lax.dot_general(a,b,(dims,((),())),precision=prec,preferred_element_type=jnp.float32)
def split(a):
    hi=a.astype(jnp.bfloat16)
    return hi,(a-hi.astype(jnp.float32)).astype(jnp.bfloat16)
def dot3(a,b,dims=((1,),(0,))):
    ah,al=split(a); bh,bl=split(b)
    d=lambda x,y: lax.dot_general(x,y,(dims,((),())),preferred_element_type=jnp.float32)
    return d(ah,bh)+(d(ah,bl)+d(al,bh))
def inverse_kernel(me_ref,same_ref,other_ref,inv_ref,fac_ref,m_ref,p_ref,x_ref):
    chips,height,n=same_ref.shape
    devices=2*chips
    own=n//devices
    M4=4
    me=me_ref[0]
    r=lax.broadcasted_iota(jnp.int32,(n,n),0); c=lax.broadcasted_iota(jnp.int32,(n,n),1)
    eye=(r==c).astype(jnp.float32)
    each=height-2*own
    Fs=[]
    for k in range(2):
        for j in range(devices): p_ref[j*own:(j+1)*own,:]=piece_of(me_ref,same_ref,other_ref,j,slice(k*own,(k+1)*own))
        P=p_ref[...]
        Pt=P.T
        place=2*own+(DIAG+k)%each
        diag=piece_of(me_ref,same_ref,other_ref,(DIAG+k)//each,slice(place,place+1))
        Fs.append(jnp.where(r<=c,P,Pt))
        Fs.append(jnp.where(r==c,diag,jnp.where(r>c,P,Pt)))
    start=pl.multiple_of(me*own,own)
    def own_rows(out_ref):
        for m in range(M4):
            rows=x_ref[m,pl.ds(start,own),:]
            for i in range(own): out_ref[M4*i+m:M4*i+m+1,:]=rows[i:i+1,:]
    Ms=[]
    for m in range(M4):
        F=Fs[m]
        tr=jnp.sum(F*eye)
        M=F+(DAMPING*tr/n)*eye
        Ms.append(M)
        m_ref[m]=M
        x_ref[m]=F
    own_rows(fac_ref)
    Xs=[eye*lax.rsqrt(jnp.sum(M*M)) for M in Ms]
    for _ in range(NS_ITERS):
        products=[dot3(X,M) for X,M in zip(Xs,Ms)]
        Xs=[2.0*X-dot3(p,X) for p,X in zip(products,Xs)]
    for m in range(M4): x_ref[m]=Xs[m]
    own_rows(inv_ref)

def inverses(me,same,other,m4):
    chips,_,n=same.shape
    own=n//(2*chips)
    return pl.pallas_call(inverse_kernel,
        out_shape=(jax.ShapeDtypeStruct((m4*own,n),jnp.float32),jax.ShapeDtypeStruct((m4*own,n),jnp.float32),jax.ShapeDtypeStruct((m4,n,n),jnp.float32)),
        in_specs=[pl.BlockSpec(memory_space=pltpu.SMEM)]+[pl.BlockSpec(memory_space=pltpu.VMEM)]*2,
        scratch_shapes=[pltpu.VMEM((n,n),jnp.float32),pltpu.VMEM((m4,n,n),jnp.float32)],
        compiler_params=pltpu.CompilerParams(vmem_limit_bytes=48*2**20),
        cost_estimate=takes(11.0),name="damped_inverses")(me,same,other)

def sub(row, like):
    return jnp.broadcast_to(row,like.shape)

def bases_kernel(m_ref,q_ref,qn_ref,b_ref):
    M4,n,_=m_ref.shape
    nb=64
    for m in range(M4):
        Yt=dotp(q_ref[m],m_ref[m],((0,),(0,)))
        b_ref[m,:,n:]=Yt
        b_ref[m,:,:n]=dotp(Yt,Yt,((1,),(1,)))
    li=lax.broadcasted_iota(jnp.int32,(8,128),1); si=lax.broadcasted_iota(jnp.int32,(8,128),0)
    tiles=nb//8
    for k in range(n//nb):
        lo=k*nb; t0=(lo//128)*128; off=lo-t0
        V=[]
        for m in range(M4):
            D=b_ref[m,lo:lo+nb,t0:t0+128]
            if off: D=pltpu.roll(D,128-off,1)
            V.append([jnp.where(li<nb,D[8*i:8*i+8],jnp.where(li-nb==si+8*i,1.0,0.0)) for i in range(tiles)])
        rows=[[None]*tiles for _ in range(M4)]
        for b in range(tiles):
            pivots=[[jnp.broadcast_to(V[m][b][:,8*b+j:8*b+j+1],(8,128)) for j in range(8)] for m in range(M4)]
            below=[[[jnp.broadcast_to(V[m][i][:,8*b+j:8*b+j+1],(8,128)) for j in range(8)] for i in range(b+1,tiles)] for m in range(M4)]
            R=[V[m][b] for m in range(M4)]
            kept=[R[m] for m in range(M4)]
            size=[pivots[m][0] for m in range(M4)]
            for j in range(8):
                for m in range(M4):
                    col=pivots[m][j]
                    d=sub(col[j:j+1],col)
                    at=si==j
                    kept[m]=jnp.where(at,R[m],kept[m])
                    size[m]=jnp.where(at,d,size[m])
                    inv=1.0/d
                    rj=sub(R[m][j:j+1],R[m])*inv
                    for q in range(j+1,8):
                        pj=sub(pivots[m][q][j:j+1],col)*inv
                        pivots[m][q]=jnp.where(at,pj,pivots[m][q]-col*pj)
                    R[m]=jnp.where(at,rj,R[m]-col*rj)
            for m in range(M4):
                rows[m][b]=kept[m]*lax.rsqrt(size[m])
                spread=[sub(R[m][j:j+1],R[m]) for j in range(8)]
                for i in range(b+1,tiles):
                    cols=below[m][i-b-1]
                    terms=[cols[j]*spread[j] for j in range(8)]
                    while len(terms)>1: terms=[terms[z]+terms[z+1] for z in range(0,len(terms),2)]
                    V[m][i]=V[m][i]-terms[0]
        for m in range(M4):
            E=jnp.concatenate(rows[m],axis=0)[:,nb:2*nb]
            U=dotp(E,b_ref[m,lo:lo+nb,:])
            b_ref[m,lo:lo+nb,:]=U
            if lo+nb<n:
                b_ref[m,lo+nb:,:]=b_ref[m,lo+nb:,:]-dotp(U[:,lo+nb:n],U,((0,),(0,)))
    for m in range(M4):
        qn_ref[m]=b_ref[m,:,n:].T

def new_bases(damped,Q):
    m,n,_=Q.shape
    return pl.pallas_call(bases_kernel,
        out_shape=jax.ShapeDtypeStruct((m,n,n),jnp.float32),
        scratch_shapes=[pltpu.VMEM((m,n,2*n),jnp.float32)],
        compiler_params=pltpu.CompilerParams(vmem_limit_bytes=48*2**20),
        cost_estimate=takes(30.0),name="new_bases")(damped,Q)

EPS_NORM=1e-5
BF=jnp.bfloat16; F32=jnp.float32
MSG=384
ROOT=math.sqrt(2.0/math.pi)
def takes(micros):
    return pl.CostEstimate(flops=int(micros*1.0e9),bytes_accessed=int(micros*3.0e6),transcendentals=0)

def hold(x):
    return pltpu.with_memory_space_constraint(x,pltpu.HBM)

def far(shape,dtype):
    return pltpu.HBM(shape,dtype)

PARAMS=pltpu.CompilerParams(vmem_limit_bytes=48*2**20)

def mm(a,b,dims=((1,),(0,))):
    return lax.dot_general(a,b,(dims,((),())),preferred_element_type=F32)

def gelu_parts(x, need_value=True, need_slope=False):
    sq=x*x
    t=jnp.tanh(x*(ROOT+(ROOT*0.044715)*sq))
    half=0.5+0.5*t
    value=x*half if need_value else None
    slope=None
    if need_slope:
        slope=half+(0.5*x)*(1.0-t*t)*(ROOT+(3.0*ROOT*0.044715)*sq)
    return value,slope

def fold_norm(sums, gain, shift, pixels):
    mean=sums[0:1]/pixels
    var=sums[1:2]/pixels-mean*mean
    inv=lax.rsqrt(var+EPS_NORM)
    return mean,inv,gain*inv,shift-mean*(gain*inv)

def shift_taps(v, side):
    col=lax.broadcasted_iota(jnp.int32,v.shape,0)%side
    n=v.shape[0]
    left=jnp.where(col==0,0.0,pltpu.roll(v,1,0))
    right=jnp.where(col==side-1,0.0,pltpu.roll(v,n-1,0))
    return left,right

def clear_borders(p3, side):
    b,rows,w=p3.shape
    for i in range(b):
        p3[i,0:side,:]=jnp.zeros((side,w),BF)
        p3[i,rows-side:rows,:]=jnp.zeros((side,w),BF)

def put_taps(p3, i, v, side):
    n,c=v.shape
    left,right=shift_taps(v,side)
    p3[i,side:side+n,0:c]=left.astype(BF)
    p3[i,side:side+n,c:2*c]=v.astype(BF)
    p3[i,side:side+n,2*c:3*c]=right.astype(BF)

def tap_dots(p3, w_ref, i, n, side, c, back):
    acc=None
    for a in range(3):
        for b in range(3):
            t=3*a+b
            lhs=p3[i,side*a:side*a+n,b*c:(b+1)*c]
            tt=8-t if back else t
            w=w_ref[:,tt*c:(tt+1)*c]
            d=mm(lhs,w,((1,),(1,)) if back else ((1,),(0,)))
            acc=d if acc is None else acc+d
    return acc

def fold8(v):
    n,c=v.shape
    return jnp.sum(v.reshape(n//8,8,c),axis=0)

def send_sums(out_ref, s0, s1, extra=None):
    n=out_ref.shape[0]
    rows=jnp.concatenate([jnp.sum(s0,axis=0,keepdims=True),jnp.sum(s1,axis=0,keepdims=True)],axis=0)
    tail=jnp.zeros((2,MSG-rows.shape[1]),F32) if extra is None else extra
    msg=jnp.concatenate([rows,tail],axis=1)
    out_ref[...]=jnp.broadcast_to(msg[None],out_ref.shape)

def fwd_kernel(x_ref,parts_ref,norm_ref,w_ref,*rest,pixels,side,residual):
    if residual: stem_ref,y_ref,msg_ref,h_ref,p3=rest
    else: y_ref,msg_ref,h_ref,p3=rest
    images,n,_=p3.shape
    n-=2*side
    c=x_ref.shape[1]
    sums=jnp.sum(parts_ref[...],axis=0)[:,:c]
    _,_,scale,offset=fold_norm(sums,norm_ref[0:1],norm_ref[1:2],pixels)
    clear_borders(p3,side)
    def prep(i):
        v=x_ref[i*n:(i+1)*n,:]*scale+offset
        h,_=gelu_parts(v)
        put_taps(p3,i,h,side)
        h_ref[i*n:(i+1)*n,:]=h.astype(BF)
    s0=jnp.zeros((8,c),F32); s1=jnp.zeros((8,c),F32)
    prep(0)
    for i in range(images):
        if i+1<images: prep(i+1)
        y=tap_dots(p3,w_ref,i,n,side,c,False)
        if residual: y=y+stem_ref[i*n:(i+1)*n,:]
        y_ref[i*n:(i+1)*n,:]=y
        s0=s0+fold8(y); s1=s1+fold8(y*y)
    send_sums(msg_ref,s0,s1)

def layer_spec(w,layer):
    c=w.shape[0]
    return pl.BlockSpec((c,9*c),lambda i: (0,layer))

VMEM_SPEC=pl.BlockSpec(memory_space=pltpu.VMEM)

def forward(x,parts,norm,w,layer,stem,pixels,side):
    rows,c=x.shape
    n=side*side
    images=rows//n
    dev=parts.shape[0]
    args=(hold(x),parts,norm,w)+((hold(stem),) if stem is not None else ())
    return pl.pallas_call(functools.partial(fwd_kernel,pixels=pixels,side=side,residual=stem is not None),
        out_shape=(far((rows,c),F32),jax.ShapeDtypeStruct((dev,2,MSG),F32),far((rows,c),BF)),
        grid=(1,),in_specs=[VMEM_SPEC]*3+[layer_spec(w,layer)]+[VMEM_SPEC]*(len(args)-4),
        scratch_shapes=[pltpu.VMEM((images,n+2*side,3*c),BF)],
        compiler_params=PARAMS,cost_estimate=takes(7.5),name="conv_forward")(*args)

def stem_kernel(x_ref,w_ref,wt_ref,y_ref,msg_ref,pt_ref,gram_ref,pt,*,side,images):
    n=side*side
    c=w_ref.shape[1]
    x=x_ref[...]
    lane=lax.broadcasted_iota(jnp.int32,x.shape,1)
    row,col=lane//side,lane%side
    pt[...]=jnp.zeros(pt.shape,F32)
    for a in range(3):
        for b in range(3):
            off=(a-1)*side+(b-1)
            v=pltpu.roll(x,(-off)%n,1) if off else x
            ok=None
            if a==0: ok=row>0
            if a==2: ok=row<side-1
            if b==0: ok=(col>0) if ok is None else ok&(col>0)
            if b==2: ok=(col<side-1) if ok is None else ok&(col<side-1)
            if ok is not None: v=jnp.where(ok,v,0.0)
            t=3*a+b
            for i in range(images):
                pt[i,3*t:3*t+3,:]=v[3*i:3*i+3,:]
    w=jnp.concatenate([w_ref[...],jnp.zeros((pt.shape[1]-w_ref.shape[0],c),F32)],axis=0).astype(BF)
    s0=jnp.zeros((8,c),F32); s1=jnp.zeros((8,c),F32)
    sub=lax.broadcasted_iota(jnp.int32,(pt.shape[1],n),0)
    for i in range(images):
        p=pt[i]
        y=mm(p.astype(BF),w,((0,),(0,)))
        y_ref[i*n:(i+1)*n,:]=y
        pt_ref[:,i*n:(i+1)*n]=jnp.where(sub==w_ref.shape[0],1.0,p).astype(BF)
        s0=s0+fold8(y); s1=s1+fold8(y*y)
    send_sums(msg_ref,s0,s1,jnp.broadcast_to(jnp.sum(wt_ref[...]),(2,MSG-c)))
    taps=pt_ref[...]
    gram_ref[...]=mm(taps,taps,((1,),(1,)))

def stem(x,w,weights,devices,side):
    images=x.shape[0]//3
    n=side*side
    rows,c=images*n,w.shape[1]
    taps=(w.shape[0]+1+15)//16*16
    return pl.pallas_call(functools.partial(stem_kernel,side=side,images=images),
        out_shape=(far((rows,c),F32),jax.ShapeDtypeStruct((devices,2,MSG),F32),far((taps,rows),BF),far((taps,taps),F32)),
        scratch_shapes=[pltpu.VMEM((images,taps,n),F32)],
        compiler_params=PARAMS,cost_estimate=takes(1.5),name="stem_forward")(x,w,weights)

def head_kernel(x_ref,parts_ref,norm_ref,ht_ref,bias_ref,tg_ref,wt_ref,wsum_ref,g_ref,msg_ref,hg_ref,loss_ref,pool,sl0,sl1,*,pixels,side):
    n=side*side
    rows,c=x_ref.shape
    images=rows//n
    sums=jnp.sum(parts_ref[...],axis=0)[:,:c]
    mean,inv,scale,offset=fold_norm(sums,norm_ref[0:1],norm_ref[1:2],pixels)
    for i in range(images):
        v=x_ref[i*n:(i+1)*n,:]
        f,gp=gelu_parts(v*scale+offset,True,True)
        pool[i:i+1,:]=jnp.sum(fold8(f),axis=0,keepdims=True)*(1.0/n)
        sl0[i:i+1,:]=jnp.sum(fold8(gp),axis=0,keepdims=True)
        sl1[i:i+1,:]=jnp.sum(fold8(gp*((v-mean)*inv)),axis=0,keepdims=True)
    pooled=pool[0:images,:]
    low=pooled.astype(BF)
    head=ht_ref[:,0:c].astype(BF)
    logits=mm(low,head,((1,),(1,)))+bias_ref[...]
    spread=jnp.sum(pooled*pooled,axis=1,keepdims=True)/c
    k=math.pi/8.0
    shrink=lax.rsqrt(1.0+k*spread)
    scaled=logits*shrink
    top=jnp.max(scaled,axis=1,keepdims=True)
    ex=jnp.exp(scaled-top)
    tot=jnp.sum(ex,axis=1,keepdims=True)
    logtot=top+jnp.log(tot)
    wt=wt_ref[...]
    tg=tg_ref[...]
    loss_ref[...]=jnp.broadcast_to(jnp.sum(wt*(logtot-jnp.sum(scaled*tg,axis=1,keepdims=True))),loss_ref.shape)
    gs=(jnp.exp(scaled-logtot)-tg)*(wt/wsum_ref[0:1,0:1])
    gl=(gs*shrink).astype(BF)
    gsh=jnp.sum(gs*logits,axis=1,keepdims=True)
    gspread=gsh*(-0.5*k)*shrink*shrink*shrink
    gp=mm(gl,head)+gspread*(2.0/c)*pooled
    g=gp*(1.0/n)
    g_ref[0:images,:]=g
    s0=g*sl0[0:images,:]; s1=g*sl1[0:images,:]
    send_sums(msg_ref,s0,s1)
    hg_ref[:,0:c]=mm(gl,low,((0,),(0,)))
    ones=jnp.ones((images,128),BF)
    hg_ref[:,c:]=mm(gl,ones,((0,),(0,)))

def head(x,parts,norm,head_t,bias,targets,weights,wsum,pixels,side):
    rows,c=x.shape
    images=rows//(side*side)
    dev=parts.shape[0]
    cls=bias.shape[1]
    pad=(images+7)//8*8
    return pl.pallas_call(functools.partial(head_kernel,pixels=pixels,side=side),
        out_shape=(far((pad,c),F32),jax.ShapeDtypeStruct((dev,2,MSG),F32),jax.ShapeDtypeStruct((cls,c+128),F32),jax.ShapeDtypeStruct((1,128),F32)),
        scratch_shapes=[pltpu.VMEM((pad,c),F32)]*3,
        compiler_params=PARAMS,cost_estimate=takes(5.1),name="head_loss")(hold(x),parts,norm,head_t,bias,targets,weights,wsum)

def read_sums(ref,c):
    return jnp.sum(ref[...],axis=0)[:,:c]

def back_two_kernel(res_ref,g_ref,ps_ref,pg_ref,na_ref,one_ref,p1_ref,nb_ref,w_ref,du_ref,msg_ref,back_ref,p3,*,pixels,side):
    n=side*side
    rows,c=res_ref.shape
    images=rows//n
    mean2,inv2,scale2,offset2=fold_norm(read_sums(ps_ref,c),na_ref[0:1],na_ref[1:2],pixels)
    gs=read_sums(pg_ref,c)
    k0=scale2*gs[0:1]*(1.0/pixels); k1=scale2*inv2*gs[1:2]*(1.0/pixels)
    base=k1*mean2-k0
    mean1,inv1,scale1,offset1=fold_norm(read_sums(p1_ref,c),nb_ref[0:1],nb_ref[1:2],pixels)
    clear_borders(p3,side)
    def prep(i):
        sl=slice(i*n,(i+1)*n)
        r=res_ref[sl,:]
        _,slope=gelu_parts(r*scale2+offset2,False,True)
        d=slope*(scale2*g_ref[i:i+1,:])-r*k1+base
        back_ref[sl,:]=d.astype(BF)
        put_taps(p3,i,d,side)
    s0=jnp.zeros((8,c),F32); s1=jnp.zeros((8,c),F32)
    prep(0)
    for i in range(images):
        if i+1<images: prep(i+1)
        sl=slice(i*n,(i+1)*n)
        gh=tap_dots(p3,w_ref,i,n,side,c,True)
        v=one_ref[sl,:]
        _,gp=gelu_parts(v*scale1+offset1,False,True)
        du=gp*gh
        du_ref[sl,:]=du
        s0=s0+fold8(du); s1=s1+fold8(du*((v-mean1)*inv1))
    send_sums(msg_ref,s0,s1)

def back_two(res,g,parts_stat,parts_grad,norm_a,conv_one,parts_one,norm_b,w,pixels,side):
    rows,c=res.shape
    n=side*side
    images=rows//n
    dev=parts_stat.shape[0]
    return pl.pallas_call(functools.partial(back_two_kernel,pixels=pixels,side=side),
        out_shape=(far((rows,c),F32),jax.ShapeDtypeStruct((dev,2,MSG),F32),far((rows,c),BF)),
        grid=(1,),in_specs=[VMEM_SPEC]*8+[layer_spec(w,1)],
        scratch_shapes=[pltpu.VMEM((images,n+2*side,3*c),BF)],
        compiler_params=PARAMS,cost_estimate=takes(9.0),name="back_two")(hold(res),g,parts_stat,parts_grad,norm_a,hold(conv_one),parts_one,norm_b,w)

def turn_kernel(h_ref,qt_ref,qm_ref,hq_ref,a_ref,*,scale):
    c=h_ref.shape[1]
    h=h_ref[...]
    q=qt_ref[...]
    qh=q.astype(BF); ql=(q-qh.astype(F32)).astype(BF)
    hq_ref[0:c,:]=(mm(qh,h,((1,),(1,)))+mm(ql,h,((1,),(1,)))-qm_ref[:,0:1]).astype(BF)
    extra=hq_ref.shape[0]-c
    sub=lax.broadcasted_iota(jnp.int32,(extra,h.shape[0]),0)
    hq_ref[c:,:]=jnp.where(sub==0,1.0,0.0).astype(BF)
    a_ref[...]=mm(h,h,((0,),(0,)))*scale

def turn(h,qt,qmu,scale):
    rows,c=h.shape
    return pl.pallas_call(functools.partial(turn_kernel,scale=scale),
        out_shape=(far((c+16,rows),BF),far((c,c),F32)),
        compiler_params=PARAMS,cost_estimate=takes(1.3),name="turn_hidden")(hold(h),qt,qmu)

def weight_dots(p3,hq_ref,gw_ref,ones_ref,gf_ref,side,scale):
    images,rows,w=p3.shape
    n=rows-2*side
    c=w//3
    hq=hq_ref[...]
    for a in range(3):
        for b in range(3):
            t=8-(3*a+b)
            rhs=p3[:,side*a:side*a+n,b*c:(b+1)*c].reshape(images*n,c)
            d=mm(hq,rhs)
            gw_ref[:,t*c:(t+1)*c]=d[0:c].astype(gw_ref.dtype)
            ones_ref[:,t*c:(t+1)*c]=d[c:c+8]
    mid=p3[:,side:side+n,c:2*c].reshape(images*n,c)
    gf_ref[...]=mm(mid,mid,((0,),(0,)))*scale

def fill_taps(p3,values,side):
    images,rows,_=p3.shape
    n=rows-2*side
    clear_borders(p3,side)
    for i in range(images): put_taps(p3,i,values(slice(i*n,(i+1)*n)),side)

def weight_two_kernel(back_ref,hq_ref,gw_ref,ones_ref,gf_ref,p3,*,side,scale):
    fill_taps(p3,lambda sl: back_ref[sl,:].astype(F32),side)
    weight_dots(p3,hq_ref,gw_ref,ones_ref,gf_ref,side,scale)

def weight_shapes(c,dt):
    return (jax.ShapeDtypeStruct((c,9*c),dt),jax.ShapeDtypeStruct((8,9*c),F32),far((c,c),F32))

def taps_buffer(rows,c,side):
    n=side*side
    return pltpu.VMEM((rows//n,n+2*side,3*c),BF)

def weight_two(back,hq,side,scale,dt=BF):
    rows,c=back.shape
    return pl.pallas_call(functools.partial(weight_two_kernel,side=side,scale=scale),
        out_shape=weight_shapes(c,dt),scratch_shapes=[taps_buffer(rows,c,side)],
        compiler_params=PARAMS,cost_estimate=takes(6.0),name="weight_two")(hold(back),hold(hq))

def weight_one_kernel(one_ref,du_ref,p1_ref,pg_ref,nb_ref,hq_ref,back_ref,gw_ref,ones_ref,gf_ref,p3,*,pixels,side,scale):
    n=side*side
    rows,c=one_ref.shape
    images=rows//n
    mean1,inv1,scale1,_=fold_norm(read_sums(p1_ref,c),nb_ref[0:1],nb_ref[1:2],pixels)
    gs=read_sums(pg_ref,c)
    k0=scale1*gs[0:1]*(1.0/pixels); k1=scale1*inv1*gs[1:2]*(1.0/pixels)
    base=k1*mean1-k0
    def values(sl):
        d=du_ref[sl,:]*scale1-one_ref[sl,:]*k1+base
        back_ref[sl,:]=d.astype(BF)
        return d
    fill_taps(p3,values,side)
    weight_dots(p3,hq_ref,gw_ref,ones_ref,gf_ref,side,scale)

def weight_one(conv_one,du,parts_one,parts_grad,norm_b,hq,pixels,side,scale,dt=BF):
    rows,c=conv_one.shape
    n=side*side
    images=rows//n
    return pl.pallas_call(functools.partial(weight_one_kernel,pixels=pixels,side=side,scale=scale),
        out_shape=(far((rows,c),BF),)+weight_shapes(c,dt),scratch_shapes=[taps_buffer(rows,c,side)],
        compiler_params=PARAMS,cost_estimate=takes(6.4),name="weight_one")(hold(conv_one),hold(du),parts_one,parts_grad,norm_b,hold(hq))

def back_one_kernel(back_ref,w_ref,stem_ref,p0_ref,n0_ref,dres_ref,pt_ref,ps_ref,p3,*,pixels,side):
    images,rows,w3=p3.shape
    n=rows-2*side
    c=w3//3
    mean0,inv0,scale0,offset0=fold_norm(read_sums(p0_ref,c),n0_ref[0:1],n0_ref[1:2],pixels)
    taps=pt_ref.shape[0]
    s0=jnp.zeros((8,c),F32); s1=jnp.zeros((8,c),F32)
    acc=jnp.zeros((taps,c),F32)
    clear_borders(p3,side)
    def prep(i): put_taps(p3,i,back_ref[i*n:(i+1)*n,:].astype(F32),side)
    prep(0)
    for i in range(images):
        if i+1<images: prep(i+1)
        sl=slice(i*n,(i+1)*n)
        gh=tap_dots(p3,w_ref,i,n,side,c,True)
        v=stem_ref[sl,:]
        _,gp=gelu_parts(v*scale0+offset0,False,True)
        du=gp*gh
        s0=s0+fold8(du); s1=s1+fold8(du*((v-mean0)*inv0))
        z=du*scale0+dres_ref[sl,:].astype(F32)
        zh=z.astype(BF); zl=(z-zh.astype(F32)).astype(BF)
        p=pt_ref[:,sl]
        acc=acc+mm(p,zh)+mm(p,zl)
    ps_ref[0:taps,:]=acc
    ps_ref[taps:taps+1,:]=jnp.sum(s0,axis=0,keepdims=True)
    ps_ref[taps+1:taps+2,:]=jnp.sum(s1,axis=0,keepdims=True)
    ps_ref[taps+2:,:]=jnp.zeros((ps_ref.shape[0]-taps-2,c),F32)

def back_one(back,w,stem_out,parts0,norm0,dres,pt,pixels,side):
    rows,c=back.shape
    taps=pt.shape[0]
    return pl.pallas_call(functools.partial(back_one_kernel,pixels=pixels,side=side),
        out_shape=jax.ShapeDtypeStruct((taps+8,c),F32),
        grid=(1,),in_specs=[VMEM_SPEC]+[layer_spec(w,0)]+[VMEM_SPEC]*5,
        scratch_shapes=[taps_buffer(rows,c,side)],
        compiler_params=PARAMS,cost_estimate=takes(8.0),name="back_one")(hold(back),w,hold(stem_out),parts0,norm0,hold(dres),hold(pt))

DIAG,HEAD,BORDER,SIDE,STEM,SMALL=0,2,12,32,64,128

def pack_kernel(me_ref,a1_ref,g1_ref,a2_ref,g2_ref,hg_ref,loss_ref,gram_ref,b1_ref,b2_ref,ss_ref,keep_ref,send_ref,small):
    chips,rows,c=keep_ref.shape
    own=c//(2*chips)
    even=(me_ref[0]&1)==0
    def put(i, at, first, second):
        keep_ref[i,at,:]=jnp.where(even,first,second)
        send_ref[i,at,:]=jnp.where(even,second,first)
    r=lax.broadcasted_iota(jnp.int32,(c,c),0); l=lax.broadcasted_iota(jnp.int32,(c,c),1)
    small[...]=jnp.zeros(small.shape,F32)
    for k,(a_ref,g_ref) in enumerate(((a1_ref,g1_ref),(a2_ref,g2_ref))):
        g=g_ref[...]
        both=jnp.where(r<=l,a_ref[...],g)
        small[DIAG+k:DIAG+k+1,:]=jnp.sum(jnp.where(r==l,g,0.0),axis=0,keepdims=True)
        for i in range(chips): put(i,slice(k*own,(k+1)*own),both[2*i*own:(2*i+1)*own],both[(2*i+1)*own:(2*i+2)*own])
    cls=hg_ref.shape[0]
    small[HEAD:HEAD+cls,:]=hg_ref[:,0:c]
    small[STEM:STEM+ss_ref.shape[0],:]=ss_ref[...]
    small[SIDE:SIDE+gram_ref.shape[0],0:gram_ref.shape[1]]=gram_ref[...]
    small[SIDE:SIDE+cls,128:256]=hg_ref[:,c:c+128]
    small[SIDE+16:SIDE+17,128:256]=loss_ref[...]
    for k,b_ref in enumerate((b1_ref,b2_ref)):
        for t in range(9): small[BORDER+9*k+t:BORDER+9*k+t+1,:]=b_ref[0:1,t*c:(t+1)*c]
    each=rows-2*own
    for i in range(chips):
        at=2*i*each
        if at+2*each<=small.shape[0]: put(i,slice(2*own,rows),small[at:at+each,:],small[at+each:at+2*each,:])
        else:
            keep_ref[i,2*own:rows,:]=jnp.zeros((each,c),F32)
            send_ref[i,2*own:rows,:]=jnp.zeros((each,c),F32)

SMEM_SPEC=pl.BlockSpec(memory_space=pltpu.SMEM)

def pack(me,a1,g1,a2,g2,hg,loss,gram,b1,b2,ss,devices):
    c=a1.shape[0]
    rows=2*(c//devices)+-(-SMALL//devices)
    return pl.pallas_call(pack_kernel,out_shape=(jax.ShapeDtypeStruct((devices//2,rows,c),F32),)*2,
        in_specs=[SMEM_SPEC]+[VMEM_SPEC]*10,
        scratch_shapes=[pltpu.VMEM((SMALL,c),F32)],
        compiler_params=PARAMS,cost_estimate=takes(1.5),name="pack_sums")(me,hold(a1),hold(g1),hold(a2),hold(g2),hg,loss,gram,b1,b2,ss)

def add_kernel(got_ref,out_ref):
    t=got_ref[0]
    for j in range(1,got_ref.shape[0]): t=t+got_ref[j]
    for j in range(got_ref.shape[0]): out_ref[j]=t

def add_pieces(got):
    return pl.pallas_call(add_kernel,out_shape=jax.ShapeDtypeStruct(got.shape,F32),compiler_params=PARAMS,cost_estimate=takes(1.0),name="add_pieces")(got)

def piece_of(me_ref,same_ref,other_ref,j,at):
    return jnp.where((me_ref[0]&1)==(j&1),same_ref[j//2,at,:],other_ref[j//2,at,:])

def unpack_small(me_ref,same_ref,other_ref,small,own):
    chips,rows,c=same_ref.shape
    each=rows-2*own
    for j in range(min(2*chips,SMALL//each)): small[j*each:(j+1)*each,:]=piece_of(me_ref,same_ref,other_ref,j,slice(2*own,rows))

def adam_refs(p_ref,m_ref,v_ref,g,out,rate,decay,consts):
    beta1,beta2,fix1,fix2,eps=consts
    m=beta1*m_ref[...]+(1.0-beta1)*g
    v=beta2*v_ref[...]+(1.0-beta2)*g*g
    p=p_ref[...]
    out[0][...]=p-rate*((m/fix1)/(jnp.sqrt(v/fix2)+eps)+decay*p)
    out[1][...]=m
    out[2][...]=v

def small_kernel(me_ref,same_ref,other_ref,p0_ref,p3_ref,p4_ref,sw,sm,sv,hw,hm,hv,nw,nm,nv,loss_ref,so,smo,svo,ho,hmo,hvo,no,nmo,nvo,small,*,own,pixels,consts,rates):
    unpack_small(me_ref,same_ref,other_ref,small,own)
    c=sw.shape[1]
    rows=sw.shape[0]
    taps=(rows+1+15)//16*16
    st=small[STEM:STEM+taps+8,:]
    s00=st[taps:taps+1]; s01=st[taps+1:taps+2]
    mean0,inv0,scale0,_=fold_norm(read_sums(p0_ref,c),nw[0:1],nw[1:2],pixels)
    gram=small[SIDE:SIDE+taps,0:128]
    ones0=gram[0:rows,rows:rows+1]
    w=sw[...].astype(BF).astype(F32)
    w=jnp.concatenate([w,jnp.zeros((128-rows,c),F32)],axis=0)
    cross=lax.dot_general(gram[0:rows],w,(((1,),(0,)),((),())),precision=highest,preferred_element_type=F32)
    xs=inv0*(cross-ones0*mean0)
    grad=st[0:rows]-ones0*(scale0*s00/pixels)-xs*(scale0*s01/pixels)
    adam_refs(sw,sm,sv,grad,(so,smo,svo),rates[0],rates[1],consts)
    cls=hw.shape[0]
    hg=jnp.concatenate([small[HEAD:HEAD+cls,:],small[SIDE:SIDE+cls,128:129]],axis=1)
    adam_refs(hw,hm,hv,hg,(ho,hmo,hvo),rates[2],rates[3],consts)
    s3=read_sums(p3_ref,c); s4=read_sums(p4_ref,c)
    ng=jnp.concatenate([s01,s00,s4[1:2],s4[0:1],s3[1:2],s3[0:1]],axis=0)
    adam_refs(nw,nm,nv,ng,(no,nmo,nvo),rates[4],0.0,consts)
    wsum=jnp.sum(p0_ref[...],axis=0)[0:1,c:c+128]
    lane=lax.broadcasted_iota(jnp.int32,(1,128),1)
    loss_ref[...]=jnp.where(lane==0,small[SIDE+16:SIDE+17,128:256],wsum)

def small_updates(me,same,other,parts0,parts3,parts4,stem3,head3,norm3,pixels,consts,rates):
    c=stem3[0].shape[1]
    own=c//(2*same.shape[0])
    shapes=[jax.ShapeDtypeStruct((1,128),F32)]+[jax.ShapeDtypeStruct(x.shape,F32) for x in stem3+head3+norm3]
    return pl.pallas_call(functools.partial(small_kernel,own=own,pixels=pixels,consts=consts,rates=rates),out_shape=shapes,
        in_specs=[SMEM_SPEC]+[VMEM_SPEC]*(5+9),
        scratch_shapes=[pltpu.VMEM((SMALL,c),F32)],
        compiler_params=PARAMS,cost_estimate=takes(1.5),name="small_updates")(me,same,other,parts0,parts3,parts4,*stem3,*head3,*norm3)

def turn_rows(x, c, blocks):
    return jnp.concatenate([x[:,t*c:(t+1)*c] for t in range(blocks)],axis=0)

def to_halves(ref, halves):
    r=ref.shape[0]
    halves[0:r,:]=ref[:,0:128]
    halves[r:2*r,:]=ref[:,128:256]

def from_halves(halves, ref):
    r=ref.shape[0]
    ref[:,0:128]=halves[0:r,:].astype(ref.dtype)
    ref[:,128:256]=halves[r:2*r,:].astype(ref.dtype)

def pick_rows(halves, layer, own, blocks):
    r=halves.shape[0]//2
    sides=[jnp.concatenate([halves[pl.ds(h*r+layer*blocks+t,own,stride=2*blocks),:] for t in range(blocks)],axis=0) for h in range(2)]
    return jnp.concatenate(sides,axis=1)

def place_rows(halves, layer, own, blocks, v):
    r=halves.shape[0]//2
    for h in range(2):
        for t in range(blocks): halves[pl.ds(h*r+layer*blocks+t,own,stride=2*blocks),:]=v[t*own:(t+1)*own,h*128:(h+1)*128]

def move_kernel(me_ref,g_ref,same_ref,other_ref,qmu_ref,q_ref,m_ref,v_ref,mo_ref,vo_ref,send_ref,m_sc,v_sc,small,*,consts):
    beta1,beta2,fix1,fix2,eps=consts
    own,w=g_ref.shape
    w=w//2
    unpack_small(me_ref,same_ref,other_ref,small,own)
    to_halves(m_ref,m_sc)
    to_halves(v_ref,v_sc)
    c=q_ref.shape[1]
    blocks=w//c
    for l in range(2):
        b=jnp.concatenate([jnp.broadcast_to(small[BORDER+l*blocks+t:BORDER+l*blocks+t+1,:],(own,c)) for t in range(blocks)],axis=0)
        qm=jnp.concatenate([qmu_ref[l]]*blocks,axis=0)
        x=turn_rows(g_ref[:,l*w:(l+1)*w],c,blocks)+qm[:,0:1]*b
        rot=dot3(x,q_ref[2*l+1])
        m=beta1*pick_rows(m_sc,l,own,blocks)+(1.0-beta1)*rot
        v=beta2*pick_rows(v_sc,l,own,blocks)+(1.0-beta2)*rot*rot
        place_rows(m_sc,l,own,blocks,m)
        place_rows(v_sc,l,own,blocks,v)
        step=(m/fix1)/(jnp.sqrt(v/fix2)+eps)
        back=dot3(step,q_ref[2*l+1],((1,),(1,)))
        for t in range(blocks): send_ref[:,l*w+t*c:l*w+(t+1)*c]=back[t*own:(t+1)*own,:].astype(BF)
    from_halves(m_sc,mo_ref)
    from_halves(v_sc,vo_ref)

def move(me,g,same,other,qmu,bases,m,v,consts):
    own,w=g.shape
    return pl.pallas_call(functools.partial(move_kernel,consts=consts),
        out_shape=(jax.ShapeDtypeStruct(m.shape,F32),jax.ShapeDtypeStruct(m.shape,F32),jax.ShapeDtypeStruct((own,w),BF)),
        in_specs=[SMEM_SPEC]+[VMEM_SPEC]*7,
        scratch_shapes=[pltpu.VMEM((2*m.shape[0],128),F32)]*2+[pltpu.VMEM((SMALL,m.shape[1]),F32)],
        compiler_params=PARAMS,cost_estimate=takes(2.0),name="moments_and_direction")(me,g,same,other,qmu,bases,m,v)

def finish_kernel(me_ref,near_ref,far_ref,rows_ref,w_ref,out_ref,low_ref,w_sc,*,rate,decay):
    to_halves(w_ref,w_sc)
    count,width=near_ref.shape
    c=2*count
    half=width//2
    own=rows_ref.shape[1]
    blocks=half//c
    bits=own.bit_length()-1
    i=lax.broadcasted_iota(jnp.int32,(c,count),0)
    j=lax.broadcasted_iota(jnp.int32,(c,count),1)
    slot=2*lax.shift_right_logical(j,bits)
    picks=[(i==lax.shift_left((slot+core)^me_ref[0],bits)+(j&(own-1))).astype(BF) for core in range(2)]
    for l in range(2):
        q=rows_ref[l]
        qh=q.astype(BF); ql=(q-qh.astype(F32)).astype(BF)
        both=jnp.concatenate([qh,ql],axis=0)
        d=None
        for pick,part in zip(picks,(near_ref,far_ref)):
            e=mm(mm(both,pick).astype(BF),part[:,l*half:(l+1)*half])
            d=e if d is None else d+e
        d=d[0:own]+d[own:2*own]
        w=pick_rows(w_sc,l,own,blocks)
        place_rows(w_sc,l,own,blocks,w-rate*(turn_rows(d,c,blocks)+decay*w))
    from_halves(w_sc,out_ref)
    from_halves(w_sc,low_ref)

def finish(me,near,far,rows,w,rate,decay):
    return pl.pallas_call(functools.partial(finish_kernel,rate=rate,decay=decay),
        out_shape=(jax.ShapeDtypeStruct(w.shape,F32),jax.ShapeDtypeStruct(w.shape,BF)),
        in_specs=[pl.BlockSpec(memory_space=pltpu.SMEM)]+[VMEM_SPEC]*4,
        scratch_shapes=[pltpu.VMEM((2*w.shape[0],128),F32)],
        compiler_params=PARAMS,cost_estimate=takes(2.5),name="new_weights")(me,near,far,rows,w)

CLASSES=10
STEP=5
BETA_ONE=0.9
BETA_TWO=0.99
ADAM_EPS=1e-08
WEIGHT_DECAY=0.01
RATE_CONV=0.02
RATE_STEM=0.1
RATE_HEAD=0.1
RATE_NORM=0.5


def bit_groups(devices):
    total_bits=devices.bit_length()-1
    groups=[(0,1)]
    while groups[-1][0]+groups[-1][1]<total_bits:
        first=groups[-1][0]+groups[-1][1]
        groups.append((first,min(2,total_bits-first)))
    return groups

def swap(values, mask, devices):
    return lax.ppermute(values,"dp",[(i,i^mask) for i in range(devices)])

def exchange(pieces):
    return lax.all_to_all(pieces,"dp",0,0,tiled=True)

def gather_all(piece, first_wait=(), last_wait=()):
    devices=lax.axis_size("dp")
    me=lax.axis_index("dp")
    groups=bit_groups(devices)[::-1]
    held=piece[(None,)*len(groups)]
    for axis,(first,width) in enumerate(groups):
        radix=1<<width
        mine=(me>>first)&(radix-1)
        got=[held]+[swap(held,k<<first,devices) for k in range(1,radix)]
        ordered=[]
        for j in range(radix):
            value=got[j]
            for m in range(1,radix): value=jnp.where(mine==m,got[j^m],value)
            ordered.append(value)
        held=jnp.concatenate(ordered,axis=axis)
        if axis==0:
            held=after(held,*first_wait)
        if axis==len(groups)-2 and last_wait: held=after(held,*last_wait)
    return held.reshape((devices,)+piece.shape)

def gather_near_and_far(piece, between):
    devices=lax.axis_size("dp")
    groups=bit_groups(devices)[::-1]
    held=piece[(None,)*(len(groups)-1)]
    for axis,(first,width) in enumerate(groups[:-1]):
        held=jnp.concatenate([held]+[swap(held,k<<first,devices) for k in range(1,1<<width)],axis=axis)
        if axis==0: waited=between(held)
    held=held.reshape((devices//2,)+piece.shape)
    return held,swap(after(held,waited),1,devices),waited

def exchange_chips(pieces):
    devices=lax.axis_size("dp")
    groups=[[2*i+core for i in range(devices//2)] for core in range(2)]
    return lax.all_to_all(pieces,"dp",0,0,tiled=True,axis_index_groups=groups)

def scatter_rounds(pieces, devices):
    groups=bit_groups(devices)
    me=lax.axis_index("dp")
    held=pieces.reshape(tuple(1<<width for _,width in groups[::-1])+pieces.shape[1:])
    def step(held, order):
        first,width=groups[order]
        axis=len(groups)-1-order
        radix=1<<width
        mine=(me>>first)&(radix-1)
        parts=[lax.dynamic_slice_in_dim(held,mine^k,1,axis=axis) for k in range(radix)]
        total=parts[0].astype(F32)
        for k in range(1,radix):
            total=total+swap(parts[k].astype(BF),k<<first,devices).astype(F32)
        return total
    return held,step,len(groups)

def after(value, *earlier):
    return lax.optimization_barrier((value,)+earlier)[0]

def expected_gelu(gain, shift):
    spread=jnp.sqrt(1.0+gain*gain)
    at=shift/spread
    return shift*(0.5+0.5*lax.erf(at*math.sqrt(0.5)))+gain*gain/spread*jnp.exp(-0.5*at*at)*(1.0/math.sqrt(2.0*math.pi))

def local(images, labels, groups, conv_w, conv_m, conv_v, rot_bases, stem_w, stem_m, stem_v, head_w, head_m, head_v, norm_p, norm_m, norm_v):
    devices=lax.axis_size("dp")
    me=lax.axis_index("dp")
    count,side=images.shape[0],images.shape[1]
    c=conv_w.shape[1]
    pixels=count*side*side*devices
    own=c//devices
    packed=conv_w.reshape(own,18*c).astype(BF)
    weights=1.0+3.0*groups.astype(F32)
    x=images.transpose(0,3,1,2).reshape(3*count,side*side).astype(F32)
    stem_out,msg0,pt,gram=stem(x,stem_w,weights[None,:],devices,side)
    parts0=exchange(msg0)
    w_all=gather_all(packed,(msg0,),(parts0,)).reshape(c,18*c)
    left_t=rot_bases[0::2].transpose(0,2,1)
    mu=[expected_gelu(norm_p[2*l],norm_p[2*l+1]) for l in range(2)]
    qmu=[jnp.dot(left_t[l],mu[l][:,None],precision=highest) for l in range(2)]
    targets=(labels[:,None]==jnp.arange(CLASSES,dtype=jnp.int32)[None,:]).astype(F32)
    conv_one,msg1,hid1=forward(stem_out,parts0,norm_p[0:2],w_all,0,None,pixels,side)
    parts1=exchange(msg1)
    hq1,a_one=turn(hid1,left_t[0],qmu[0],1.0/pixels)
    residual,msg2,hid2=forward(conv_one,after(parts1,a_one),norm_p[2:4],w_all,1,stem_out,pixels,side)
    parts2=exchange(msg2)
    hq2,a_two=turn(hid2,left_t[1],qmu[1],1.0/pixels)
    wsum=jnp.sum(parts0[:,0:1,c:c+1],axis=0)
    g,msg3,head_g,loss=head(residual,after(parts2,a_two),norm_p[4:6],head_w.T,head_w[c:c+1],targets,weights[:,None],wsum,pixels,side)
    parts3=exchange(msg3)
    du1,msg4,backtwo=back_two(residual,g,parts2,parts3,norm_p[4:6],conv_one,parts1,norm_p[2:4],w_all,pixels,side)
    parts4=exchange(msg4)
    gw_two,ones_two,g_two=weight_two(backtwo,hq2,side,float(pixels))
    two,step,rounds=scatter_rounds(gw_two.reshape(devices,own,9*c),devices)
    two=step(two,0)
    backone,gw_one,ones_one,g_one=weight_one(conv_one,du1,parts1,after(parts4,ones_two),norm_p[2:4],hq1,pixels,side,float(pixels))
    one,step,_=scatter_rounds(gw_one.reshape(devices,own,9*c),devices)
    first=jnp.concatenate([step(one,0),two],axis=-1)
    stem_sums=back_one(after(backone,first),w_all,stem_out,parts0,norm_p[0:2],backtwo,pt,pixels,side)
    where=jnp.reshape(me,(1,)).astype(jnp.int32)
    keep,send=pack(where,a_one,g_one,a_two,g_two,head_g,loss,gram,ones_one,ones_two,stem_sums,devices)
    both=after(step(first,1),keep)
    same=exchange_chips(add_pieces(exchange_chips(keep+swap(send,1,devices))))
    other=swap(same,1,devices)
    for order in range(2,rounds): both=step(both,order)
    both=both.reshape(own,18*c)
    inverse,factors,damped=inverses(where,same,other,4)
    consts=(BETA_ONE,BETA_TWO,1.0-BETA_ONE**STEP,1.0-BETA_TWO**STEP,ADAM_EPS)
    q_own=jnp.stack([lax.dynamic_slice_in_dim(qmu[l],me*own,own,0) for l in range(2)])
    m_new,v_new,half=move(where,after(both,inverse),same,other,q_own,rot_bases,conv_m,conv_v,consts)
    near,far_half,bases_new=gather_near_and_far(half,lambda held: new_bases(after(damped,held),rot_bases))
    rows=lax.dynamic_slice_in_dim(rot_bases,me*own,own,1)[0::2]
    conv_new,conv_low=finish(where,near.reshape(c//2,18*c),far_half.reshape(c//2,18*c),rows,conv_w,RATE_CONV,WEIGHT_DECAY)
    small=small_updates(where,same,other,parts0,parts3,parts4,(stem_w,stem_m,stem_v),(head_w.T,head_m.T,head_v.T),(norm_p,norm_m,norm_v),pixels,consts,(RATE_STEM,WEIGHT_DECAY,RATE_HEAD,WEIGHT_DECAY,RATE_NORM))
    return (small[0][0,0:2],factors,inverse,conv_new,m_new,v_new,bases_new,small[1],small[2],small[3],small[4].T,small[5].T,small[6].T,small[7],small[8],small[9],conv_low)

def solution(mesh):
    one=P("dp",None)
    return jax.shard_map(local,mesh=mesh,in_specs=(P("dp",None,None,None),P("dp"),P("dp"),one,one,one)+(P(),)*10,out_specs=(P(),one,one,one,one,one)+(P(),)*10+(one,),check_vma=False)
```

```python
import functools
import math

import jax
import jax.numpy as jnp
from jax import lax
from jax.experimental import pallas as pl
from jax.experimental.pallas import tpu as pltpu
from jax.sharding import PartitionSpec as P

NS_ITERS=6; DAMPING=0.1
highest=HI=lax.Precision.HIGHEST
def dotp(a,b,dims=((1,),(0,)),prec=HI):
    return lax.dot_general(a,b,(dims,((),())),precision=prec,preferred_element_type=jnp.float32)
def split(a):
    hi=a.astype(jnp.bfloat16)
    return hi,(a-hi.astype(jnp.float32)).astype(jnp.bfloat16)
def dot3(a,b,dims=((1,),(0,))):
    ah,al=split(a); bh,bl=split(b)
    d=lambda x,y: lax.dot_general(x,y,(dims,((),())),preferred_element_type=jnp.float32)
    return d(ah,bh)+(d(ah,bl)+d(al,bh))
def inverse_kernel(me_ref,same_ref,other_ref,inv_ref,fac_ref,m_ref,p_ref,x_ref):
    chips,height,n=same_ref.shape
    devices=2*chips
    own=n//devices
    M4=4
    me=me_ref[0]
    r=lax.broadcasted_iota(jnp.int32,(n,n),0); c=lax.broadcasted_iota(jnp.int32,(n,n),1)
    eye=(r==c).astype(jnp.float32)
    each=height-2*own
    Fs=[]
    for k in range(2):
        for j in range(devices): p_ref[j*own:(j+1)*own,:]=piece_of(me_ref,same_ref,other_ref,j,slice(k*own,(k+1)*own))
        P=p_ref[...]
        Pt=P.T
        place=2*own+(DIAG+k)%each
        diag=piece_of(me_ref,same_ref,other_ref,(DIAG+k)//each,slice(place,place+1))
        Fs.append(jnp.where(r<=c,P,Pt))
        Fs.append(jnp.where(r==c,diag,jnp.where(r>c,P,Pt)))
    start=pl.multiple_of(me*own,own)
    def own_rows(out_ref, which):
        for m in which:
            rows=x_ref[m,pl.ds(start,own),:]
            for i in range(own): out_ref[M4*i+m:M4*i+m+1,:]=rows[i:i+1,:]
    Ms=[]
    for m in range(M4):
        F=Fs[m]
        tr=jnp.sum(F*eye)
        M=F+(DAMPING*tr/n)*eye
        Ms.append(M)
        m_ref[m]=M
        x_ref[m]=F
    own_rows(fac_ref,range(M4))
    inv_ref[...]=jnp.zeros(inv_ref.shape,jnp.float32)
    iterate(Ms,x_ref,range(M4//2),eye)
    own_rows(inv_ref,range(M4//2))

def iterate(Ms, x_ref, which, eye):
    Xs=[eye*lax.rsqrt(jnp.sum(Ms[m]*Ms[m])) for m in which]
    for _ in range(NS_ITERS):
        products=[dot3(X,Ms[m]) for X,m in zip(Xs,which)]
        Xs=[2.0*X-dot3(p,X) for p,X in zip(products,Xs)]
    for m,X in zip(which,Xs): x_ref[m]=X

def more_inverses_kernel(me_ref,part_ref,m_ref,inv_ref,x_ref):
    M4,n,_=m_ref.shape
    own=part_ref.shape[0]//M4
    r=lax.broadcasted_iota(jnp.int32,(n,n),0); c=lax.broadcasted_iota(jnp.int32,(n,n),1)
    which=range(M4//2,M4)
    iterate([m_ref[m] for m in range(M4)],x_ref,which,(r==c).astype(jnp.float32))
    inv_ref[...]=part_ref[...]
    start=pl.multiple_of(me_ref[0]*own,own)
    for m in which:
        rows=x_ref[m,pl.ds(start,own),:]
        for i in range(own): inv_ref[M4*i+m:M4*i+m+1,:]=rows[i:i+1,:]

def more_inverses(me,part,damped):
    return pl.pallas_call(more_inverses_kernel,out_shape=jax.ShapeDtypeStruct(part.shape,jnp.float32),
        in_specs=[pl.BlockSpec(memory_space=pltpu.SMEM)]+[pl.BlockSpec(memory_space=pltpu.VMEM)]*2,
        scratch_shapes=[pltpu.VMEM(damped.shape,jnp.float32)],
        compiler_params=pltpu.CompilerParams(vmem_limit_bytes=48*2**20),
        cost_estimate=takes(3.5),name="more_inverses")(me,part,damped)

def inverses(me,same,other,m4):
    chips,_,n=same.shape
    own=n//(2*chips)
    return pl.pallas_call(inverse_kernel,
        out_shape=(jax.ShapeDtypeStruct((m4*own,n),jnp.float32),jax.ShapeDtypeStruct((m4*own,n),jnp.float32),jax.ShapeDtypeStruct((m4,n,n),jnp.float32)),
        in_specs=[pl.BlockSpec(memory_space=pltpu.SMEM)]+[pl.BlockSpec(memory_space=pltpu.VMEM)]*2,
        scratch_shapes=[pltpu.VMEM((n,n),jnp.float32),pltpu.VMEM((m4,n,n),jnp.float32)],
        compiler_params=pltpu.CompilerParams(vmem_limit_bytes=48*2**20),
        cost_estimate=takes(4.0),name="damped_inverses")(me,same,other)

def sub(row, like):
    return jnp.broadcast_to(row,like.shape)

def bases_kernel(m_ref,q_ref,qn_ref,b_ref):
    M4,n,_=m_ref.shape
    nb=64
    for m in range(M4):
        Yt=dotp(q_ref[m],m_ref[m],((0,),(0,)))
        b_ref[m,:,n:]=Yt
        b_ref[m,:,:n]=dotp(Yt,Yt,((1,),(1,)))
    li=lax.broadcasted_iota(jnp.int32,(8,128),1); si=lax.broadcasted_iota(jnp.int32,(8,128),0)
    tiles=nb//8
    for k in range(n//nb):
        lo=k*nb; t0=(lo//128)*128; off=lo-t0
        V=[]
        for m in range(M4):
            D=b_ref[m,lo:lo+nb,t0:t0+128]
            if off: D=pltpu.roll(D,128-off,1)
            V.append([jnp.where(li<nb,D[8*i:8*i+8],jnp.where(li-nb==si+8*i,1.0,0.0)) for i in range(tiles)])
        rows=[[None]*tiles for _ in range(M4)]
        for b in range(tiles):
            pivots=[[jnp.broadcast_to(V[m][b][:,8*b+j:8*b+j+1],(8,128)) for j in range(8)] for m in range(M4)]
            below=[[[jnp.broadcast_to(V[m][i][:,8*b+j:8*b+j+1],(8,128)) for j in range(8)] for i in range(b+1,tiles)] for m in range(M4)]
            R=[V[m][b] for m in range(M4)]
            kept=[R[m] for m in range(M4)]
            size=[pivots[m][0] for m in range(M4)]
            for j in range(8):
                for m in range(M4):
                    col=pivots[m][j]
                    d=sub(col[j:j+1],col)
                    at=si==j
                    kept[m]=jnp.where(at,R[m],kept[m])
                    size[m]=jnp.where(at,d,size[m])
                    inv=1.0/d
                    rj=sub(R[m][j:j+1],R[m])*inv
                    for q in range(j+1,8):
                        pj=sub(pivots[m][q][j:j+1],col)*inv
                        pivots[m][q]=jnp.where(at,pj,pivots[m][q]-col*pj)
                    R[m]=jnp.where(at,rj,R[m]-col*rj)
            for m in range(M4):
                rows[m][b]=kept[m]*lax.rsqrt(size[m])
                spread=[sub(R[m][j:j+1],R[m]) for j in range(8)]
                for i in range(b+1,tiles):
                    cols=below[m][i-b-1]
                    terms=[cols[j]*spread[j] for j in range(8)]
                    while len(terms)>1: terms=[terms[z]+terms[z+1] for z in range(0,len(terms),2)]
                    V[m][i]=V[m][i]-terms[0]
        for m in range(M4):
            E=jnp.concatenate(rows[m],axis=0)[:,nb:2*nb]
            U=dotp(E,b_ref[m,lo:lo+nb,t0:])
            b_ref[m,lo:lo+nb,n:]=U[:,n-t0:]
            if lo+nb<n:
                t1=((lo+nb)//128)*128
                b_ref[m,lo+nb:,t1:]=b_ref[m,lo+nb:,t1:]-dotp(U[:,lo+nb-t0:n-t0],U[:,t1-t0:],((0,),(0,)))
    for m in range(M4):
        qn_ref[m]=b_ref[m,:,n:].T

def new_bases(damped,Q):
    m,n,_=Q.shape
    return pl.pallas_call(bases_kernel,
        out_shape=jax.ShapeDtypeStruct((m,n,n),jnp.float32),
        scratch_shapes=[pltpu.VMEM((m,n,2*n),jnp.float32)],
        compiler_params=pltpu.CompilerParams(vmem_limit_bytes=48*2**20),
        cost_estimate=takes(30.0),name="new_bases")(damped,Q)

EPS_NORM=1e-5
BF=jnp.bfloat16; F32=jnp.float32
MSG=384
ROOT=math.sqrt(2.0/math.pi)
def takes(micros):
    return pl.CostEstimate(flops=int(micros*1.0e9),bytes_accessed=int(micros*3.0e6),transcendentals=0)

def hold(x):
    return pltpu.with_memory_space_constraint(x,pltpu.HBM)

def far(shape,dtype):
    return pltpu.HBM(shape,dtype)

PARAMS=pltpu.CompilerParams(vmem_limit_bytes=48*2**20)

def mm(a,b,dims=((1,),(0,))):
    return lax.dot_general(a,b,(dims,((),())),preferred_element_type=F32)

def gelu_parts(x, need_value=True, need_slope=False):
    sq=x*x
    t=jnp.tanh(x*(ROOT+(ROOT*0.044715)*sq))
    half=0.5+0.5*t
    value=x*half if need_value else None
    slope=None
    if need_slope:
        slope=half+(0.5*x)*(1.0-t*t)*(ROOT+(3.0*ROOT*0.044715)*sq)
    return value,slope

def fold_norm(sums, gain, shift, pixels):
    mean=sums[0:1]/pixels
    var=sums[1:2]/pixels-mean*mean
    inv=lax.rsqrt(var+EPS_NORM)
    return mean,inv,gain*inv,shift-mean*(gain*inv)

def shift_taps(v, side):
    col=lax.broadcasted_iota(jnp.int32,v.shape,0)%side
    n=v.shape[0]
    left=jnp.where(col==0,0.0,pltpu.roll(v,1,0))
    right=jnp.where(col==side-1,0.0,pltpu.roll(v,n-1,0))
    return left,right

def clear_borders(p3, side):
    b,rows,w=p3.shape
    for i in range(b):
        p3[i,0:side,:]=jnp.zeros((side,w),BF)
        p3[i,rows-side:rows,:]=jnp.zeros((side,w),BF)

def put_taps(p3, i, v, side):
    n,c=v.shape
    left,right=shift_taps(v,side)
    p3[i,side:side+n,0:c]=left.astype(BF)
    p3[i,side:side+n,c:2*c]=v.astype(BF)
    p3[i,side:side+n,2*c:3*c]=right.astype(BF)

def tap_dots(p3, w_ref, i, n, side, c, back):
    acc=None
    for a in range(3):
        for b in range(3):
            t=3*a+b
            lhs=p3[i,side*a:side*a+n,b*c:(b+1)*c]
            tt=8-t if back else t
            w=w_ref[:,tt*c:(tt+1)*c]
            d=mm(lhs,w,((1,),(1,)) if back else ((1,),(0,)))
            acc=d if acc is None else acc+d
    return acc

def fold8(v):
    n,c=v.shape
    return jnp.sum(v.reshape(n//8,8,c),axis=0)

def send_sums(out_ref, s0, s1, extra=None):
    n=out_ref.shape[0]
    rows=jnp.concatenate([jnp.sum(s0,axis=0,keepdims=True),jnp.sum(s1,axis=0,keepdims=True)],axis=0)
    tail=jnp.zeros((2,MSG-rows.shape[1]),F32) if extra is None else extra
    msg=jnp.concatenate([rows,tail],axis=1)
    out_ref[...]=jnp.broadcast_to(msg[None],out_ref.shape)

def fwd_kernel(x_ref,parts_ref,norm_ref,w_ref,*rest,pixels,side,residual):
    if residual: stem_ref,y_ref,msg_ref,h_ref,p3=rest
    else: y_ref,msg_ref,h_ref,p3=rest
    images,n,_=p3.shape
    n-=2*side
    c=x_ref.shape[1]
    sums=jnp.sum(parts_ref[...],axis=0)[:,:c]
    _,_,scale,offset=fold_norm(sums,norm_ref[0:1],norm_ref[1:2],pixels)
    clear_borders(p3,side)
    def prep(i):
        v=x_ref[i*n:(i+1)*n,:]*scale+offset
        h,_=gelu_parts(v)
        put_taps(p3,i,h,side)
        h_ref[i*n:(i+1)*n,:]=h.astype(BF)
    s0=jnp.zeros((8,c),F32); s1=jnp.zeros((8,c),F32)
    prep(0)
    for i in range(images):
        if i+1<images: prep(i+1)
        y=tap_dots(p3,w_ref,i,n,side,c,False)
        if residual: y=y+stem_ref[i*n:(i+1)*n,:]
        y_ref[i*n:(i+1)*n,:]=y
        s0=s0+fold8(y); s1=s1+fold8(y*y)
    send_sums(msg_ref,s0,s1)

def layer_spec(w,layer):
    c=w.shape[0]
    return pl.BlockSpec((c,9*c),lambda i: (0,layer))

VMEM_SPEC=pl.BlockSpec(memory_space=pltpu.VMEM)

def forward(x,parts,norm,w,layer,stem,pixels,side):
    rows,c=x.shape
    n=side*side
    images=rows//n
    dev=parts.shape[0]
    args=(hold(x),parts,norm,w)+((hold(stem),) if stem is not None else ())
    return pl.pallas_call(functools.partial(fwd_kernel,pixels=pixels,side=side,residual=stem is not None),
        out_shape=(far((rows,c),F32),jax.ShapeDtypeStruct((dev,2,MSG),F32),far((rows,c),BF)),
        grid=(1,),in_specs=[VMEM_SPEC]*3+[layer_spec(w,layer)]+[VMEM_SPEC]*(len(args)-4),
        scratch_shapes=[pltpu.VMEM((images,n+2*side,3*c),BF)],
        compiler_params=PARAMS,cost_estimate=takes(7.5),name="conv_forward")(*args)

def stem_kernel(x_ref,w_ref,wt_ref,y_ref,msg_ref,pt_ref,gram_ref,pt,*,side,images):
    n=side*side
    c=w_ref.shape[1]
    x=x_ref[...]
    lane=lax.broadcasted_iota(jnp.int32,x.shape,1)
    row,col=lane//side,lane%side
    pt[...]=jnp.zeros(pt.shape,F32)
    for a in range(3):
        for b in range(3):
            off=(a-1)*side+(b-1)
            v=pltpu.roll(x,(-off)%n,1) if off else x
            ok=None
            if a==0: ok=row>0
            if a==2: ok=row<side-1
            if b==0: ok=(col>0) if ok is None else ok&(col>0)
            if b==2: ok=(col<side-1) if ok is None else ok&(col<side-1)
            if ok is not None: v=jnp.where(ok,v,0.0)
            t=3*a+b
            for i in range(images):
                pt[i,3*t:3*t+3,:]=v[3*i:3*i+3,:]
    w=jnp.concatenate([w_ref[...],jnp.zeros((pt.shape[1]-w_ref.shape[0],c),F32)],axis=0).astype(BF)
    s0=jnp.zeros((8,c),F32); s1=jnp.zeros((8,c),F32)
    sub=lax.broadcasted_iota(jnp.int32,(pt.shape[1],n),0)
    for i in range(images):
        p=pt[i]
        y=mm(p.astype(BF),w,((0,),(0,)))
        y_ref[i*n:(i+1)*n,:]=y
        pt_ref[:,i*n:(i+1)*n]=jnp.where(sub==w_ref.shape[0],1.0,p).astype(BF)
        s0=s0+fold8(y); s1=s1+fold8(y*y)
    send_sums(msg_ref,s0,s1,jnp.broadcast_to(jnp.sum(wt_ref[...]),(2,MSG-c)))
    taps=pt_ref[...]
    gram_ref[...]=mm(taps,taps,((1,),(1,)))

def stem(x,w,weights,devices,side):
    images=x.shape[0]//3
    n=side*side
    rows,c=images*n,w.shape[1]
    taps=(w.shape[0]+1+15)//16*16
    return pl.pallas_call(functools.partial(stem_kernel,side=side,images=images),
        out_shape=(far((rows,c),F32),jax.ShapeDtypeStruct((devices,2,MSG),F32),far((taps,rows),BF),far((taps,taps),F32)),
        scratch_shapes=[pltpu.VMEM((images,taps,n),F32)],
        compiler_params=PARAMS,cost_estimate=takes(1.5),name="stem_forward")(x,w,weights)

def head_kernel(x_ref,parts_ref,norm_ref,ht_ref,bias_ref,tg_ref,wt_ref,wsum_ref,g_ref,msg_ref,hg_ref,loss_ref,pool,sl0,sl1,*,pixels,side):
    n=side*side
    rows,c=x_ref.shape
    images=rows//n
    sums=jnp.sum(parts_ref[...],axis=0)[:,:c]
    mean,inv,scale,offset=fold_norm(sums,norm_ref[0:1],norm_ref[1:2],pixels)
    for i in range(images):
        v=x_ref[i*n:(i+1)*n,:]
        f,gp=gelu_parts(v*scale+offset,True,True)
        pool[i:i+1,:]=jnp.sum(fold8(f),axis=0,keepdims=True)*(1.0/n)
        sl0[i:i+1,:]=jnp.sum(fold8(gp),axis=0,keepdims=True)
        sl1[i:i+1,:]=jnp.sum(fold8(gp*((v-mean)*inv)),axis=0,keepdims=True)
    pooled=pool[0:images,:]
    low=pooled.astype(BF)
    head=ht_ref[:,0:c].astype(BF)
    logits=mm(low,head,((1,),(1,)))+bias_ref[...]
    spread=jnp.sum(pooled*pooled,axis=1,keepdims=True)/c
    k=math.pi/8.0
    shrink=lax.rsqrt(1.0+k*spread)
    scaled=logits*shrink
    top=jnp.max(scaled,axis=1,keepdims=True)
    ex=jnp.exp(scaled-top)
    tot=jnp.sum(ex,axis=1,keepdims=True)
    logtot=top+jnp.log(tot)
    wt=wt_ref[...]
    tg=tg_ref[...]
    loss_ref[...]=jnp.broadcast_to(jnp.sum(wt*(logtot-jnp.sum(scaled*tg,axis=1,keepdims=True))),loss_ref.shape)
    gs=(jnp.exp(scaled-logtot)-tg)*(wt/wsum_ref[0:1,0:1])
    gl=(gs*shrink).astype(BF)
    gsh=jnp.sum(gs*logits,axis=1,keepdims=True)
    gspread=gsh*(-0.5*k)*shrink*shrink*shrink
    gp=mm(gl,head)+gspread*(2.0/c)*pooled
    g=gp*(1.0/n)
    g_ref[0:images,:]=g
    s0=g*sl0[0:images,:]; s1=g*sl1[0:images,:]
    send_sums(msg_ref,s0,s1)
    hg_ref[:,0:c]=mm(gl,low,((0,),(0,)))
    ones=jnp.ones((images,128),BF)
    hg_ref[:,c:]=mm(gl,ones,((0,),(0,)))

def head(x,parts,norm,head_t,bias,targets,weights,wsum,pixels,side):
    rows,c=x.shape
    images=rows//(side*side)
    dev=parts.shape[0]
    cls=bias.shape[1]
    pad=(images+7)//8*8
    return pl.pallas_call(functools.partial(head_kernel,pixels=pixels,side=side),
        out_shape=(far((pad,c),F32),jax.ShapeDtypeStruct((dev,2,MSG),F32),jax.ShapeDtypeStruct((cls,c+128),F32),jax.ShapeDtypeStruct((1,128),F32)),
        scratch_shapes=[pltpu.VMEM((pad,c),F32)]*3,
        compiler_params=PARAMS,cost_estimate=takes(5.1),name="head_loss")(hold(x),parts,norm,head_t,bias,targets,weights,wsum)

def read_sums(ref,c):
    return jnp.sum(ref[...],axis=0)[:,:c]

def back_two_kernel(res_ref,g_ref,ps_ref,pg_ref,na_ref,one_ref,p1_ref,nb_ref,w_ref,du_ref,msg_ref,back_ref,p3,*,pixels,side):
    n=side*side
    rows,c=res_ref.shape
    images=rows//n
    mean2,inv2,scale2,offset2=fold_norm(read_sums(ps_ref,c),na_ref[0:1],na_ref[1:2],pixels)
    gs=read_sums(pg_ref,c)
    k0=scale2*gs[0:1]*(1.0/pixels); k1=scale2*inv2*gs[1:2]*(1.0/pixels)
    base=k1*mean2-k0
    mean1,inv1,scale1,offset1=fold_norm(read_sums(p1_ref,c),nb_ref[0:1],nb_ref[1:2],pixels)
    clear_borders(p3,side)
    def prep(i):
        sl=slice(i*n,(i+1)*n)
        r=res_ref[sl,:]
        _,slope=gelu_parts(r*scale2+offset2,False,True)
        d=slope*(scale2*g_ref[i:i+1,:])-r*k1+base
        back_ref[sl,:]=d.astype(BF)
        put_taps(p3,i,d,side)
    s0=jnp.zeros((8,c),F32); s1=jnp.zeros((8,c),F32)
    prep(0)
    for i in range(images):
        if i+1<images: prep(i+1)
        sl=slice(i*n,(i+1)*n)
        gh=tap_dots(p3,w_ref,i,n,side,c,True)
        v=one_ref[sl,:]
        _,gp=gelu_parts(v*scale1+offset1,False,True)
        du=gp*gh
        du_ref[sl,:]=du
        s0=s0+fold8(du); s1=s1+fold8(du*((v-mean1)*inv1))
    send_sums(msg_ref,s0,s1)

def back_two(res,g,parts_stat,parts_grad,norm_a,conv_one,parts_one,norm_b,w,pixels,side):
    rows,c=res.shape
    n=side*side
    images=rows//n
    dev=parts_stat.shape[0]
    return pl.pallas_call(functools.partial(back_two_kernel,pixels=pixels,side=side),
        out_shape=(far((rows,c),F32),jax.ShapeDtypeStruct((dev,2,MSG),F32),far((rows,c),BF)),
        grid=(1,),in_specs=[VMEM_SPEC]*8+[layer_spec(w,1)],
        scratch_shapes=[pltpu.VMEM((images,n+2*side,3*c),BF)],
        compiler_params=PARAMS,cost_estimate=takes(9.0),name="back_two")(hold(res),g,parts_stat,parts_grad,norm_a,hold(conv_one),parts_one,norm_b,w)

def turn_kernel(h_ref,qt_ref,qm_ref,hq_ref,a_ref,*,scale):
    c=h_ref.shape[1]
    h=h_ref[...]
    q=qt_ref[...]
    qh=q.astype(BF); ql=(q-qh.astype(F32)).astype(BF)
    hq_ref[0:c,:]=(mm(qh,h,((1,),(1,)))+mm(ql,h,((1,),(1,)))-qm_ref[:,0:1]).astype(BF)
    extra=hq_ref.shape[0]-c
    sub=lax.broadcasted_iota(jnp.int32,(extra,h.shape[0]),0)
    hq_ref[c:,:]=jnp.where(sub==0,1.0,0.0).astype(BF)
    a_ref[...]=mm(h,h,((0,),(0,)))*scale

def turn(h,qt,qmu,scale):
    rows,c=h.shape
    return pl.pallas_call(functools.partial(turn_kernel,scale=scale),
        out_shape=(far((c+16,rows),BF),far((c,c),F32)),
        compiler_params=PARAMS,cost_estimate=takes(1.3),name="turn_hidden")(hold(h),qt,qmu)

def weight_dots(p3,hq_ref,gw_ref,ones_ref,gf_ref,side,scale):
    images,rows,w=p3.shape
    n=rows-2*side
    c=w//3
    hq=hq_ref[...]
    for a in range(3):
        for b in range(3):
            t=8-(3*a+b)
            rhs=p3[:,side*a:side*a+n,b*c:(b+1)*c].reshape(images*n,c)
            d=mm(hq,rhs)
            gw_ref[:,t*c:(t+1)*c]=d[0:c].astype(gw_ref.dtype)
            ones_ref[:,t*c:(t+1)*c]=d[c:c+8]
    mid=p3[:,side:side+n,c:2*c].reshape(images*n,c)
    gf_ref[...]=mm(mid,mid,((0,),(0,)))*scale

def fill_taps(p3,values,side):
    images,rows,_=p3.shape
    n=rows-2*side
    clear_borders(p3,side)
    for i in range(images): put_taps(p3,i,values(slice(i*n,(i+1)*n)),side)

def weight_two_kernel(back_ref,hq_ref,gw_ref,ones_ref,gf_ref,p3,*,side,scale):
    fill_taps(p3,lambda sl: back_ref[sl,:].astype(F32),side)
    weight_dots(p3,hq_ref,gw_ref,ones_ref,gf_ref,side,scale)

def weight_shapes(c,dt):
    return (jax.ShapeDtypeStruct((c,9*c),dt),jax.ShapeDtypeStruct((8,9*c),F32),far((c,c),F32))

def taps_buffer(rows,c,side):
    n=side*side
    return pltpu.VMEM((rows//n,n+2*side,3*c),BF)

def weight_two(back,hq,side,scale,dt=BF):
    rows,c=back.shape
    return pl.pallas_call(functools.partial(weight_two_kernel,side=side,scale=scale),
        out_shape=weight_shapes(c,dt),scratch_shapes=[taps_buffer(rows,c,side)],
        compiler_params=PARAMS,cost_estimate=takes(6.0),name="weight_two")(hold(back),hold(hq))

def weight_one_kernel(one_ref,du_ref,p1_ref,pg_ref,nb_ref,hq_ref,back_ref,gw_ref,ones_ref,gf_ref,p3,*,pixels,side,scale):
    n=side*side
    rows,c=one_ref.shape
    images=rows//n
    mean1,inv1,scale1,_=fold_norm(read_sums(p1_ref,c),nb_ref[0:1],nb_ref[1:2],pixels)
    gs=read_sums(pg_ref,c)
    k0=scale1*gs[0:1]*(1.0/pixels); k1=scale1*inv1*gs[1:2]*(1.0/pixels)
    base=k1*mean1-k0
    def values(sl):
        d=du_ref[sl,:]*scale1-one_ref[sl,:]*k1+base
        back_ref[sl,:]=d.astype(BF)
        return d
    fill_taps(p3,values,side)
    weight_dots(p3,hq_ref,gw_ref,ones_ref,gf_ref,side,scale)

def weight_one(conv_one,du,parts_one,parts_grad,norm_b,hq,pixels,side,scale,dt=BF):
    rows,c=conv_one.shape
    n=side*side
    images=rows//n
    return pl.pallas_call(functools.partial(weight_one_kernel,pixels=pixels,side=side,scale=scale),
        out_shape=(far((rows,c),BF),)+weight_shapes(c,dt),scratch_shapes=[taps_buffer(rows,c,side)],
        compiler_params=PARAMS,cost_estimate=takes(6.4),name="weight_one")(hold(conv_one),hold(du),parts_one,parts_grad,norm_b,hold(hq))

def back_one_kernel(back_ref,w_ref,stem_ref,p0_ref,n0_ref,dres_ref,pt_ref,ps_ref,p3,*,pixels,side):
    images,rows,w3=p3.shape
    n=rows-2*side
    c=w3//3
    mean0,inv0,scale0,offset0=fold_norm(read_sums(p0_ref,c),n0_ref[0:1],n0_ref[1:2],pixels)
    taps=pt_ref.shape[0]
    s0=jnp.zeros((8,c),F32); s1=jnp.zeros((8,c),F32)
    acc=jnp.zeros((taps,c),F32)
    clear_borders(p3,side)
    def prep(i): put_taps(p3,i,back_ref[i*n:(i+1)*n,:].astype(F32),side)
    prep(0)
    for i in range(images):
        if i+1<images: prep(i+1)
        sl=slice(i*n,(i+1)*n)
        gh=tap_dots(p3,w_ref,i,n,side,c,True)
        v=stem_ref[sl,:]
        _,gp=gelu_parts(v*scale0+offset0,False,True)
        du=gp*gh
        s0=s0+fold8(du); s1=s1+fold8(du*((v-mean0)*inv0))
        z=du*scale0+dres_ref[sl,:].astype(F32)
        zh=z.astype(BF); zl=(z-zh.astype(F32)).astype(BF)
        p=pt_ref[:,sl]
        acc=acc+mm(p,zh)+mm(p,zl)
    ps_ref[0:taps,:]=acc
    ps_ref[taps:taps+1,:]=jnp.sum(s0,axis=0,keepdims=True)
    ps_ref[taps+1:taps+2,:]=jnp.sum(s1,axis=0,keepdims=True)
    ps_ref[taps+2:,:]=jnp.zeros((ps_ref.shape[0]-taps-2,c),F32)

def back_one(back,w,stem_out,parts0,norm0,dres,pt,pixels,side):
    rows,c=back.shape
    taps=pt.shape[0]
    return pl.pallas_call(functools.partial(back_one_kernel,pixels=pixels,side=side),
        out_shape=jax.ShapeDtypeStruct((taps+8,c),F32),
        grid=(1,),in_specs=[VMEM_SPEC]+[layer_spec(w,0)]+[VMEM_SPEC]*5,
        scratch_shapes=[taps_buffer(rows,c,side)],
        compiler_params=PARAMS,cost_estimate=takes(8.0),name="back_one")(hold(back),w,hold(stem_out),parts0,norm0,hold(dres),hold(pt))

DIAG,HEAD,BORDER,SIDE,STEM,SMALL=0,2,12,32,64,128

def pack_kernel(me_ref,a1_ref,g1_ref,a2_ref,g2_ref,hg_ref,loss_ref,gram_ref,b1_ref,b2_ref,ss_ref,keep_ref,send_ref,small):
    chips,rows,c=keep_ref.shape
    own=c//(2*chips)
    even=(me_ref[0]&1)==0
    def put(i, at, first, second):
        keep_ref[i,at,:]=jnp.where(even,first,second)
        send_ref[i,at,:]=jnp.where(even,second,first)
    r=lax.broadcasted_iota(jnp.int32,(c,c),0); l=lax.broadcasted_iota(jnp.int32,(c,c),1)
    small[...]=jnp.zeros(small.shape,F32)
    for k,(a_ref,g_ref) in enumerate(((a1_ref,g1_ref),(a2_ref,g2_ref))):
        g=g_ref[...]
        both=jnp.where(r<=l,a_ref[...],g)
        small[DIAG+k:DIAG+k+1,:]=jnp.sum(jnp.where(r==l,g,0.0),axis=0,keepdims=True)
        for i in range(chips): put(i,slice(k*own,(k+1)*own),both[2*i*own:(2*i+1)*own],both[(2*i+1)*own:(2*i+2)*own])
    cls=hg_ref.shape[0]
    small[HEAD:HEAD+cls,:]=hg_ref[:,0:c]
    small[STEM:STEM+ss_ref.shape[0],:]=ss_ref[...]
    small[SIDE:SIDE+gram_ref.shape[0],0:gram_ref.shape[1]]=gram_ref[...]
    small[SIDE:SIDE+cls,128:256]=hg_ref[:,c:c+128]
    small[SIDE+16:SIDE+17,128:256]=loss_ref[...]
    for k,b_ref in enumerate((b1_ref,b2_ref)):
        for t in range(9): small[BORDER+9*k+t:BORDER+9*k+t+1,:]=b_ref[0:1,t*c:(t+1)*c]
    each=rows-2*own
    for i in range(chips):
        at=2*i*each
        if at+2*each<=small.shape[0]: put(i,slice(2*own,rows),small[at:at+each,:],small[at+each:at+2*each,:])
        else:
            keep_ref[i,2*own:rows,:]=jnp.zeros((each,c),F32)
            send_ref[i,2*own:rows,:]=jnp.zeros((each,c),F32)

SMEM_SPEC=pl.BlockSpec(memory_space=pltpu.SMEM)

def pack(me,a1,g1,a2,g2,hg,loss,gram,b1,b2,ss,devices):
    c=a1.shape[0]
    rows=2*(c//devices)+-(-SMALL//devices)
    return pl.pallas_call(pack_kernel,out_shape=(jax.ShapeDtypeStruct((devices//2,rows,c),F32),)*2,
        in_specs=[SMEM_SPEC]+[VMEM_SPEC]*10,
        scratch_shapes=[pltpu.VMEM((SMALL,c),F32)],
        compiler_params=PARAMS,cost_estimate=takes(1.5),name="pack_sums")(me,hold(a1),hold(g1),hold(a2),hold(g2),hg,loss,gram,b1,b2,ss)

def add_kernel(got_ref,out_ref):
    t=got_ref[0]
    for j in range(1,got_ref.shape[0]): t=t+got_ref[j]
    for j in range(got_ref.shape[0]): out_ref[j]=t

def add_pieces(got):
    return pl.pallas_call(add_kernel,out_shape=jax.ShapeDtypeStruct(got.shape,F32),compiler_params=PARAMS,cost_estimate=takes(1.0),name="add_pieces")(got)

def piece_of(me_ref,same_ref,other_ref,j,at):
    return jnp.where((me_ref[0]&1)==(j&1),same_ref[j//2,at,:],other_ref[j//2,at,:])

def unpack_small(me_ref,same_ref,other_ref,small,own):
    chips,rows,c=same_ref.shape
    each=rows-2*own
    for j in range(min(2*chips,SMALL//each)): small[j*each:(j+1)*each,:]=piece_of(me_ref,same_ref,other_ref,j,slice(2*own,rows))

def adam_refs(p_ref,m_ref,v_ref,g,out,rate,decay,consts):
    beta1,beta2,fix1,fix2,eps=consts
    m=beta1*m_ref[...]+(1.0-beta1)*g
    v=beta2*v_ref[...]+(1.0-beta2)*g*g
    p=p_ref[...]
    out[0][...]=p-rate*((m/fix1)/(jnp.sqrt(v/fix2)+eps)+decay*p)
    out[1][...]=m
    out[2][...]=v

def small_kernel(me_ref,same_ref,other_ref,p0_ref,p3_ref,p4_ref,sw,sm,sv,hw,hm,hv,nw,nm,nv,loss_ref,so,smo,svo,ho,hmo,hvo,no,nmo,nvo,small,*,own,pixels,consts,rates):
    unpack_small(me_ref,same_ref,other_ref,small,own)
    c=sw.shape[1]
    rows=sw.shape[0]
    taps=(rows+1+15)//16*16
    st=small[STEM:STEM+taps+8,:]
    s00=st[taps:taps+1]; s01=st[taps+1:taps+2]
    mean0,inv0,scale0,_=fold_norm(read_sums(p0_ref,c),nw[0:1],nw[1:2],pixels)
    gram=small[SIDE:SIDE+taps,0:128]
    ones0=gram[0:rows,rows:rows+1]
    w=sw[...].astype(BF).astype(F32)
    w=jnp.concatenate([w,jnp.zeros((128-rows,c),F32)],axis=0)
    cross=lax.dot_general(gram[0:rows],w,(((1,),(0,)),((),())),precision=highest,preferred_element_type=F32)
    xs=inv0*(cross-ones0*mean0)
    grad=st[0:rows]-ones0*(scale0*s00/pixels)-xs*(scale0*s01/pixels)
    adam_refs(sw,sm,sv,grad,(so,smo,svo),rates[0],rates[1],consts)
    cls=hw.shape[0]
    hg=jnp.concatenate([small[HEAD:HEAD+cls,:],small[SIDE:SIDE+cls,128:129]],axis=1)
    adam_refs(hw,hm,hv,hg,(ho,hmo,hvo),rates[2],rates[3],consts)
    s3=read_sums(p3_ref,c); s4=read_sums(p4_ref,c)
    ng=jnp.concatenate([s01,s00,s4[1:2],s4[0:1],s3[1:2],s3[0:1]],axis=0)
    adam_refs(nw,nm,nv,ng,(no,nmo,nvo),rates[4],0.0,consts)
    wsum=jnp.sum(p0_ref[...],axis=0)[0:1,c:c+128]
    lane=lax.broadcasted_iota(jnp.int32,(1,128),1)
    loss_ref[...]=jnp.where(lane==0,small[SIDE+16:SIDE+17,128:256],wsum)

def small_updates(me,same,other,parts0,parts3,parts4,stem3,head3,norm3,pixels,consts,rates):
    c=stem3[0].shape[1]
    own=c//(2*same.shape[0])
    shapes=[jax.ShapeDtypeStruct((1,128),F32)]+[jax.ShapeDtypeStruct(x.shape,F32) for x in stem3+head3+norm3]
    return pl.pallas_call(functools.partial(small_kernel,own=own,pixels=pixels,consts=consts,rates=rates),out_shape=shapes,
        in_specs=[SMEM_SPEC]+[VMEM_SPEC]*(5+9),
        scratch_shapes=[pltpu.VMEM((SMALL,c),F32)],
        compiler_params=PARAMS,cost_estimate=takes(1.5),name="small_updates")(me,same,other,parts0,parts3,parts4,*stem3,*head3,*norm3)

def turn_rows(x, c, blocks):
    return jnp.concatenate([x[:,t*c:(t+1)*c] for t in range(blocks)],axis=0)

def to_halves(ref, halves):
    r=ref.shape[0]
    halves[0:r,:]=ref[:,0:128]
    halves[r:2*r,:]=ref[:,128:256]

def from_halves(halves, ref):
    r=ref.shape[0]
    ref[:,0:128]=halves[0:r,:].astype(ref.dtype)
    ref[:,128:256]=halves[r:2*r,:].astype(ref.dtype)

def pick_rows(halves, layer, own, blocks):
    r=halves.shape[0]//2
    sides=[jnp.concatenate([halves[pl.ds(h*r+layer*blocks+t,own,stride=2*blocks),:] for t in range(blocks)],axis=0) for h in range(2)]
    return jnp.concatenate(sides,axis=1)

def place_rows(halves, layer, own, blocks, v):
    r=halves.shape[0]//2
    for h in range(2):
        for t in range(blocks): halves[pl.ds(h*r+layer*blocks+t,own,stride=2*blocks),:]=v[t*own:(t+1)*own,h*128:(h+1)*128]

def move_kernel(me_ref,g_ref,same_ref,other_ref,qmu_ref,q_ref,m_ref,v_ref,mo_ref,vo_ref,send_ref,m_sc,v_sc,small,*,consts):
    beta1,beta2,fix1,fix2,eps=consts
    own,w=g_ref.shape
    w=w//2
    unpack_small(me_ref,same_ref,other_ref,small,own)
    to_halves(m_ref,m_sc)
    to_halves(v_ref,v_sc)
    c=q_ref.shape[1]
    blocks=w//c
    for l in range(2):
        b=jnp.concatenate([jnp.broadcast_to(small[BORDER+l*blocks+t:BORDER+l*blocks+t+1,:],(own,c)) for t in range(blocks)],axis=0)
        qm=jnp.concatenate([qmu_ref[l]]*blocks,axis=0)
        x=turn_rows(g_ref[:,l*w:(l+1)*w],c,blocks)+qm[:,0:1]*b
        rot=dot3(x,q_ref[2*l+1])
        m=beta1*pick_rows(m_sc,l,own,blocks)+(1.0-beta1)*rot
        v=beta2*pick_rows(v_sc,l,own,blocks)+(1.0-beta2)*rot*rot
        place_rows(m_sc,l,own,blocks,m)
        place_rows(v_sc,l,own,blocks,v)
        step=(m/fix1)/(jnp.sqrt(v/fix2)+eps)
        back=dot3(step,q_ref[2*l+1],((1,),(1,)))
        for t in range(blocks): send_ref[:,l*w+t*c:l*w+(t+1)*c]=back[t*own:(t+1)*own,:].astype(BF)
    from_halves(m_sc,mo_ref)
    from_halves(v_sc,vo_ref)

def move(me,g,same,other,qmu,bases,m,v,consts):
    own,w=g.shape
    return pl.pallas_call(functools.partial(move_kernel,consts=consts),
        out_shape=(jax.ShapeDtypeStruct(m.shape,F32),jax.ShapeDtypeStruct(m.shape,F32),jax.ShapeDtypeStruct((own,w),BF)),
        in_specs=[SMEM_SPEC]+[VMEM_SPEC]*7,
        scratch_shapes=[pltpu.VMEM((2*m.shape[0],128),F32)]*2+[pltpu.VMEM((SMALL,m.shape[1]),F32)],
        compiler_params=PARAMS,cost_estimate=takes(2.0),name="moments_and_direction")(me,g,same,other,qmu,bases,m,v)

def finish_kernel(me_ref,near_ref,far_ref,rows_ref,w_ref,out_ref,low_ref,w_sc,*,rate,decay):
    to_halves(w_ref,w_sc)
    count,width=near_ref.shape
    c=2*count
    half=width//2
    own=rows_ref.shape[1]
    blocks=half//c
    bits=own.bit_length()-1
    i=lax.broadcasted_iota(jnp.int32,(c,count),0)
    j=lax.broadcasted_iota(jnp.int32,(c,count),1)
    slot=2*lax.shift_right_logical(j,bits)
    picks=[(i==lax.shift_left((slot+core)^me_ref[0],bits)+(j&(own-1))).astype(BF) for core in range(2)]
    for l in range(2):
        q=rows_ref[l]
        qh=q.astype(BF); ql=(q-qh.astype(F32)).astype(BF)
        both=jnp.concatenate([qh,ql],axis=0)
        d=None
        for pick,part in zip(picks,(near_ref,far_ref)):
            e=mm(mm(both,pick).astype(BF),part[:,l*half:(l+1)*half])
            d=e if d is None else d+e
        d=d[0:own]+d[own:2*own]
        w=pick_rows(w_sc,l,own,blocks)
        place_rows(w_sc,l,own,blocks,w-rate*(turn_rows(d,c,blocks)+decay*w))
    from_halves(w_sc,out_ref)
    from_halves(w_sc,low_ref)

def finish(me,near,far,rows,w,rate,decay):
    return pl.pallas_call(functools.partial(finish_kernel,rate=rate,decay=decay),
        out_shape=(jax.ShapeDtypeStruct(w.shape,F32),jax.ShapeDtypeStruct(w.shape,BF)),
        in_specs=[pl.BlockSpec(memory_space=pltpu.SMEM)]+[VMEM_SPEC]*4,
        scratch_shapes=[pltpu.VMEM((2*w.shape[0],128),F32)],
        compiler_params=PARAMS,cost_estimate=takes(2.5),name="new_weights")(me,near,far,rows,w)

CLASSES=10
STEP=5
BETA_ONE=0.9
BETA_TWO=0.99
ADAM_EPS=1e-08
WEIGHT_DECAY=0.01
RATE_CONV=0.02
RATE_STEM=0.1
RATE_HEAD=0.1
RATE_NORM=0.5


def bit_groups(devices):
    total_bits=devices.bit_length()-1
    groups=[(0,1)]
    while groups[-1][0]+groups[-1][1]<total_bits:
        first=groups[-1][0]+groups[-1][1]
        groups.append((first,min(2,total_bits-first)))
    return groups

def swap(values, mask, devices):
    return lax.ppermute(values,"dp",[(i,i^mask) for i in range(devices)])

def exchange(pieces):
    return lax.all_to_all(pieces,"dp",0,0,tiled=True)

def gather_all(piece, first_wait=(), last_wait=()):
    devices=lax.axis_size("dp")
    me=lax.axis_index("dp")
    groups=bit_groups(devices)[::-1]
    held=piece[(None,)*len(groups)]
    for axis,(first,width) in enumerate(groups):
        radix=1<<width
        mine=(me>>first)&(radix-1)
        got=[held]+[swap(held,k<<first,devices) for k in range(1,radix)]
        ordered=[]
        for j in range(radix):
            value=got[j]
            for m in range(1,radix): value=jnp.where(mine==m,got[j^m],value)
            ordered.append(value)
        held=jnp.concatenate(ordered,axis=axis)
        if axis==0:
            held=after(held,*first_wait)
        if axis==len(groups)-2 and last_wait: held=after(held,*last_wait)
    return held.reshape((devices,)+piece.shape)

def gather_near_and_far(piece, between):
    devices=lax.axis_size("dp")
    groups=bit_groups(devices)[::-1]
    held=piece[(None,)*(len(groups)-1)]
    for axis,(first,width) in enumerate(groups[:-1]):
        held=jnp.concatenate([held]+[swap(held,k<<first,devices) for k in range(1,1<<width)],axis=axis)
        if axis==0: waited=between(held)
    held=held.reshape((devices//2,)+piece.shape)
    return held,swap(after(held,waited),1,devices),waited

def exchange_chips(pieces):
    devices=lax.axis_size("dp")
    groups=[[2*i+core for i in range(devices//2)] for core in range(2)]
    return lax.all_to_all(pieces,"dp",0,0,tiled=True,axis_index_groups=groups)

def scatter_rounds(pieces, devices):
    groups=bit_groups(devices)
    me=lax.axis_index("dp")
    held=pieces.reshape(tuple(1<<width for _,width in groups[::-1])+pieces.shape[1:])
    def step(held, order):
        first,width=groups[order]
        axis=len(groups)-1-order
        radix=1<<width
        mine=(me>>first)&(radix-1)
        parts=[lax.dynamic_slice_in_dim(held,mine^k,1,axis=axis) for k in range(radix)]
        total=parts[0].astype(F32)
        for k in range(1,radix):
            total=total+swap(parts[k].astype(BF),k<<first,devices).astype(F32)
        return total
    return held,step,len(groups)

def after(value, *earlier):
    return lax.optimization_barrier((value,)+earlier)[0]

def expected_gelu(gain, shift):
    spread=jnp.sqrt(1.0+gain*gain)
    at=shift/spread
    return shift*(0.5+0.5*lax.erf(at*math.sqrt(0.5)))+gain*gain/spread*jnp.exp(-0.5*at*at)*(1.0/math.sqrt(2.0*math.pi))

def local(images, labels, groups, conv_w, conv_m, conv_v, rot_bases, stem_w, stem_m, stem_v, head_w, head_m, head_v, norm_p, norm_m, norm_v):
    devices=lax.axis_size("dp")
    me=lax.axis_index("dp")
    count,side=images.shape[0],images.shape[1]
    c=conv_w.shape[1]
    pixels=count*side*side*devices
    own=c//devices
    packed=conv_w.reshape(own,18*c).astype(BF)
    weights=1.0+3.0*groups.astype(F32)
    x=images.transpose(0,3,1,2).reshape(3*count,side*side).astype(F32)
    stem_out,msg0,pt,gram=stem(x,stem_w,weights[None,:],devices,side)
    parts0=exchange(msg0)
    w_all=gather_all(packed,(msg0,),(parts0,)).reshape(c,18*c)
    left_t=rot_bases[0::2].transpose(0,2,1)
    mu=[expected_gelu(norm_p[2*l],norm_p[2*l+1]) for l in range(2)]
    qmu=[jnp.dot(left_t[l],mu[l][:,None],precision=highest) for l in range(2)]
    targets=(labels[:,None]==jnp.arange(CLASSES,dtype=jnp.int32)[None,:]).astype(F32)
    conv_one,msg1,hid1=forward(stem_out,parts0,norm_p[0:2],w_all,0,None,pixels,side)
    parts1=exchange(msg1)
    hq1,a_one=turn(hid1,left_t[0],qmu[0],1.0/pixels)
    residual,msg2,hid2=forward(conv_one,after(parts1,a_one),norm_p[2:4],w_all,1,stem_out,pixels,side)
    parts2=exchange(msg2)
    hq2,a_two=turn(hid2,left_t[1],qmu[1],1.0/pixels)
    wsum=jnp.sum(parts0[:,0:1,c:c+1],axis=0)
    g,msg3,head_g,loss=head(residual,after(parts2,a_two),norm_p[4:6],head_w.T,head_w[c:c+1],targets,weights[:,None],wsum,pixels,side)
    parts3=exchange(msg3)
    du1,msg4,backtwo=back_two(residual,g,parts2,parts3,norm_p[4:6],conv_one,parts1,norm_p[2:4],w_all,pixels,side)
    parts4=exchange(msg4)
    gw_two,ones_two,g_two=weight_two(backtwo,hq2,side,float(pixels))
    two,step,rounds=scatter_rounds(gw_two.reshape(devices,own,9*c),devices)
    two=step(two,0)
    backone,gw_one,ones_one,g_one=weight_one(conv_one,du1,parts1,after(parts4,ones_two),norm_p[2:4],hq1,pixels,side,float(pixels))
    one,step,_=scatter_rounds(gw_one.reshape(devices,own,9*c),devices)
    first=jnp.concatenate([step(one,0),two],axis=-1)
    stem_sums=back_one(after(backone,first),w_all,stem_out,parts0,norm_p[0:2],backtwo,pt,pixels,side)
    where=jnp.reshape(me,(1,)).astype(jnp.int32)
    keep,send=pack(where,a_one,g_one,a_two,g_two,head_g,loss,gram,ones_one,ones_two,stem_sums,devices)
    both=after(step(first,1),keep)
    same=exchange_chips(add_pieces(exchange_chips(keep+swap(send,1,devices))))
    other=swap(same,1,devices)
    for order in range(2,rounds): both=step(both,order)
    both=both.reshape(own,18*c)
    inverse,factors,damped=inverses(where,same,other,4)
    consts=(BETA_ONE,BETA_TWO,1.0-BETA_ONE**STEP,1.0-BETA_TWO**STEP,ADAM_EPS)
    q_own=jnp.stack([lax.dynamic_slice_in_dim(qmu[l],me*own,own,0) for l in range(2)])
    m_new,v_new,half=move(where,after(both,inverse),same,other,q_own,rot_bases,conv_m,conv_v,consts)
    inverse=more_inverses(where,inverse,after(damped,half))
    near,far_half,bases_new=gather_near_and_far(half,lambda held: new_bases(after(damped,held,inverse),rot_bases))
    rows=lax.dynamic_slice_in_dim(rot_bases,me*own,own,1)[0::2]
    conv_new,conv_low=finish(where,near.reshape(c//2,18*c),far_half.reshape(c//2,18*c),rows,conv_w,RATE_CONV,WEIGHT_DECAY)
    small=small_updates(where,same,other,parts0,parts3,parts4,(stem_w,stem_m,stem_v),(head_w.T,head_m.T,head_v.T),(norm_p,norm_m,norm_v),pixels,consts,(RATE_STEM,WEIGHT_DECAY,RATE_HEAD,WEIGHT_DECAY,RATE_NORM))
    return (small[0][0,0:2],factors,inverse,conv_new,m_new,v_new,bases_new,small[1],small[2],small[3],small[4].T,small[5].T,small[6].T,small[7],small[8],small[9],conv_low)

def solution(mesh):
    one=P("dp",None)
    return jax.shard_map(local,mesh=mesh,in_specs=(P("dp",None,None,None),P("dp"),P("dp"),one,one,one)+(P(),)*10,out_specs=(P(),one,one,one,one,one)+(P(),)*10+(one,),check_vma=False)
```
